256 devices in a mesh: sec: 4 (over x_lo, core), tile: 64 (over z, y, x_hi).
Axes of the slice: x: 4 (x_hi: 2, x_lo: 2; x = x_hi * 2 + x_lo), y: 4, z: 8, core: 2. Of those that a mesh axis runs over, the one named last changes fastest.
Arguments:
- flow_field: float32 [4, 32, 1024, 512], P(None, 'sec', 'tile'), may hold values from -6 to 6
- viscosity: float32 [32, 1024, 512], P('sec', 'tile'), may hold values from 0.05 to 0.16
- port_plane: float32 [4, 8192], P(None, ('sec', 'tile')), may hold values from -8 to 8
- port_match: int32 [8192], P(('sec', 'tile')), may hold values from 0 to 8191, each once
- inlet_cell: int32 [8192], P(('sec', 'tile')), may hold values from 0 to 65535
- inclusion_state: float32 [4, 4, 64, 64, 128], P(None, 'sec', 'tile'), may hold values from -6 to 6
- response_rate: float32 [4, 64, 64, 128], P('sec', 'tile'), may hold values from 0.1 to 0.9
- inclusion_mass: float32 [4, 64, 64, 128], P('sec', 'tile'), may hold values from 0.1 to 1
- anchor_cell: int32 [4, 64, 64, 128], P('sec', 'tile'), may hold values from 0 to 65535
- live_counts: int32 [4, 64, 64], P('sec', 'tile'), may hold values from 0 to 128, as said below
- arrival_cell: int32 [4, 64, 64, 128], P('sec', 'tile'), may hold values from 0 to 65535
Outputs:
- flow_next: float32 [4, 32, 1024, 512], P(None, 'sec', 'tile')
- arrived_state: float32 [4, 4, 64, 64, 128], P(None, 'sec', 'tile')
The draws below stay inside these ranges and needn't reach their ends.
Inputs may be any that keep to these rules, and one draw needn't show every extreme that they name: `live_counts`: in each sender's row one partner gets exactly 128 live inclusions; live slots come first.
All inputs are finite; a program needn't handle non-finite values.
Results may differ from the reference program's by a relative error of at most 0.00002.
Values sent between devices are 32-bit elements; how exact they have to be, the bound alone decides.
No kernel may reach another device: no remote copies, remote signals or barrier semaphores. Data moves between devices by JAX's collectives and lax.ppermute only.
A program may use at most 128 MiB of HBM per device.

```python
import math
import jax
import jax.numpy as jnp
from jax import lax

CZ = 8
CX = 16
NY = 512
CAP = 128
PORT_DEV = 32
COMPS = 4
NZ = 32
NX = 1024
CELLS = 65536
PORTS = 8192
N_SEC = 4
N_TILE = 64


def draw_live_counts(key, part):
    key = jax.random.fold_in(key, 7)
    first_key, second_key, third_key = jax.random.split(key, 3)
    shape = (N_SEC, N_TILE, N_TILE)
    factor_one = jax.random.randint(first_key, shape, 0, CAP + 1)
    factor_two = jax.random.randint(second_key, shape, 0, CAP + 1)
    base = factor_one * factor_two // CAP
    chosen = jax.random.randint(third_key, (N_SEC, N_TILE, 1), 0, N_TILE)
    position = lax.broadcasted_iota(jnp.int32, shape, 2)
    return jnp.where(position == chosen, CAP, base).astype(jnp.int32)


def with_ends(array, own_key, least, top_value):
    longest = array.shape.index(max(array.shape))
    spots = []
    for shift in (0, 1):
        where = [jax.random.randint(jax.random.fold_in(own_key, axis), (), 0, length) for axis, length in enumerate(array.shape)]
        where[longest] = (where[longest] + shift) % array.shape[longest]
        spots.append(tuple(where))
    return array.at[spots[0]].set(least).at[spots[1]].set(top_value)


def level_of(key, shape, shards, smallest, largest):
    def one(dim, parts):
        heights = jax.random.uniform(jax.random.fold_in(jax.random.fold_in(key, 6), dim), (parts,), jnp.float32, smallest / len(shards), largest / len(shards))
        return jnp.repeat(jnp.exp(heights), shape[dim] // parts).reshape((-1,) + (1,) * (len(shape) - dim - 1))

    level = one(*shards[0])
    for cut in shards[1:]:
        level = level * one(*cut)
    return level


def scatter_about(key, shape, deviation, reach, cuts=(), held_as=jnp.bfloat16):
    result = jax.random.normal(key, shape, jnp.float32) * deviation
    if len(cuts) > 0:
        result = level_of(key, shape, cuts, -0.22, 0.18) * result
    return jnp.clip(result, min=-reach, max=reach).astype(held_as)


def setup_inputs(seed: int = 0) -> dict:
    arg_keys = jax.random.split(jax.random.key(seed), 12)
    flow_field = scatter_about(arg_keys[0], (COMPS, NZ, NX, NY), 1.0, 6.0, ((1, 4), (2, 64)), jnp.float32)
    viscosity = jnp.clip(jnp.exp(math.log(0.16) - 1.1631508 * jax.random.uniform(arg_keys[1], (NZ, NX, NY), jnp.float32) ** level_of(arg_keys[1], (NZ, NX, NY), ((0, 4), (1, 64)), -0.2, 0.2)), 0.05, 0.16)
    port_plane = scatter_about(arg_keys[2], (COMPS, PORTS), 2.0, 8.0, ((1, 256),), jnp.float32)
    port_match = jax.random.permutation(arg_keys[3], PORTS).astype(jnp.int32)
    inlet_cell = with_ends(jax.random.randint(arg_keys[4], (PORTS,), 0, CELLS), jax.random.fold_in(arg_keys[4], 1), 0, CELLS - 1).astype(jnp.int32)
    inclusion_state = scatter_about(arg_keys[5], (COMPS, N_SEC, N_TILE, N_TILE, CAP), 1.0, 6.0, ((1, 4), (2, 64)), jnp.float32)
    response_rate = jnp.clip(jnp.exp(math.log(0.9) - 2.1972245 * jax.random.uniform(arg_keys[6], (N_SEC, N_TILE, N_TILE, CAP), jnp.float32) ** level_of(arg_keys[6], (N_SEC, N_TILE, N_TILE, CAP), ((0, 4), (1, 64)), -0.2, 0.2)), 0.1, 0.9)
    inclusion_mass = jnp.clip(jnp.exp(math.log(1.0) - 2.3025851 * jax.random.uniform(arg_keys[7], (N_SEC, N_TILE, N_TILE, CAP), jnp.float32) ** level_of(arg_keys[7], (N_SEC, N_TILE, N_TILE, CAP), ((0, 4), (1, 64)), -0.2, 0.2)), 0.1, 1.0)
    anchor_cell = with_ends(jax.random.randint(arg_keys[8], (N_SEC, N_TILE, N_TILE, CAP), 0, CELLS), jax.random.fold_in(arg_keys[8], 1), 0, CELLS - 1).astype(jnp.int32)
    live_counts = draw_live_counts(jax.random.fold_in(arg_keys[11], 71), 0)
    arrival_cell = with_ends(jax.random.randint(arg_keys[10], (N_SEC, N_TILE, N_TILE, CAP), 0, CELLS), jax.random.fold_in(arg_keys[10], 1), 0, CELLS - 1).astype(jnp.int32)
    return {"flow_field": flow_field, "viscosity": viscosity, "port_plane": port_plane, "port_match": port_match, "inlet_cell": inlet_cell, "inclusion_state": inclusion_state, "response_rate": response_rate, "inclusion_mass": inclusion_mass, "anchor_cell": anchor_cell, "live_counts": live_counts, "arrival_cell": arrival_cell}


time_step = 0.5
relaxation = 0.5


def tendency(padded, viscosity):
    center = padded[:, 1:-1, 1:-1, :]
    upper_z = padded[:, 2:, 1:-1, :]
    lower_z = padded[:, :-2, 1:-1, :]
    upper_x = padded[:, 1:-1, 2:, :]
    lower_x = padded[:, 1:-1, :-2, :]
    zeros_row = jnp.zeros(center.shape[:-1] + (1,), center.dtype)
    upper_y = jnp.concatenate([center[..., 1:], zeros_row], axis=-1)
    lower_y = jnp.concatenate([zeros_row, center[..., :-1]], axis=-1)
    laplace = upper_z + lower_z + upper_x + lower_x + upper_y + lower_y - 6.0 * center
    grad_z = 0.5 * (upper_z - lower_z)
    grad_x = 0.5 * (upper_x - lower_x)
    grad_y = 0.5 * (upper_y - lower_y)
    strain = jnp.sum(grad_z[:3] * grad_z[:3] + grad_x[:3] * grad_x[:3] + grad_y[:3] * grad_y[:3], axis=0)
    eddy = viscosity * (1.0 + strain / (1.0 + strain))
    carried = center[0:1] * grad_z + center[1:2] * grad_x + center[2:3] * grad_y
    return eddy * laplace - carried


def to_blocks(state):
    shaped = state.reshape(COMPS, N_SEC, CZ, N_TILE, CX, NY)
    return jnp.transpose(shaped, (0, 1, 3, 2, 4, 5)).reshape(COMPS, N_SEC * N_TILE * CELLS)


def from_blocks(flat):
    shaped = flat.reshape(COMPS, N_SEC, N_TILE, CZ, CX, NY)
    return jnp.transpose(shaped, (0, 1, 3, 2, 4, 5)).reshape(COMPS, NZ, NX, NY)


def reference(flow_field, viscosity, port_plane, port_match, inlet_cell, inclusion_state, response_rate, inclusion_mass, anchor_cell, live_counts, arrival_cell):
    def full_tendency(state):
        padded = jnp.pad(state, ((0, 0), (1, 1), (1, 1), (0, 0)))

        def slab(number):
            block = lax.dynamic_slice_in_dim(padded, number * CZ, CZ + 2, 1)
            local_visc = lax.dynamic_slice_in_dim(viscosity, number * CZ, CZ, 0)
            return tendency(block, local_visc)

        pieces = lax.map(slab, jnp.arange(N_SEC, dtype=jnp.int32))
        return jnp.transpose(pieces, (1, 0, 2, 3, 4)).reshape(state.shape)

    first = flow_field + time_step * full_tendency(flow_field)
    second = 0.5 * flow_field + 0.5 * (first + time_step * full_tendency(first))
    flat_start = to_blocks(flow_field)
    flat_second = to_blocks(second)
    device = jnp.arange(N_SEC * N_TILE, dtype=jnp.int32).reshape(N_SEC, N_TILE, 1, 1)
    sample_index = (device * CELLS + anchor_cell).reshape(-1)
    sampled = flat_start[:, sample_index].reshape(inclusion_state.shape)
    slot = lax.broadcasted_iota(jnp.int32, anchor_cell.shape, 3)
    live = (slot < live_counts[..., None]).astype(jnp.float32)
    moved = live * (inclusion_state + response_rate * (sampled - inclusion_state))
    deposit = live * inclusion_mass * response_rate * (inclusion_state - sampled)
    arrived_state = jnp.transpose(moved, (0, 1, 3, 2, 4))
    arrived_deposit = jnp.transpose(deposit, (0, 1, 3, 2, 4))
    owner = jnp.arange(PORTS, dtype=jnp.int32) // PORT_DEV
    port_index = owner * CELLS + inlet_cell
    target = port_plane[:, port_match]
    updated = flat_second.at[:, port_index].add(relaxation * (target - flat_second[:, port_index]))
    land_index = (device * CELLS + arrival_cell).reshape(-1)
    updated = updated.at[:, land_index].add(arrived_deposit.reshape(COMPS, -1))
    return from_blocks(updated), arrived_state
```

```python
import jax
import jax.numpy as jnp
from jax import lax
from jax.sharding import PartitionSpec as P

time_step = 0.5
relaxation = 0.5


def with_halo(cells, sides, width):
    for axis, dim in sides:
        count = lax.axis_size(axis)
        ends = count - 1
        head = lax.slice_in_dim(cells, 0, width, axis=dim)
        tail = lax.slice_in_dim(cells, cells.shape[dim] - width, cells.shape[dim], axis=dim)
        cells = jnp.concatenate(
            [
                lax.ppermute(tail, axis, [(i, (i + 1) % count) for i in range(ends)]),
                cells,
                lax.ppermute(head, axis, [((i + 1) % count, i) for i in range(ends)]),
            ],
            axis=dim,
        )
    return cells


def tendency(padded, viscosity):
    center = padded[:, 1:-1, 1:-1, :]
    upper_z = padded[:, 2:, 1:-1, :]
    lower_z = padded[:, :-2, 1:-1, :]
    upper_x = padded[:, 1:-1, 2:, :]
    lower_x = padded[:, 1:-1, :-2, :]
    zeros_row = jnp.zeros(center.shape[:-1] + (1,), center.dtype)
    upper_y = jnp.concatenate([center[..., 1:], zeros_row], axis=-1)
    lower_y = jnp.concatenate([zeros_row, center[..., :-1]], axis=-1)
    laplace = upper_z + lower_z + upper_x + lower_x + upper_y + lower_y - 6.0 * center
    grad_z = 0.5 * (upper_z - lower_z)
    grad_x = 0.5 * (upper_x - lower_x)
    grad_y = 0.5 * (upper_y - lower_y)
    strain = jnp.sum(
        grad_z[:3] * grad_z[:3] + grad_x[:3] * grad_x[:3] + grad_y[:3] * grad_y[:3], axis=0
    )
    eddy = viscosity * (1.0 + strain / (1.0 + strain))
    carried = center[0:1] * grad_z + center[1:2] * grad_x + center[2:3] * grad_y
    return eddy * laplace - carried


def margins(state):
    return with_halo(state, (("sec", 1), ("tile", 2)), 1)


def on_device(
    flow_field,
    viscosity,
    port_plane,
    port_match,
    inlet_cell,
    inclusion_state,
    response_rate,
    inclusion_mass,
    anchor_cell,
    live_counts,
    arrival_cell,
):
    components = flow_field.shape[0]
    flat_start = flow_field.reshape(components, -1)
    sampled = flat_start[:, anchor_cell.reshape(-1)].reshape(inclusion_state.shape)
    slot = lax.broadcasted_iota(jnp.int32, anchor_cell.shape, 3)
    live = (slot < live_counts[..., None]).astype(jnp.float32)
    moved = live * (inclusion_state + response_rate * (sampled - inclusion_state))
    deposit = live * inclusion_mass * response_rate * (inclusion_state - sampled)
    section_ports = lax.all_gather(port_plane.reshape(1, -1), "sec", axis=0, tiled=True)
    port_rows = jnp.broadcast_to(section_ports[:, None, None, None, :], moved.shape)
    outgoing = jnp.concatenate([moved, deposit, port_rows], axis=0)
    incoming = lax.all_to_all(outgoing, "tile", split_axis=3, concat_axis=2, tiled=True)
    incoming = incoming.reshape(outgoing.shape)
    first = flow_field + time_step * tendency(margins(flow_field), viscosity)
    second = 0.5 * flow_field + 0.5 * (first + time_step * tendency(margins(first), viscosity))
    gathered = incoming[2 * components :].reshape(lax.axis_size("sec"), -1, components, port_plane.shape[1])
    whole_plane = jnp.transpose(gathered, (2, 0, 1, 3)).reshape(components, -1)
    target = whole_plane[:, port_match]
    flat = second.reshape(components, -1)
    flat = flat.at[:, inlet_cell].add(relaxation * (target - flat[:, inlet_cell]))
    flat = flat.at[:, arrival_cell.reshape(-1)].add(incoming[components : 2 * components].reshape(components, -1))
    return (flat.reshape(flow_field.shape), incoming[:components])


def solution(mesh):
    return jax.shard_map(
        on_device,
        mesh=mesh,
        in_specs=(
            P(None, "sec", "tile", None),
            P("sec", "tile", None),
            P(None, ("sec", "tile")),
            P(("sec", "tile")),
            P(("sec", "tile")),
            P(None, "sec", "tile", None, None),
            P("sec", "tile", None, None),
            P("sec", "tile", None, None),
            P("sec", "tile", None, None),
            P("sec", "tile", None),
            P("sec", "tile", None, None),
        ),
        out_specs=(P(None, "sec", "tile", None), P(None, "sec", "tile", None, None)),
        check_vma=False,
    )
```

```python
import functools

import jax
import jax.numpy as jnp
from jax import lax
from jax.experimental import pallas as pl
from jax.experimental.pallas import tpu as pltpu

from jax.sharding import PartitionSpec as P

VM = pl.BlockSpec(memory_space=pltpu.VMEM)
SM = pl.BlockSpec(memory_space=pltpu.SMEM)


def halves(value):
    high = value.astype(jnp.bfloat16)
    low = (value - high.astype(jnp.float32)).astype(jnp.bfloat16)
    return high, low


def column_hot(cells, depth):
    at = lax.broadcasted_iota(jnp.int32, (depth, cells.shape[1]), 0)
    return jnp.where(at == (cells & (depth - 1)), 1.0, 0.0).astype(jnp.bfloat16)


def slip_kernel(GP, counts, flow, anchor, state, rate, mass, ports, out, table):
    comps, partners, cap = state.shape
    total, depth = flow.shape
    rows = total // comps
    shift = depth.bit_length() - 1
    high, low = halves(flow[...])
    table[0:total] = high
    table[total:] = low
    lane = lax.broadcasted_iota(jnp.int32, (1, cap), 1)

    def group(g, carry):
        first = g * GP
        cells = jnp.concatenate([anchor[pl.ds(first + i, 1), :] for i in range(GP)], axis=1)
        hot = column_hot(cells, depth)
        picked = jnp.dot(table[...], hot, preferred_element_type=jnp.float32)
        row = lax.broadcasted_iota(jnp.int32, (rows, cells.shape[1]), 0) == (cells >> shift)
        parts = []
        for c in range(comps):
            both = picked[c * rows : (c + 1) * rows] + picked[total + c * rows : total + (c + 1) * rows]
            parts.append(jnp.sum(jnp.where(row, both, 0.0), axis=0, keepdims=True))
        sampled = jnp.concatenate(parts, axis=0)
        for i in range(GP):
            p = first + i
            live = jnp.where(lane < counts[p], 1.0, 0.0)
            own = jnp.concatenate([state[c, pl.ds(p, 1), :] for c in range(comps)], axis=0)
            r = rate[pl.ds(p, 1), :]
            slip = own - sampled[:, i * cap : (i + 1) * cap]
            out[3 * p] = live * (own - r * slip)
            out[3 * p + 1] = (live * mass[pl.ds(p, 1), :] * r) * slip
            out[3 * p + 2] = ports[...]
        return carry

    lax.fori_loop(0, partners // GP, group, 0)


def slip(counts, flow, anchor, state, rate, mass, ports, GP=4):
    comps, partners, cap = state.shape
    return pl.pallas_call(
        functools.partial(slip_kernel, GP),
        out_shape=jax.ShapeDtypeStruct((partners * 3, comps, cap), jnp.float32),
        in_specs=[SM] + [VM] * 6,
        out_specs=VM,
        scratch_shapes=[pltpu.VMEM((2 * flow.shape[0], flow.shape[1]), jnp.bfloat16)],
        compiler_params=pltpu.CompilerParams(vmem_limit_bytes=48 * 1024 * 1024),
        cost_estimate=pl.CostEstimate(flops=2 * 8192 * 512 * 1024, bytes_accessed=2**21, transcendentals=0),
        name="slip",
    )(counts, flow, anchor, state, rate, mass, ports)


def land_kernel(GP, match, second, inlet_now, inlet, arrival, arrived, flow_out, state_out, rows_ref, total_ref):
    comps, partners, cap = state_out.shape
    total, depth = second.shape
    rows = total // comps
    shift = depth.bit_length() - 1
    entries = match.shape[0]
    per = cap // comps
    nt = (((1,), (1,)), ((), ()))

    def spread(cells, values):
        row = lax.broadcasted_iota(jnp.int32, (rows, cells.shape[1]), 0) == (cells >> shift)
        high, low = halves(values)
        parts = []
        for part in (high.astype(jnp.float32), low.astype(jnp.float32)):
            for c in range(comps):
                parts.append(jnp.where(row, part[c : c + 1], 0.0).astype(jnp.bfloat16))
        return jnp.concatenate(parts, axis=0)

    def product(cells, values):
        both = lax.dot_general(spread(cells, values), column_hot(cells, depth), nt, preferred_element_type=jnp.float32)
        return both[:total] + both[total:]

    rows_ref[...] = jnp.zeros_like(rows_ref)
    for k in range(entries):
        port = match[k]
        device = port // entries
        rows_ref[k : k + 1, :] = arrived[3 * (device % partners) + 2, pl.ds(device // partners, 1), :]
    turned = rows_ref[...].T
    slot = lax.broadcasted_iota(jnp.int32, (1, cap), 1)
    which = inlet[1:2, :] % entries
    pick = lax.broadcasted_iota(jnp.int32, (per, cap), 0) == which
    target = jnp.concatenate(
        [jnp.sum(jnp.where(pick, turned[c * per : (c + 1) * per], 0.0), axis=0, keepdims=True) for c in range(comps)], axis=0
    )
    change = jnp.where(slot < entries, 0.5 * (target - inlet_now[...]), 0.0)
    flow_out[...] = second[...] + product(inlet[0:1, :], change)

    def group(g, carry):
        first = g * GP
        cells = jnp.concatenate([arrival[pl.ds(first + i, 1), :] for i in range(GP)], axis=1)
        values = jnp.concatenate([arrived[3 * (first + i) + 1] for i in range(GP)], axis=1)
        flow_out[...] += product(cells, values)
        for i in range(GP):
            p = first + i
            moved = arrived[3 * p]
            for c in range(comps):
                state_out[c, pl.ds(p, 1), :] = moved[c : c + 1]
        return carry

    lax.fori_loop(0, partners // GP, group, 0)


def land(match, second, inlet_now, inlet, arrival, arrived, GP=8):
    partners, cap = arrival.shape
    comps = arrived.shape[1]
    return pl.pallas_call(
        functools.partial(land_kernel, GP),
        out_shape=(
            jax.ShapeDtypeStruct(second.shape, jnp.float32),
            jax.ShapeDtypeStruct((comps, partners, cap), jnp.float32),
        ),
        in_specs=[SM] + [VM] * 5,
        out_specs=(VM, VM),
        scratch_shapes=[pltpu.VMEM((cap, cap), jnp.float32), pltpu.VMEM((8, 128), jnp.float32)],
        compiler_params=pltpu.CompilerParams(vmem_limit_bytes=48 * 1024 * 1024),
        cost_estimate=pl.CostEstimate(flops=2 * 8192 * 512 * 1024, bytes_accessed=2**21, transcendentals=0),
        name="land",
    )(match, second, inlet_now, inlet, arrival, arrived)


def edge_kernel(comps, depth_z, width, flow, viscosity, low_out, high_out):
    for k in range(comps * depth_z):
        low_out[2 * k : 2 * k + 2, :] = flow[k * width : k * width + 2, :]
        high_out[2 * k : 2 * k + 2, :] = flow[(k + 1) * width - 2 : (k + 1) * width, :]
    base = 2 * comps * depth_z
    for z in range(depth_z):
        low_out[base + z : base + z + 1, :] = viscosity[z * width : z * width + 1, :]
        high_out[base + z : base + z + 1, :] = viscosity[(z + 1) * width - 1 : (z + 1) * width, :]


def edges(comps, depth_z, width, flow, viscosity):
    shape = jax.ShapeDtypeStruct(((2 * comps + 1) * depth_z, flow.shape[1]), jnp.float32)
    return pl.pallas_call(
        functools.partial(edge_kernel, comps, depth_z, width),
        out_shape=(shape, shape),
        in_specs=[VM] * 2,
        out_specs=(VM, VM),
        name="edges",
    )(flow, viscosity)


def side_tile(tile, left, right, k, reach):
    tile[...] = jnp.zeros_like(tile)
    tile[0:reach, :] = right[2 * k : 2 * k + reach, :]
    tile[8 - reach : 8, :] = left[2 * k + 2 - reach : 2 * k + 2, :]


def cap_kernel(comps, depth_z, width, flow, viscosity, left, right, low_out, high_out, tile):
    per = 2 * width + 8
    for c in range(comps):
        for out, near, far in ((low_out, 0, 1), (high_out, depth_z - 1, depth_z - 2)):
            k = c * depth_z + near
            out[c * per : c * per + width, :] = flow[k * width : (k + 1) * width, :]
            side_tile(tile, left, right, k, 1)
            out[c * per + width : c * per + width + 8, :] = tile[...]
            k = c * depth_z + far
            out[c * per + width + 8 : (c + 1) * per, :] = flow[k * width : (k + 1) * width, :]
    low_out[comps * per :, :] = viscosity[0:width, :]
    high_out[comps * per :, :] = viscosity[(depth_z - 1) * width : depth_z * width, :]


def caps(comps, depth_z, width, flow, viscosity, left, right):
    shape = jax.ShapeDtypeStruct((comps * (2 * width + 8) + width, flow.shape[1]), jnp.float32)
    return pl.pallas_call(
        functools.partial(cap_kernel, comps, depth_z, width),
        out_shape=(shape, shape),
        in_specs=[VM] * 4,
        out_specs=(VM, VM),
        scratch_shapes=[pltpu.VMEM((8, flow.shape[1]), jnp.float32)],
        name="caps",
    )(flow, viscosity, left, right)


def stencil_kernel(comps, depth_z, width, flow, viscosity, left, right, below, above, inlet, second_out, inlet_now, state, first, visc, table):
    depth = flow.shape[1]
    per = 2 * width + 8
    total = comps * depth_z * width
    rows = depth_z * width
    wide = width + 8
    base = 2 * comps * depth_z
    blank = jnp.zeros((8, depth), jnp.float32)
    for c in range(comps):
        for z in range(depth_z):
            k = c * depth_z + z
            state[c, z + 2, 0:width, :] = flow[k * width : (k + 1) * width, :]
            state[c, z + 2, width:wide, :] = blank
            state[c, z + 2, width : width + 2, :] = right[2 * k : 2 * k + 2, :]
            state[c, z + 2, wide - 2 : wide, :] = left[2 * k : 2 * k + 2, :]
        for near, far, source in ((1, 0, below), (depth_z + 2, depth_z + 3, above)):
            state[c, near] = source[c * per : c * per + wide, :]
            state[c, far, 0:width, :] = source[c * per + wide : (c + 1) * per, :]
            state[c, far, width:wide, :] = blank
    for z in range(depth_z):
        visc[z + 1, 0:width, :] = viscosity[z * width : (z + 1) * width, :]
        visc[z + 1, width:wide, :] = blank
        visc[z + 1, width : width + 1, :] = right[base + z : base + z + 1, :]
        visc[z + 1, wide - 1 : wide, :] = left[base + z : base + z + 1, :]
    for z, source in ((0, below), (depth_z + 1, above)):
        visc[z, 0:width, :] = source[comps * per :, :]
        visc[z, width:wide, :] = blank

    place = lax.broadcasted_iota(jnp.int32, (1, depth), 1)

    def tendency(ref, z, eddy_base, keep):
        centers, laps, dz, dx, dy = [], [], [], [], []
        for c in range(comps):
            plane = ref[c, z]
            center = plane[:keep]
            up_x = pltpu.roll(plane, wide - 1, 0)[:keep]
            low_x = pltpu.roll(plane, 1, 0)[:keep]
            up_y = jnp.where(place == depth - 1, 0.0, pltpu.roll(center, depth - 1, 1))
            low_y = jnp.where(place == 0, 0.0, pltpu.roll(center, 1, 1))
            up_z = ref[c, z + 1, 0:keep, :]
            low_z = ref[c, z - 1, 0:keep, :]
            centers.append(center)
            laps.append((up_z + low_z) + (up_x + low_x) + (up_y + low_y) - 6.0 * center)
            dz.append(up_z - low_z)
            dx.append(up_x - low_x)
            dy.append(up_y - low_y)
        strain = sum(d[c] * d[c] for c in range(3) for d in (dz, dx, dy)) * 0.25
        eddy = eddy_base * (1.0 + strain / (1.0 + strain))
        out = []
        for c in range(comps):
            carried = centers[0] * dz[c] + centers[1] * dx[c] + centers[2] * dy[c]
            out.append(0.5 * (eddy * laps[c]) - 0.25 * carried)
        return centers, out

    def one(z, carry):
        centers, change = tendency(state, z + 1, visc[z], wide)
        for c in range(comps):
            first[c, z] = centers[c] + change[c]
        return carry

    lax.fori_loop(0, depth_z + 2, one, 0)

    def two(z, carry):
        centers, change = tendency(first, z + 1, visc[z + 1, 0:width, :], width)
        for c in range(comps):
            value = 0.5 * state[c, z + 2, 0:width, :] + 0.5 * (centers[c] + change[c])
            spot = pl.multiple_of((c * depth_z + z) * width, width)
            second_out[pl.ds(spot, width), :] = value
            high, low = halves(value)
            table[pl.ds(spot, width), :] = high
            table[pl.ds(total + spot, width), :] = low
        return carry

    lax.fori_loop(0, depth_z, two, 0)

    cells = inlet[0:1, :]
    picked = jnp.dot(table[...], column_hot(cells, depth), preferred_element_type=jnp.float32)
    row = lax.broadcasted_iota(jnp.int32, (rows, cells.shape[1]), 0) == (cells >> (depth.bit_length() - 1))
    for c in range(comps):
        both = picked[c * rows : (c + 1) * rows] + picked[total + c * rows : total + (c + 1) * rows]
        inlet_now[c : c + 1, :] = jnp.sum(jnp.where(row, both, 0.0), axis=0, keepdims=True)


def stencil(comps, depth_z, width, flow, viscosity, left, right, below, above, inlet):
    depth = flow.shape[1]
    wide = width + 8
    return pl.pallas_call(
        functools.partial(stencil_kernel, comps, depth_z, width),
        out_shape=(
            jax.ShapeDtypeStruct(flow.shape, jnp.float32),
            jax.ShapeDtypeStruct((comps, inlet.shape[1]), jnp.float32),
        ),
        in_specs=[VM] * 7,
        out_specs=(VM, VM),
        scratch_shapes=[
            pltpu.VMEM((comps, depth_z + 4, wide, depth), jnp.float32),
            pltpu.VMEM((comps, depth_z + 2, wide, depth), jnp.float32),
            pltpu.VMEM((depth_z + 2, wide, depth), jnp.float32),
            pltpu.VMEM((2 * flow.shape[0], depth), jnp.bfloat16),
        ],
        compiler_params=pltpu.CompilerParams(vmem_limit_bytes=48 * 1024 * 1024),
        cost_estimate=pl.CostEstimate(flops=2 * 10**7, bytes_accessed=2**22, transcendentals=0),
        name="stencil",
    )(flow, viscosity, left, right, below, above, inlet)


def on_device(
    flow_field,
    viscosity,
    port_plane,
    port_match,
    inlet_cell,
    inclusion_state,
    response_rate,
    inclusion_mass,
    anchor_cell,
    live_counts,
    arrival_cell,
):
    comps, depth_z, width, depth = flow_field.shape
    partners, cap = anchor_cell.shape[2:]
    sizes = (comps, depth_z, width)
    flow = flow_field.reshape(-1, depth)
    visc = viscosity.reshape(-1, depth)
    count = lax.axis_size("tile")
    forth = [(i, i + 1) for i in range(count - 1)]
    back = [(i + 1, i) for i in range(count - 1)]
    levels = lax.axis_size("sec")
    up = [(i, i + 1) for i in range(levels - 1)]
    down = [(i + 1, i) for i in range(levels - 1)]

    ports = lax.all_gather(port_plane.reshape(1, -1), "sec", axis=0, tiled=True)
    low_edge, high_edge = edges(*sizes, flow, visc)
    left = lax.ppermute(high_edge, "tile", forth)
    right = lax.ppermute(low_edge, "tile", back)
    outgoing = slip(
        live_counts.reshape(-1),
        flow,
        anchor_cell.reshape(partners, cap),
        inclusion_state.reshape(comps, partners, cap),
        response_rate.reshape(partners, cap),
        inclusion_mass.reshape(partners, cap),
        ports,
    )
    arrived = lax.all_to_all(outgoing, "tile", split_axis=0, concat_axis=0, tiled=True)
    low_cap, high_cap = caps(*sizes, flow, visc, left, right)
    below = lax.ppermute(high_cap, "sec", up)
    above = lax.ppermute(low_cap, "sec", down)
    inlet = jnp.pad(jnp.stack([inlet_cell, port_match]), ((0, 0), (0, cap - inlet_cell.shape[0])))
    second, inlet_now = stencil(*sizes, flow, visc, left, right, below, above, inlet)
    flow_next, arrived_state = land(
        port_match, second, inlet_now, inlet, arrival_cell.reshape(partners, cap), arrived
    )
    return flow_next.reshape(flow_field.shape), arrived_state.reshape(inclusion_state.shape)


def solution(mesh):
    return jax.shard_map(
        on_device,
        mesh=mesh,
        in_specs=(
            P(None, "sec", "tile", None),
            P("sec", "tile", None),
            P(None, ("sec", "tile")),
            P(("sec", "tile")),
            P(("sec", "tile")),
            P(None, "sec", "tile", None, None),
            P("sec", "tile", None, None),
            P("sec", "tile", None, None),
            P("sec", "tile", None, None),
            P("sec", "tile", None),
            P("sec", "tile", None, None),
        ),
        out_specs=(P(None, "sec", "tile", None), P(None, "sec", "tile", None, None)),
        check_vma=False,
    )
```

```python
import functools

import jax
import jax.numpy as jnp
from jax import lax
from jax.experimental import pallas as pl
from jax.experimental.pallas import tpu as pltpu
from jax.sharding import PartitionSpec as P

VM = pl.BlockSpec(memory_space=pltpu.VMEM)
SM = pl.BlockSpec(memory_space=pltpu.SMEM)
HB = pl.BlockSpec(memory_space=pltpu.HBM)


def halves(value):
    high = value.astype(jnp.bfloat16)
    low = (value - high.astype(jnp.float32)).astype(jnp.bfloat16)
    return high, low


def column_hot(cells, depth):
    at = lax.broadcasted_iota(jnp.int32, (depth, cells.shape[1]), 0)
    return jnp.where(at == (cells & (depth - 1)), 1.0, 0.0).astype(jnp.bfloat16)


def slip_kernel(GP, counts, flow_far, anchor_far, state_far, rate_far, mass_far, ports, out, flow, anchor, state, rate, mass, table, packed, sampled, sems):
    comps, partners, cap = state.shape
    total, depth = flow.shape
    rows = total // comps
    shift = depth.bit_length() - 1
    cap_shift = cap.bit_length() - 1
    pairs = ((anchor_far, anchor), (flow_far, flow), (state_far, state), (rate_far, rate), (mass_far, mass))
    copies = [pltpu.make_async_copy(far, near, sems.at[i]) for i, (far, near) in enumerate(pairs)]
    for copy in copies:
        copy.start()
    lane = lax.broadcasted_iota(jnp.int32, (1, cap), 1)
    packed[...] = jnp.zeros_like(packed)
    copies[0].wait()

    def pack(p, base):
        begin = base & (cap - 1)
        spot = base >> cap_shift
        turned = pltpu.roll(anchor[pl.ds(p, 1), :], begin, 1)
        pltpu.store(packed.at[pl.ds(spot, 1), :], turned, mask=lane >= begin)
        pltpu.store(packed.at[pl.ds(spot + 1, 1), :], turned, mask=lane < begin)
        return base + counts[p]

    used = lax.fori_loop(0, partners, pack, 0, unroll=8)
    copies[1].wait()
    high, low = halves(flow[...])
    table[0:total] = high
    table[total:] = low

    def group(g, carry):
        first = g * GP
        cells = jnp.concatenate([packed[pl.ds(first + i, 1), :] for i in range(GP)], axis=1)
        hot = column_hot(cells, depth)
        picked = jnp.dot(table[...], hot, preferred_element_type=jnp.float32)
        row = lax.broadcasted_iota(jnp.int32, (rows, cells.shape[1]), 0) == (cells >> shift)
        parts = []
        for c in range(comps):
            both = picked[c * rows : (c + 1) * rows] + picked[total + c * rows : total + (c + 1) * rows]
            parts.append(jnp.sum(jnp.where(row, both, 0.0), axis=0, keepdims=True))
        found = jnp.concatenate(parts, axis=0)
        for i in range(GP):
            sampled[first + i] = found[:, i * cap : (i + 1) * cap]
        return carry

    lax.fori_loop(0, (used + GP * cap - 1) // (GP * cap), group, 0)
    for copy in copies[2:]:
        copy.wait()

    def finish(p, base):
        n = counts[p]
        begin = base & (cap - 1)
        spot = base >> cap_shift
        both = jnp.where(lane >= begin, sampled[spot], sampled[spot + 1])
        value = pltpu.roll(both, (cap - begin) & (cap - 1), 1)
        own = jnp.concatenate([state[c, pl.ds(p, 1), :] for c in range(comps)], axis=0)
        r = rate[pl.ds(p, 1), :]
        drop = r * (own - value)
        live = lane < n
        out[3 * p] = jnp.where(live, own - drop, 0.0)
        out[3 * p + 1] = jnp.where(live, mass[pl.ds(p, 1), :] * drop, 0.0)
        out[3 * p + 2] = ports[...]
        return base + n

    lax.fori_loop(0, partners, finish, 0, unroll=8)


def slip(counts, flow, anchor, state, rate, mass, ports, GP=4):
    comps, partners, cap = state.shape
    near = [pltpu.VMEM(x.shape, x.dtype) for x in (flow, anchor, state, rate, mass)]
    return pl.pallas_call(
        functools.partial(slip_kernel, GP),
        out_shape=jax.ShapeDtypeStruct((partners * 3, comps, cap), jnp.float32),
        in_specs=[SM] + [HB] * 5 + [VM],
        out_specs=VM,
        scratch_shapes=near
        + [
            pltpu.VMEM((2 * flow.shape[0], flow.shape[1]), jnp.bfloat16),
            pltpu.VMEM((partners + 8, cap), jnp.int32),
            pltpu.VMEM((partners + 8, comps, cap), jnp.float32),
            pltpu.SemaphoreType.DMA((5,)),
        ],
        compiler_params=pltpu.CompilerParams(vmem_limit_bytes=60 * 1024 * 1024),
        cost_estimate=pl.CostEstimate(flops=2 * 8192 * 512 * 1024, bytes_accessed=2**21, transcendentals=0),
        name="slip",
    )(counts, flow, anchor, state, rate, mass, ports)


def land_kernel(GP, match, second, inlet_now, inlet, arrival, arrived, flow_out, state_out, rows_ref, last_ref, last, packed, sem):
    comps, partners, cap = state_out.shape
    total, depth = second.shape
    rows = total // comps
    shift = depth.bit_length() - 1
    cap_shift = cap.bit_length() - 1
    entries = match.shape[0]
    per = cap // comps
    nt = (((1,), (1,)), ((), ()))
    slot = lax.broadcasted_iota(jnp.int32, (1, cap), 1)

    def ends(p, carry):
        moved = arrived[3 * p]
        gift = arrived[3 * p + 1]
        for c in range(comps):
            state_out[c, pl.ds(p, 1), :] = moved[c : c + 1]
        biggest = jnp.max(jnp.abs(gift), axis=0, keepdims=True)
        last_ref[pl.ds(p, 1), :] = jnp.where(biggest > 0.0, slot + 1, 0)
        return carry

    lax.fori_loop(0, partners, ends, 0, unroll=8)
    last_ref[partners:, :] = jnp.zeros_like(last_ref[partners:, :])
    top = jnp.max(last_ref[...].T, axis=0, keepdims=True)
    last_ref[0:1, :] = top
    fetch = pltpu.make_async_copy(last_ref.at[0:1, :], last, sem)
    fetch.start()

    def spread(cells, values):
        row = lax.broadcasted_iota(jnp.int32, (rows, cells.shape[1]), 0) == (cells >> shift)
        high, low = halves(values)
        parts = []
        for part in (high.astype(jnp.float32), low.astype(jnp.float32)):
            for c in range(comps):
                parts.append(jnp.where(row, part[c : c + 1], 0.0).astype(jnp.bfloat16))
        return jnp.concatenate(parts, axis=0)

    def product(cells, values):
        both = lax.dot_general(spread(cells, values), column_hot(cells, depth), nt, preferred_element_type=jnp.float32)
        return both[:total] + both[total:]

    rows_ref[...] = jnp.zeros_like(rows_ref)
    for k in range(entries):
        port = match[k]
        device = port // entries
        rows_ref[k : k + 1, :] = arrived[3 * (device % partners) + 2, pl.ds(device // partners, 1), :]
    turned = rows_ref[...].T
    which = inlet[1:2, :] % entries
    pick = lax.broadcasted_iota(jnp.int32, (per, cap), 0) == which
    target = jnp.concatenate(
        [jnp.sum(jnp.where(pick, turned[c * per : (c + 1) * per], 0.0), axis=0, keepdims=True) for c in range(comps)], axis=0
    )
    change = jnp.where(slot < entries, 0.5 * (target - inlet_now[...]), 0.0)
    flow_out[...] = second[...] + product(inlet[0:1, :], change)
    packed[...] = jnp.zeros_like(packed)
    fetch.wait()

    def pack(p, base):
        begin = base & (cap - 1)
        spot = base >> cap_shift
        cells = arrival[pl.ds(p, 1), :].astype(jnp.float32)
        both = jnp.concatenate([arrived[3 * p + 1], jnp.broadcast_to(cells, (8 - comps, cap))], axis=0)
        turned = pltpu.roll(both, begin, 1)
        wide = lax.broadcasted_iota(jnp.int32, (8, cap), 1)
        pltpu.store(packed.at[spot], turned, mask=wide >= begin)
        pltpu.store(packed.at[spot + 1], turned, mask=wide < begin)
        return base + last[0, p]

    used = lax.fori_loop(0, partners, pack, 0, unroll=8)

    def group(g, carry):
        first = g * GP
        both = jnp.concatenate([packed[first + i] for i in range(GP)], axis=1)
        flow_out[...] += product(both[comps : comps + 1].astype(jnp.int32), both[:comps])
        return carry

    lax.fori_loop(0, (used + GP * cap - 1) // (GP * cap), group, 0)


def land(match, second, inlet_now, inlet, arrival, arrived, GP=4):
    partners, cap = arrival.shape
    comps = arrived.shape[1]
    return pl.pallas_call(
        functools.partial(land_kernel, GP),
        out_shape=(
            jax.ShapeDtypeStruct(second.shape, jnp.float32),
            jax.ShapeDtypeStruct((comps, partners, cap), jnp.float32),
        ),
        in_specs=[SM] + [VM] * 5,
        out_specs=(VM, VM),
        scratch_shapes=[
            pltpu.VMEM((cap, cap), jnp.float32),
            pltpu.VMEM((cap, cap), jnp.int32),
            pltpu.SMEM((1, cap), jnp.int32),
            pltpu.VMEM((partners + 8, 8, cap), jnp.float32),
            pltpu.SemaphoreType.DMA,
        ],
        compiler_params=pltpu.CompilerParams(vmem_limit_bytes=32 * 1024 * 1024),
        cost_estimate=pl.CostEstimate(flops=2 * 8192 * 512 * 1024, bytes_accessed=2**21, transcendentals=0),
        name="land",
    )(match, second, inlet_now, inlet, arrival, arrived)


def edge_kernel(comps, depth_z, width, flow, viscosity, low_out, high_out):
    for k in range(comps * depth_z):
        low_out[2 * k : 2 * k + 2, :] = flow[k * width : k * width + 2, :]
        high_out[2 * k : 2 * k + 2, :] = flow[(k + 1) * width - 2 : (k + 1) * width, :]
    base = 2 * comps * depth_z
    for z in range(depth_z):
        low_out[base + z : base + z + 1, :] = viscosity[z * width : z * width + 1, :]
        high_out[base + z : base + z + 1, :] = viscosity[(z + 1) * width - 1 : (z + 1) * width, :]


def edges(comps, depth_z, width, flow, viscosity):
    shape = jax.ShapeDtypeStruct(((2 * comps + 1) * depth_z, flow.shape[1]), jnp.float32)
    return pl.pallas_call(
        functools.partial(edge_kernel, comps, depth_z, width),
        out_shape=(shape, shape),
        in_specs=[VM] * 2,
        out_specs=(VM, VM),
        compiler_params=pltpu.CompilerParams(vmem_limit_bytes=60 * 1024 * 1024),
        name="edges",
    )(flow, viscosity)


def side_tile(tile, left, right, k, reach):
    tile[...] = jnp.zeros_like(tile)
    tile[0:reach, :] = right[2 * k : 2 * k + reach, :]
    tile[8 - reach : 8, :] = left[2 * k + 2 - reach : 2 * k + 2, :]


def cap_kernel(comps, depth_z, width, flow, viscosity, left, right, low_out, high_out, tile):
    per = 2 * width + 8
    for c in range(comps):
        for out, near, far in ((low_out, 0, 1), (high_out, depth_z - 1, depth_z - 2)):
            k = c * depth_z + near
            out[c * per : c * per + width, :] = flow[k * width : (k + 1) * width, :]
            side_tile(tile, left, right, k, 1)
            out[c * per + width : c * per + width + 8, :] = tile[...]
            k = c * depth_z + far
            out[c * per + width + 8 : (c + 1) * per, :] = flow[k * width : (k + 1) * width, :]
    low_out[comps * per :, :] = viscosity[0:width, :]
    high_out[comps * per :, :] = viscosity[(depth_z - 1) * width : depth_z * width, :]


def caps(comps, depth_z, width, flow, viscosity, left, right):
    shape = jax.ShapeDtypeStruct((comps * (2 * width + 8) + width, flow.shape[1]), jnp.float32)
    return pl.pallas_call(
        functools.partial(cap_kernel, comps, depth_z, width),
        out_shape=(shape, shape),
        in_specs=[VM] * 4,
        out_specs=(VM, VM),
        scratch_shapes=[pltpu.VMEM((8, flow.shape[1]), jnp.float32)],
        compiler_params=pltpu.CompilerParams(vmem_limit_bytes=24 * 1024 * 1024),
        name="caps",
    )(flow, viscosity, left, right)


def stencil_kernel(comps, depth_z, width, flow, viscosity, left, right, below, above, inlet, second_out, inlet_now, state, first, visc, table):
    depth = flow.shape[1]
    per = 2 * width + 8
    total = comps * depth_z * width
    rows = depth_z * width
    wide = width + 8
    base = 2 * comps * depth_z
    blank = jnp.zeros((8, depth), jnp.float32)
    for c in range(comps):
        for z in range(depth_z):
            k = c * depth_z + z
            state[c, z + 2, 0:width, :] = flow[k * width : (k + 1) * width, :]
            state[c, z + 2, width:wide, :] = blank
            state[c, z + 2, width : width + 2, :] = right[2 * k : 2 * k + 2, :]
            state[c, z + 2, wide - 2 : wide, :] = left[2 * k : 2 * k + 2, :]
        for near, far, source in ((1, 0, below), (depth_z + 2, depth_z + 3, above)):
            state[c, near] = source[c * per : c * per + wide, :]
            state[c, far, 0:width, :] = source[c * per + wide : (c + 1) * per, :]
            state[c, far, width:wide, :] = blank
    for z in range(depth_z):
        visc[z + 1, 0:width, :] = viscosity[z * width : (z + 1) * width, :]
        visc[z + 1, width:wide, :] = blank
        visc[z + 1, width : width + 1, :] = right[base + z : base + z + 1, :]
        visc[z + 1, wide - 1 : wide, :] = left[base + z : base + z + 1, :]
    for z, source in ((0, below), (depth_z + 1, above)):
        visc[z, 0:width, :] = source[comps * per :, :]
        visc[z, width:wide, :] = blank

    place = lax.broadcasted_iota(jnp.int32, (1, depth), 1)

    def tendency(ref, z, eddy_base, keep):
        centers, laps, dz, dx, dy = [], [], [], [], []
        for c in range(comps):
            plane = ref[c, z]
            center = plane[:keep]
            up_x = pltpu.roll(plane, wide - 1, 0)[:keep]
            low_x = pltpu.roll(plane, 1, 0)[:keep]
            up_y = jnp.where(place == depth - 1, 0.0, pltpu.roll(center, depth - 1, 1))
            low_y = jnp.where(place == 0, 0.0, pltpu.roll(center, 1, 1))
            up_z = ref[c, z + 1, 0:keep, :]
            low_z = ref[c, z - 1, 0:keep, :]
            centers.append(center)
            laps.append((up_z + low_z) + (up_x + low_x) + (up_y + low_y) - 6.0 * center)
            dz.append(up_z - low_z)
            dx.append(up_x - low_x)
            dy.append(up_y - low_y)
        strain = sum(d[c] * d[c] for c in range(3) for d in (dz, dx, dy)) * 0.25
        eddy = eddy_base * (1.0 + strain / (1.0 + strain))
        out = []
        for c in range(comps):
            carried = centers[0] * dz[c] + centers[1] * dx[c] + centers[2] * dy[c]
            out.append(0.5 * (eddy * laps[c]) - 0.25 * carried)
        return centers, out

    def one(z, carry):
        centers, change = tendency(state, z + 1, visc[z], wide)
        for c in range(comps):
            first[c, z] = centers[c] + change[c]
        return carry

    lax.fori_loop(0, depth_z + 2, one, 0)

    def two(z, carry):
        centers, change = tendency(first, z + 1, visc[z + 1, 0:width, :], width)
        for c in range(comps):
            value = 0.5 * state[c, z + 2, 0:width, :] + 0.5 * (centers[c] + change[c])
            spot = pl.multiple_of((c * depth_z + z) * width, width)
            second_out[pl.ds(spot, width), :] = value
            high, low = halves(value)
            table[pl.ds(spot, width), :] = high
            table[pl.ds(total + spot, width), :] = low
        return carry

    lax.fori_loop(0, depth_z, two, 0)

    cells = inlet[0:1, :]
    picked = jnp.dot(table[...], column_hot(cells, depth), preferred_element_type=jnp.float32)
    row = lax.broadcasted_iota(jnp.int32, (rows, cells.shape[1]), 0) == (cells >> (depth.bit_length() - 1))
    for c in range(comps):
        both = picked[c * rows : (c + 1) * rows] + picked[total + c * rows : total + (c + 1) * rows]
        inlet_now[c : c + 1, :] = jnp.sum(jnp.where(row, both, 0.0), axis=0, keepdims=True)


def stencil(comps, depth_z, width, flow, viscosity, left, right, below, above, inlet):
    depth = flow.shape[1]
    wide = width + 8
    return pl.pallas_call(
        functools.partial(stencil_kernel, comps, depth_z, width),
        out_shape=(
            jax.ShapeDtypeStruct(flow.shape, jnp.float32),
            jax.ShapeDtypeStruct((comps, inlet.shape[1]), jnp.float32),
        ),
        in_specs=[VM] * 7,
        out_specs=(VM, VM),
        scratch_shapes=[
            pltpu.VMEM((comps, depth_z + 4, wide, depth), jnp.float32),
            pltpu.VMEM((comps, depth_z + 2, wide, depth), jnp.float32),
            pltpu.VMEM((depth_z + 2, wide, depth), jnp.float32),
            pltpu.VMEM((2 * flow.shape[0], depth), jnp.bfloat16),
        ],
        compiler_params=pltpu.CompilerParams(vmem_limit_bytes=32 * 1024 * 1024),
        cost_estimate=pl.CostEstimate(flops=2 * 10**7, bytes_accessed=2**22, transcendentals=0),
        name="stencil",
    )(flow, viscosity, left, right, below, above, inlet)


def on_device(
    flow_field,
    viscosity,
    port_plane,
    port_match,
    inlet_cell,
    inclusion_state,
    response_rate,
    inclusion_mass,
    anchor_cell,
    live_counts,
    arrival_cell,
):
    comps, depth_z, width, depth = flow_field.shape
    partners, cap = anchor_cell.shape[2:]
    sizes = (comps, depth_z, width)
    flow = flow_field.reshape(-1, depth)
    visc = viscosity.reshape(-1, depth)
    count = lax.axis_size("tile")
    forth = [(i, i + 1) for i in range(count - 1)]
    back = [(i + 1, i) for i in range(count - 1)]
    levels = lax.axis_size("sec")
    up = [(i, i + 1) for i in range(levels - 1)]
    down = [(i + 1, i) for i in range(levels - 1)]

    ports = lax.all_gather(port_plane.reshape(1, -1), "sec", axis=0, tiled=True)
    low_edge, high_edge = edges(*sizes, flow, visc)
    left = lax.ppermute(high_edge, "tile", forth)
    right = lax.ppermute(low_edge, "tile", back)
    counts, low_edge, high_edge = lax.optimization_barrier((live_counts.reshape(-1), low_edge, high_edge))
    outgoing = slip(
        counts,
        flow,
        anchor_cell.reshape(partners, cap),
        inclusion_state.reshape(comps, partners, cap),
        response_rate.reshape(partners, cap),
        inclusion_mass.reshape(partners, cap),
        ports,
    )
    left, right, outgoing = lax.optimization_barrier((left, right, outgoing))
    arrived = lax.all_to_all(outgoing, "tile", split_axis=0, concat_axis=0, tiled=True)
    low_cap, high_cap = caps(*sizes, flow, visc, left, right)
    below = lax.ppermute(high_cap, "sec", up)
    above = lax.ppermute(low_cap, "sec", down)
    inlet = jnp.pad(jnp.stack([inlet_cell, port_match]), ((0, 0), (0, cap - inlet_cell.shape[0])))
    second, inlet_now = stencil(*sizes, flow, visc, left, right, below, above, inlet)
    flow_next, arrived_state = land(
        port_match, second, inlet_now, inlet, arrival_cell.reshape(partners, cap), arrived
    )
    return flow_next.reshape(flow_field.shape), arrived_state.reshape(inclusion_state.shape)


def solution(mesh):
    return jax.shard_map(
        on_device,
        mesh=mesh,
        in_specs=(
            P(None, "sec", "tile", None),
            P("sec", "tile", None),
            P(None, ("sec", "tile")),
            P(("sec", "tile")),
            P(("sec", "tile")),
            P(None, "sec", "tile", None, None),
            P("sec", "tile", None, None),
            P("sec", "tile", None, None),
            P("sec", "tile", None, None),
            P("sec", "tile", None),
            P("sec", "tile", None, None),
        ),
        out_specs=(P(None, "sec", "tile", None), P(None, "sec", "tile", None, None)),
        check_vma=False,
    )
```

```python
import functools

import jax
import jax.numpy as jnp
from jax import lax
from jax.experimental import pallas as pl
from jax.experimental.pallas import tpu as pltpu
from jax.sharding import PartitionSpec as P

VM = pl.BlockSpec(memory_space=pltpu.VMEM)
SM = pl.BlockSpec(memory_space=pltpu.SMEM)
HB = pl.BlockSpec(memory_space=pltpu.HBM)


def halves(value):
    high = value.astype(jnp.bfloat16)
    low = (value - high.astype(jnp.float32)).astype(jnp.bfloat16)
    return high, low


def column_hot(cells, depth):
    at = lax.broadcasted_iota(jnp.int32, (depth, cells.shape[1]), 0)
    return jnp.where(at == (cells & (depth - 1)), 1.0, 0.0).astype(jnp.bfloat16)


chunks = 4


def slip_kernel(GP, counts, flow_far, anchor_far, state_far, rate_far, mass_far, ports, far, out, flow, anchor, state, rate, mass, table, packed, sampled, sems, out_sems):
    comps, partners, cap = state.shape
    total, depth = flow.shape
    rows = total // comps
    shift = depth.bit_length() - 1
    cap_shift = cap.bit_length() - 1
    pairs = ((anchor_far, anchor), (flow_far, flow), (state_far, state), (rate_far, rate), (mass_far, mass))
    copies = [pltpu.make_async_copy(source, target, sems.at[i]) for i, (source, target) in enumerate(pairs)]
    for copy in copies:
        copy.start()
    lane = lax.broadcasted_iota(jnp.int32, (1, cap), 1)
    packed[...] = jnp.zeros_like(packed)
    copies[0].wait()

    def pack(p, base):
        begin = base & (cap - 1)
        spot = base >> cap_shift
        turned = pltpu.roll(anchor[pl.ds(p, 1), :], begin, 1)
        pltpu.store(packed.at[pl.ds(spot, 1), :], turned, mask=lane >= begin)
        pltpu.store(packed.at[pl.ds(spot + 1, 1), :], turned, mask=lane < begin)
        return base + counts[p]

    used = lax.fori_loop(0, partners, pack, 0, unroll=8)
    copies[1].wait()
    high, low = halves(flow[...])
    table[0:total] = high
    table[total:] = low

    def group(g, carry):
        first = g * GP
        cells = jnp.concatenate([packed[pl.ds(first + i, 1), :] for i in range(GP)], axis=1)
        hot = column_hot(cells, depth)
        picked = jnp.dot(table[...], hot, preferred_element_type=jnp.float32)
        row = lax.broadcasted_iota(jnp.int32, (rows, cells.shape[1]), 0) == (cells >> shift)
        parts = []
        for c in range(comps):
            both = picked[c * rows : (c + 1) * rows] + picked[total + c * rows : total + (c + 1) * rows]
            parts.append(jnp.sum(jnp.where(row, both, 0.0), axis=0, keepdims=True))
        found = jnp.concatenate(parts, axis=0)
        for i in range(GP):
            sampled[first + i] = found[:, i * cap : (i + 1) * cap]
        return carry

    lax.fori_loop(0, (used + GP * cap - 1) // (GP * cap), group, 0)
    for copy in copies[2:]:
        copy.wait()

    def finish(p, base):
        n = counts[p]
        begin = base & (cap - 1)
        spot = base >> cap_shift
        both = jnp.where(lane >= begin, sampled[spot], sampled[spot + 1])
        value = pltpu.roll(both, (cap - begin) & (cap - 1), 1)
        own = jnp.concatenate([state[c, pl.ds(p, 1), :] for c in range(comps)], axis=0)
        r = rate[pl.ds(p, 1), :]
        drop = r * (own - value)
        live = lane < n
        out[3 * p] = jnp.where(live, own - drop, 0.0)
        out[3 * p + 1] = jnp.where(live, mass[pl.ds(p, 1), :] * drop, 0.0)
        out[3 * p + 2] = ports[...]
        return base + n

    block = partners // chunks
    base = 0
    copies = []
    for i in range(chunks):
        base = lax.fori_loop(i * block, (i + 1) * block, finish, base, unroll=8)
        part = pl.ds(3 * i * block, 3 * block)
        copies.append(pltpu.make_async_copy(out.at[part], far.at[part], out_sems.at[i]))
        copies[i].start()
    for copy in copies:
        copy.wait()


def slip(counts, flow, anchor, state, rate, mass, ports, GP=8):
    comps, partners, cap = state.shape
    near = [pltpu.VMEM(x.shape, x.dtype) for x in (flow, anchor, state, rate, mass)]
    return pl.pallas_call(
        functools.partial(slip_kernel, GP),
        out_shape=jax.ShapeDtypeStruct((partners * 3, comps, cap), jnp.float32),
        in_specs=[SM] + [HB] * 5 + [VM],
        out_specs=HB,
        scratch_shapes=[pltpu.VMEM((partners * 3, comps, cap), jnp.float32)] + near
        + [
            pltpu.VMEM((2 * flow.shape[0], flow.shape[1]), jnp.bfloat16),
            pltpu.VMEM((partners + 8, cap), jnp.int32),
            pltpu.VMEM((partners + 8, comps, cap), jnp.float32),
            pltpu.SemaphoreType.DMA((5,)),
            pltpu.SemaphoreType.DMA((chunks,)),
        ],
        compiler_params=pltpu.CompilerParams(vmem_limit_bytes=60 * 1024 * 1024),
        cost_estimate=pl.CostEstimate(flops=2 * 8192 * 512 * 1024, bytes_accessed=2**21, transcendentals=0),
        name="slip",
    )(counts, flow, anchor, state, rate, mass, ports)


def land_kernel(GP, match, second, inlet_now, inlet, arrival, arrived, flow_out, state_out, rows_ref, last_ref, last, packed, sem):
    comps, partners, cap = state_out.shape
    total, depth = second.shape
    rows = total // comps
    shift = depth.bit_length() - 1
    cap_shift = cap.bit_length() - 1
    entries = match.shape[0]
    per = cap // comps
    nt = (((1,), (1,)), ((), ()))
    slot = lax.broadcasted_iota(jnp.int32, (1, cap), 1)

    def ends(p, carry):
        moved = arrived[3 * p]
        gift = arrived[3 * p + 1]
        for c in range(comps):
            state_out[c, pl.ds(p, 1), :] = moved[c : c + 1]
        biggest = jnp.max(jnp.abs(gift), axis=0, keepdims=True)
        last_ref[pl.ds(p, 1), :] = jnp.where(biggest > 0.0, slot + 1, 0)
        return carry

    lax.fori_loop(0, partners, ends, 0, unroll=8)
    last_ref[partners:, :] = jnp.zeros_like(last_ref[partners:, :])
    top = jnp.max(last_ref[...].T, axis=0, keepdims=True)
    last_ref[0:1, :] = top
    fetch = pltpu.make_async_copy(last_ref.at[0:1, :], last, sem)
    fetch.start()

    def spread(cells, values):
        row = lax.broadcasted_iota(jnp.int32, (rows, cells.shape[1]), 0) == (cells >> shift)
        high, low = halves(values)
        parts = []
        for part in (high.astype(jnp.float32), low.astype(jnp.float32)):
            for c in range(comps):
                parts.append(jnp.where(row, part[c : c + 1], 0.0).astype(jnp.bfloat16))
        return jnp.concatenate(parts, axis=0)

    def product(cells, values):
        both = lax.dot_general(spread(cells, values), column_hot(cells, depth), nt, preferred_element_type=jnp.float32)
        return both[:total] + both[total:]

    rows_ref[...] = jnp.zeros_like(rows_ref)
    for k in range(entries):
        port = match[k]
        device = port // entries
        rows_ref[k : k + 1, :] = arrived[3 * (device % partners) + 2, pl.ds(device // partners, 1), :]
    turned = rows_ref[...].T
    which = inlet[1:2, :] % entries
    pick = lax.broadcasted_iota(jnp.int32, (per, cap), 0) == which
    target = jnp.concatenate(
        [jnp.sum(jnp.where(pick, turned[c * per : (c + 1) * per], 0.0), axis=0, keepdims=True) for c in range(comps)], axis=0
    )
    change = jnp.where(slot < entries, 0.5 * (target - inlet_now[...]), 0.0)
    flow_out[...] = second[...] + product(inlet[0:1, :], change)
    packed[...] = jnp.zeros_like(packed)
    fetch.wait()

    def pack(p, base):
        begin = base & (cap - 1)
        spot = base >> cap_shift
        cells = arrival[pl.ds(p, 1), :].astype(jnp.float32)
        both = jnp.concatenate([arrived[3 * p + 1], jnp.broadcast_to(cells, (8 - comps, cap))], axis=0)
        turned = pltpu.roll(both, begin, 1)
        wide = lax.broadcasted_iota(jnp.int32, (8, cap), 1)
        pltpu.store(packed.at[spot], turned, mask=wide >= begin)
        pltpu.store(packed.at[spot + 1], turned, mask=wide < begin)
        return base + last[0, p]

    used = lax.fori_loop(0, partners, pack, 0, unroll=8)

    def group(g, carry):
        first = g * GP
        both = jnp.concatenate([packed[first + i] for i in range(GP)], axis=1)
        flow_out[...] += product(both[comps : comps + 1].astype(jnp.int32), both[:comps])
        return carry

    lax.fori_loop(0, (used + GP * cap - 1) // (GP * cap), group, 0)


def land(match, second, inlet_now, inlet, arrival, arrived, GP=8):
    partners, cap = arrival.shape
    comps = arrived.shape[1]
    return pl.pallas_call(
        functools.partial(land_kernel, GP),
        out_shape=(
            jax.ShapeDtypeStruct(second.shape, jnp.float32),
            jax.ShapeDtypeStruct((comps, partners, cap), jnp.float32),
        ),
        in_specs=[SM] + [VM] * 5,
        out_specs=(VM, VM),
        scratch_shapes=[
            pltpu.VMEM((cap, cap), jnp.float32),
            pltpu.VMEM((cap, cap), jnp.int32),
            pltpu.SMEM((1, cap), jnp.int32),
            pltpu.VMEM((partners + 8, 8, cap), jnp.float32),
            pltpu.SemaphoreType.DMA,
        ],
        compiler_params=pltpu.CompilerParams(vmem_limit_bytes=24 * 1024 * 1024),
        cost_estimate=pl.CostEstimate(flops=2 * 8192 * 512 * 1024, bytes_accessed=2**21, transcendentals=0),
        name="land",
    )(match, second, inlet_now, inlet, arrival, arrived)


def edge_kernel(comps, depth_z, width, flow, viscosity, low_out, high_out):
    for k in range(comps * depth_z):
        low_out[2 * k : 2 * k + 2, :] = flow[k * width : k * width + 2, :]
        high_out[2 * k : 2 * k + 2, :] = flow[(k + 1) * width - 2 : (k + 1) * width, :]
    base = 2 * comps * depth_z
    for z in range(depth_z):
        low_out[base + z : base + z + 1, :] = viscosity[z * width : z * width + 1, :]
        high_out[base + z : base + z + 1, :] = viscosity[(z + 1) * width - 1 : (z + 1) * width, :]


def edges(comps, depth_z, width, flow, viscosity):
    shape = jax.ShapeDtypeStruct(((2 * comps + 1) * depth_z, flow.shape[1]), jnp.float32)
    return pl.pallas_call(
        functools.partial(edge_kernel, comps, depth_z, width),
        out_shape=(shape, shape),
        in_specs=[VM] * 2,
        out_specs=(VM, VM),
        compiler_params=pltpu.CompilerParams(vmem_limit_bytes=60 * 1024 * 1024),
        name="edges",
    )(flow, viscosity)


def side_tile(tile, left, right, k, reach):
    tile[...] = jnp.zeros_like(tile)
    tile[0:reach, :] = right[2 * k : 2 * k + reach, :]
    tile[8 - reach : 8, :] = left[2 * k + 2 - reach : 2 * k + 2, :]


def cap_kernel(comps, depth_z, width, flow, viscosity, left, right, low_out, high_out, tile):
    per = 2 * width + 8
    for c in range(comps):
        for out, near, far in ((low_out, 0, 1), (high_out, depth_z - 1, depth_z - 2)):
            k = c * depth_z + near
            out[c * per : c * per + width, :] = flow[k * width : (k + 1) * width, :]
            side_tile(tile, left, right, k, 1)
            out[c * per + width : c * per + width + 8, :] = tile[...]
            k = c * depth_z + far
            out[c * per + width + 8 : (c + 1) * per, :] = flow[k * width : (k + 1) * width, :]
    low_out[comps * per :, :] = viscosity[0:width, :]
    high_out[comps * per :, :] = viscosity[(depth_z - 1) * width : depth_z * width, :]


def caps(comps, depth_z, width, flow, viscosity, left, right):
    shape = jax.ShapeDtypeStruct((comps * (2 * width + 8) + width, flow.shape[1]), jnp.float32)
    return pl.pallas_call(
        functools.partial(cap_kernel, comps, depth_z, width),
        out_shape=(shape, shape),
        in_specs=[VM] * 4,
        out_specs=(VM, VM),
        scratch_shapes=[pltpu.VMEM((8, flow.shape[1]), jnp.float32)],
        compiler_params=pltpu.CompilerParams(vmem_limit_bytes=24 * 1024 * 1024),
        name="caps",
    )(flow, viscosity, left, right)


def tendency(plane, upper, lower, viscosity, keep):
    place = lax.broadcasted_iota(jnp.int32, (1, viscosity.shape[1]), 1)
    depth = viscosity.shape[1]
    centers, laps, dz, dx, dy = [], [], [], [], []
    for c in range(len(plane)):
        whole = plane[c]
        center = whole[:keep]
        up_x = pltpu.roll(whole, whole.shape[0] - 1, 0)[:keep]
        low_x = pltpu.roll(whole, 1, 0)[:keep]
        up_y = jnp.where(place == depth - 1, 0.0, pltpu.roll(center, depth - 1, 1))
        low_y = jnp.where(place == 0, 0.0, pltpu.roll(center, 1, 1))
        centers.append(center)
        laps.append((upper[c] + lower[c]) + (up_x + low_x) + (up_y + low_y) - 6.0 * center)
        dz.append(upper[c] - lower[c])
        dx.append(up_x - low_x)
        dy.append(up_y - low_y)
    strain = sum(d[c] * d[c] for c in range(3) for d in (dz, dx, dy)) * 0.25
    eddy = viscosity * (1.0 + strain / (1.0 + strain))
    out = []
    for c in range(len(plane)):
        carried = centers[0] * dz[c] + centers[1] * dx[c] + centers[2] * dy[c]
        out.append(0.5 * (eddy * laps[c]) - 0.25 * carried)
    return centers, out


def inner_kernel(comps, depth_z, width, flow, viscosity, left, right, state, visc, first, second):
    depth = flow.shape[1]
    wide = width + 8
    base = 2 * comps * depth_z
    blank = jnp.zeros((8, depth), jnp.float32)
    for z in range(depth_z):
        for c in range(comps):
            k = c * depth_z + z
            state[c, z, 0:width, :] = flow[k * width : (k + 1) * width, :]
            state[c, z, width:wide, :] = blank
            state[c, z, width : width + 2, :] = right[2 * k : 2 * k + 2, :]
            state[c, z, wide - 2 : wide, :] = left[2 * k : 2 * k + 2, :]
        visc[z, 0:width, :] = viscosity[z * width : (z + 1) * width, :]
        visc[z, width:wide, :] = blank
        visc[z, width : width + 1, :] = right[base + z : base + z + 1, :]
        visc[z, wide - 1 : wide, :] = left[base + z : base + z + 1, :]

    def one(z, carry):
        plane, upper, lower = ([state[c, z + d] for c in range(comps)] for d in (0, 1, -1))
        centers, change = tendency(plane, upper, lower, visc[z], wide)
        for c in range(comps):
            first[c, z - 1] = centers[c] + change[c]
        return carry

    lax.fori_loop(1, depth_z - 1, one, 0)

    def two(z, carry):
        plane = [first[c, z - 1] for c in range(comps)]
        upper, lower = ([first[c, z - 1 + d, 0:width, :] for c in range(comps)] for d in (1, -1))
        centers, change = tendency(plane, upper, lower, visc[z, 0:width, :], width)
        for c in range(comps):
            second[c, z - 2] = 0.5 * state[c, z, 0:width, :] + 0.5 * (centers[c] + change[c])
        return carry

    lax.fori_loop(2, depth_z - 2, two, 0)


def inner(comps, depth_z, width, flow, viscosity, left, right):
    depth = flow.shape[1]
    wide = width + 8
    shapes = ((comps, depth_z, wide), (depth_z, wide), (comps, depth_z - 2, wide), (comps, depth_z - 4, width))
    return pl.pallas_call(
        functools.partial(inner_kernel, comps, depth_z, width),
        out_shape=tuple(jax.ShapeDtypeStruct(shape + (depth,), jnp.float32) for shape in shapes),
        in_specs=[VM] * 4,
        out_specs=(VM,) * 4,
        compiler_params=pltpu.CompilerParams(vmem_limit_bytes=24 * 1024 * 1024),
        cost_estimate=pl.CostEstimate(flops=10**7, bytes_accessed=2**22, transcendentals=0),
        name="inner",
    )(flow, viscosity, left, right)


def outer_kernel(state, visc, first, second, below, above, inlet, second_out, inlet_now, rim, table):
    comps, depth_z, wide, depth = state.shape
    width = second.shape[2]
    per = width + wide
    rows = depth_z * width
    total = comps * rows
    last = depth_z - 1

    def near(source):
        return [source[c * per : c * per + wide, :] for c in range(comps)]

    def far(source):
        return [source[c * per + wide : (c + 1) * per, :] for c in range(comps)]

    def own(z, keep):
        return [state[c, z, 0:keep, :] for c in range(comps)]

    def put(slot, keep, plane, upper, lower, viscosity):
        centers, change = tendency(plane, upper, lower, viscosity, keep)
        for c in range(comps):
            rim[c, slot, 0:keep, :] = centers[c] + change[c]

    put(0, width, near(below), own(0, width), far(below), below[comps * per :, :])
    put(1, wide, own(0, wide), own(1, wide), near(below), visc[0])
    put(2, wide, own(last, wide), near(above), own(last - 1, wide), visc[last])
    put(3, width, near(above), far(above), own(last, width), above[comps * per :, :])

    def started(z, keep):
        if z < 1 or z > last - 1:
            slot = {-1: 0, 0: 1, last: 2, last + 1: 3}[z]
            return [rim[c, slot, 0:keep, :] for c in range(comps)]
        return [first[c, z - 1, 0:keep, :] for c in range(comps)]

    def keep_value(c, z, value):
        spot = (c * depth_z + z) * width
        count = value.shape[0]
        second_out[spot : spot + count, :] = value
        high, low = halves(value)
        table[spot : spot + count] = high
        table[total + spot : total + spot + count] = low

    for z in (0, 1, last - 1, last):
        centers, change = tendency(
            started(z, wide), started(z + 1, width), started(z - 1, width), visc[z, 0:width, :], width
        )
        for c in range(comps):
            keep_value(c, z, 0.5 * state[c, z, 0:width, :] + 0.5 * (centers[c] + change[c]))
    for c in range(comps):
        for z in range(2, last - 1):
            keep_value(c, z, second[c, z - 2])

    cells = inlet[0:1, :]
    picked = jnp.dot(table[...], column_hot(cells, depth), preferred_element_type=jnp.float32)
    row = lax.broadcasted_iota(jnp.int32, (rows, cells.shape[1]), 0) == (cells >> (depth.bit_length() - 1))
    for c in range(comps):
        both = picked[c * rows : (c + 1) * rows] + picked[total + c * rows : total + (c + 1) * rows]
        inlet_now[c : c + 1, :] = jnp.sum(jnp.where(row, both, 0.0), axis=0, keepdims=True)


def outer(state, visc, first, second, below, above, inlet):
    comps, depth_z, wide, depth = state.shape
    total = comps * depth_z * second.shape[2]
    return pl.pallas_call(
        outer_kernel,
        out_shape=(
            jax.ShapeDtypeStruct((total, depth), jnp.float32),
            jax.ShapeDtypeStruct((comps, inlet.shape[1]), jnp.float32),
        ),
        in_specs=[VM] * 7,
        out_specs=(VM, VM),
        scratch_shapes=[
            pltpu.VMEM((comps, 4, wide, depth), jnp.float32),
            pltpu.VMEM((2 * total, depth), jnp.bfloat16),
        ],
        compiler_params=pltpu.CompilerParams(vmem_limit_bytes=24 * 1024 * 1024),
        cost_estimate=pl.CostEstimate(flops=10**7, bytes_accessed=2**22, transcendentals=0),
        name="outer",
    )(state, visc, first, second, below, above, inlet)


def on_device(
    flow_field,
    viscosity,
    port_plane,
    port_match,
    inlet_cell,
    inclusion_state,
    response_rate,
    inclusion_mass,
    anchor_cell,
    live_counts,
    arrival_cell,
):
    comps, depth_z, width, depth = flow_field.shape
    partners, cap = anchor_cell.shape[2:]
    sizes = (comps, depth_z, width)
    flow = flow_field.reshape(-1, depth)
    visc = viscosity.reshape(-1, depth)
    count = lax.axis_size("tile")
    forth = [(i, i + 1) for i in range(count - 1)]
    back = [(i + 1, i) for i in range(count - 1)]
    levels = lax.axis_size("sec")
    up = [(i, i + 1) for i in range(levels - 1)]
    down = [(i + 1, i) for i in range(levels - 1)]

    ports = lax.all_gather(port_plane.reshape(1, -1), "sec", axis=0, tiled=True)
    low_edge, high_edge = edges(*sizes, flow, visc)
    left = lax.ppermute(high_edge, "tile", forth)
    right = lax.ppermute(low_edge, "tile", back)
    counts, low_edge, high_edge = lax.optimization_barrier((live_counts.reshape(-1), low_edge, high_edge))
    outgoing = slip(
        counts,
        flow,
        anchor_cell.reshape(partners, cap),
        inclusion_state.reshape(comps, partners, cap),
        response_rate.reshape(partners, cap),
        inclusion_mass.reshape(partners, cap),
        ports,
    )
    left, right, outgoing = lax.optimization_barrier((left, right, outgoing))
    arrived = lax.all_to_all(outgoing, "tile", split_axis=0, concat_axis=0, tiled=True)
    low_cap, high_cap = caps(*sizes, flow, visc, left, right)
    below = lax.ppermute(high_cap, "sec", up)
    above = lax.ppermute(low_cap, "sec", down)
    inlet = jnp.pad(jnp.stack([inlet_cell, port_match]), ((0, 0), (0, cap - inlet_cell.shape[0])))
    middle = inner(*sizes, flow, visc, left, right)
    second, inlet_now = outer(*middle, below, above, inlet)
    flow_next, arrived_state = land(
        port_match, second, inlet_now, inlet, arrival_cell.reshape(partners, cap), arrived
    )
    return flow_next.reshape(flow_field.shape), arrived_state.reshape(inclusion_state.shape)


def solution(mesh):
    return jax.shard_map(
        on_device,
        mesh=mesh,
        in_specs=(
            P(None, "sec", "tile", None),
            P("sec", "tile", None),
            P(None, ("sec", "tile")),
            P(("sec", "tile")),
            P(("sec", "tile")),
            P(None, "sec", "tile", None, None),
            P("sec", "tile", None, None),
            P("sec", "tile", None, None),
            P("sec", "tile", None, None),
            P("sec", "tile", None),
            P("sec", "tile", None, None),
        ),
        out_specs=(P(None, "sec", "tile", None), P(None, "sec", "tile", None, None)),
        check_vma=False,
    )
```

```python
import functools

import jax
import jax.numpy as jnp
from jax import lax
from jax.experimental import pallas as pl
from jax.experimental.pallas import tpu as pltpu
from jax.sharding import PartitionSpec as P

VM = pl.BlockSpec(memory_space=pltpu.VMEM)
SM = pl.BlockSpec(memory_space=pltpu.SMEM)
HB = pl.BlockSpec(memory_space=pltpu.HBM)


def halves(value):
    high = value.astype(jnp.bfloat16)
    low = (value - high.astype(jnp.float32)).astype(jnp.bfloat16)
    return high, low


def column_hot(cells, depth):
    at = lax.broadcasted_iota(jnp.int32, (depth, cells.shape[1]), 0)
    return jnp.where(at == (cells & (depth - 1)), 1.0, 0.0).astype(jnp.bfloat16)


def sample_kernel(GP, counts, flow, anchor, sampled, table, packed):
    partners, cap = anchor.shape
    total, depth = flow.shape
    comps = sampled.shape[1]
    rows = total // comps
    shift = depth.bit_length() - 1
    cap_shift = cap.bit_length() - 1
    lane = lax.broadcasted_iota(jnp.int32, (1, cap), 1)
    packed[...] = jnp.zeros_like(packed)

    def pack(p, base):
        begin = base & (cap - 1)
        spot = base >> cap_shift
        turned = pltpu.roll(anchor[pl.ds(p, 1), :], begin, 1)
        pltpu.store(packed.at[pl.ds(spot, 1), :], turned, mask=lane >= begin)
        pltpu.store(packed.at[pl.ds(spot + 1, 1), :], turned, mask=lane < begin)
        return base + counts[p]

    used = lax.fori_loop(0, partners, pack, 0, unroll=8)
    high, low = halves(flow[...])
    table[0:total] = high
    table[total:] = low

    def group(g, carry):
        first = g * GP
        cells = jnp.concatenate([packed[pl.ds(first + i, 1), :] for i in range(GP)], axis=1)
        hot = column_hot(cells, depth)
        picked = jnp.dot(table[...], hot, preferred_element_type=jnp.float32)
        row = lax.broadcasted_iota(jnp.int32, (rows, cells.shape[1]), 0) == (cells >> shift)
        parts = []
        for c in range(comps):
            both = picked[c * rows : (c + 1) * rows] + picked[total + c * rows : total + (c + 1) * rows]
            parts.append(jnp.sum(jnp.where(row, both, 0.0), axis=0, keepdims=True))
        found = jnp.concatenate(parts, axis=0)
        for i in range(GP):
            sampled[first + i] = found[:, i * cap : (i + 1) * cap]
        return carry

    lax.fori_loop(0, (used + GP * cap - 1) // (GP * cap), group, 0)


def sample(comps, counts, flow, anchor, GP=4):
    partners, cap = anchor.shape
    return pl.pallas_call(
        functools.partial(sample_kernel, GP),
        out_shape=jax.ShapeDtypeStruct((partners + 8, comps, cap), jnp.float32),
        in_specs=[SM, VM, VM],
        out_specs=VM,
        scratch_shapes=[
            pltpu.VMEM((2 * flow.shape[0], flow.shape[1]), jnp.bfloat16),
            pltpu.VMEM((partners + 8, cap), jnp.int32),
        ],
        compiler_params=pltpu.CompilerParams(vmem_limit_bytes=24 * 1024 * 1024),
        cost_estimate=pl.CostEstimate(flops=2 * 8192 * 512 * 1024, bytes_accessed=2**21, transcendentals=0),
        name="sample",
    )(counts, flow, anchor)


chunks = 4


def slip_kernel(counts, sampled, state, rate, mass, ports, above, across, below, far, out, whole, out_sems):
    comps, partners, cap = state.shape
    per = ports.shape[1]
    cap_shift = cap.bit_length() - 1
    last = above.shape[0] - 8
    lane = lax.broadcasted_iota(jnp.int32, (1, cap), 1)
    whole[:, 0:per] = ports[...]
    whole[:, per : 2 * per] = above[last : last + comps, 0:per]
    whole[:, 2 * per : 3 * per] = across[...]
    whole[:, 3 * per :] = below[last : last + comps, 0:per]

    def finish(p, base):
        n = counts[p]
        begin = base & (cap - 1)
        spot = base >> cap_shift
        both = jnp.where(lane >= begin, sampled[spot], sampled[spot + 1])
        value = pltpu.roll(both, (cap - begin) & (cap - 1), 1)
        own = jnp.concatenate([state[c, pl.ds(p, 1), :] for c in range(comps)], axis=0)
        r = rate[pl.ds(p, 1), :]
        drop = r * (own - value)
        live = lane < n
        out[3 * p] = jnp.where(live, own - drop, 0.0)
        out[3 * p + 1] = jnp.where(live, mass[pl.ds(p, 1), :] * drop, 0.0)
        out[3 * p + 2] = whole[...]
        return base + n

    block = partners // chunks
    base = 0
    copies = []
    for i in range(chunks):
        base = lax.fori_loop(i * block, (i + 1) * block, finish, base, unroll=8)
        part = pl.ds(3 * i * block, 3 * block)
        copies.append(pltpu.make_async_copy(out.at[part], far.at[part], out_sems.at[i]))
        copies[i].start()
    for copy in copies:
        copy.wait()


def slip(counts, sampled, state, rate, mass, ports, above, across, below):
    comps, partners, cap = state.shape
    return pl.pallas_call(
        slip_kernel,
        out_shape=jax.ShapeDtypeStruct((partners * 3, comps, cap), jnp.float32),
        in_specs=[SM] + [VM] * 8,
        out_specs=HB,
        scratch_shapes=[
            pltpu.VMEM((partners * 3, comps, cap), jnp.float32),
            pltpu.VMEM((comps, cap), jnp.float32),
            pltpu.SemaphoreType.DMA((chunks,)),
        ],
        compiler_params=pltpu.CompilerParams(vmem_limit_bytes=24 * 1024 * 1024),
        cost_estimate=pl.CostEstimate(flops=2 * 10**6, bytes_accessed=2**20, transcendentals=0),
        name="slip",
    )(counts, sampled, state, rate, mass, ports, above, across, below)


def land_kernel(GP, match, second, inlet_now, inlet, arrival, arrived, flow_out, state_out, last_ref, last, packed, sem):
    comps, partners, cap = state_out.shape
    total, depth = second.shape
    rows = total // comps
    shift = depth.bit_length() - 1
    cap_shift = cap.bit_length() - 1
    entries = match.shape[0]
    per = entries
    nt = (((1,), (1,)), ((), ()))
    slot = lax.broadcasted_iota(jnp.int32, (1, cap), 1)

    def ends(p, carry):
        moved = arrived[3 * p]
        gift = arrived[3 * p + 1]
        for c in range(comps):
            state_out[c, pl.ds(p, 1), :] = moved[c : c + 1]
        biggest = jnp.max(jnp.abs(gift), axis=0, keepdims=True)
        last_ref[pl.ds(p, 1), :] = jnp.where(biggest > 0.0, slot + 1, 0)
        return carry

    lax.fori_loop(0, partners, ends, 0, unroll=8)
    last_ref[partners:, :] = jnp.zeros_like(last_ref[partners:, :])
    top = jnp.max(last_ref[...].T, axis=0, keepdims=True)
    last_ref[0:1, :] = top
    fetch = pltpu.make_async_copy(last_ref.at[0:1, :], last, sem)
    fetch.start()

    def spread(cells, values):
        row = lax.broadcasted_iota(jnp.int32, (rows, cells.shape[1]), 0) == (cells >> shift)
        high, low = halves(values)
        parts = []
        for part in (high.astype(jnp.float32), low.astype(jnp.float32)):
            for c in range(comps):
                parts.append(jnp.where(row, part[c : c + 1], 0.0).astype(jnp.bfloat16))
        return jnp.concatenate(parts, axis=0)

    def product(cells, values):
        both = lax.dot_general(spread(cells, values), column_hot(cells, depth), nt, preferred_element_type=jnp.float32)
        return both[:total] + both[total:]

    section = lax.axis_index("sec")
    sections = cap // per
    target = jnp.zeros((comps, cap), jnp.float32)
    for k in range(entries):
        port = match[k]
        device = port // entries
        place = (device // partners + sections - section) % sections * per + port % entries
        turned = pltpu.roll(arrived[3 * (device % partners) + 2], (k + cap - place) % cap, 1)
        target = jnp.where(slot == k, turned, target)
    change = jnp.where(slot < entries, 0.5 * (target - inlet_now[...]), 0.0)
    flow_out[...] = second[...] + product(inlet[0:1, :], change)
    packed[...] = jnp.zeros_like(packed)
    fetch.wait()

    def pack(p, base):
        begin = base & (cap - 1)
        spot = base >> cap_shift
        cells = arrival[pl.ds(p, 1), :].astype(jnp.float32)
        both = jnp.concatenate([arrived[3 * p + 1], jnp.broadcast_to(cells, (8 - comps, cap))], axis=0)
        turned = pltpu.roll(both, begin, 1)
        wide = lax.broadcasted_iota(jnp.int32, (8, cap), 1)
        pltpu.store(packed.at[spot], turned, mask=wide >= begin)
        pltpu.store(packed.at[spot + 1], turned, mask=wide < begin)
        return base + last[0, p]

    used = lax.fori_loop(0, partners, pack, 0, unroll=8)

    def group(g, carry):
        first = g * GP
        both = jnp.concatenate([packed[first + i] for i in range(GP)], axis=1)
        flow_out[...] += product(both[comps : comps + 1].astype(jnp.int32), both[:comps])
        return carry

    lax.fori_loop(0, (used + GP * cap - 1) // (GP * cap), group, 0)


def land(match, second, inlet_now, inlet, arrival, arrived, GP=8):
    partners, cap = arrival.shape
    comps = arrived.shape[1]
    return pl.pallas_call(
        functools.partial(land_kernel, GP),
        out_shape=(
            jax.ShapeDtypeStruct(second.shape, jnp.float32),
            jax.ShapeDtypeStruct((comps, partners, cap), jnp.float32),
        ),
        in_specs=[SM] + [VM] * 5,
        out_specs=(VM, VM),
        scratch_shapes=[
            pltpu.VMEM((cap, cap), jnp.int32),
            pltpu.SMEM((1, cap), jnp.int32),
            pltpu.VMEM((partners + 8, 8, cap), jnp.float32),
            pltpu.SemaphoreType.DMA,
        ],
        compiler_params=pltpu.CompilerParams(vmem_limit_bytes=24 * 1024 * 1024),
        cost_estimate=pl.CostEstimate(flops=2 * 8192 * 512 * 1024, bytes_accessed=2**21, transcendentals=0),
        name="land",
    )(match, second, inlet_now, inlet, arrival, arrived)


def tendency(plane, upper, lower, viscosity, keep):
    place = lax.broadcasted_iota(jnp.int32, (1, viscosity.shape[1]), 1)
    depth = viscosity.shape[1]
    centers, laps, dz, dx, dy = [], [], [], [], []
    for c in range(len(plane)):
        whole = plane[c]
        center = whole[:keep]
        up_x = pltpu.roll(whole, whole.shape[0] - 1, 0)[:keep]
        low_x = pltpu.roll(whole, 1, 0)[:keep]
        up_y = jnp.where(place == depth - 1, 0.0, pltpu.roll(center, depth - 1, 1))
        low_y = jnp.where(place == 0, 0.0, pltpu.roll(center, 1, 1))
        centers.append(center)
        laps.append((upper[c] + lower[c]) + (up_x + low_x) + (up_y + low_y) - 6.0 * center)
        dz.append(upper[c] - lower[c])
        dx.append(up_x - low_x)
        dy.append(up_y - low_y)
    strain = sum(d[c] * d[c] for c in range(3) for d in (dz, dx, dy)) * 0.25
    eddy = viscosity * (1.0 + strain / (1.0 + strain))
    out = []
    for c in range(len(plane)):
        carried = centers[0] * dz[c] + centers[1] * dx[c] + centers[2] * dy[c]
        out.append(0.5 * (eddy * laps[c]) - 0.25 * carried)
    return centers, out


def cap_kernel(comps, depth_z, width, flow, viscosity, ports, low_out, high_out, tile, sems):
    tile[...] = jnp.zeros_like(tile)
    tile[0:comps, 0 : ports.shape[1]] = ports[...]
    copies = []

    def copy(source, target):
        copies.append(pltpu.make_async_copy(source, target, sems.at[len(copies)]))
        copies[-1].start()

    two = 2 * width
    last = (depth_z - 1) * width
    for c in range(comps):
        base = c * depth_z * width
        copy(flow.at[base : base + two, :], low_out.at[c * two : (c + 1) * two, :])
        copy(flow.at[base + last - width : base + last + width, :], high_out.at[c * two : (c + 1) * two, :])
    base = comps * two
    copy(viscosity.at[0:width, :], low_out.at[base : base + width, :])
    copy(viscosity.at[last : last + width, :], high_out.at[base : base + width, :])
    copy(tile, low_out.at[base + width :, :])
    copy(tile, high_out.at[base + width :, :])
    for started in copies:
        started.wait()


def caps(comps, depth_z, width, flow, viscosity, ports):
    shape = jax.ShapeDtypeStruct((2 * comps * width + width + 8, flow.shape[1]), jnp.float32)
    return pl.pallas_call(
        functools.partial(cap_kernel, comps, depth_z, width),
        out_shape=(shape, shape),
        in_specs=[HB, HB, VM],
        out_specs=(HB, HB),
        scratch_shapes=[pltpu.VMEM((8, flow.shape[1]), jnp.float32), pltpu.SemaphoreType.DMA((2 * comps + 4,))],
        compiler_params=pltpu.CompilerParams(vmem_limit_bytes=60 * 1024 * 1024),
        name="caps",
    )(flow, viscosity, ports)


def edge_kernel(comps, depth_z, width, flow, viscosity, below, above, low_out, high_out, bottom, top):
    section = lax.axis_index("sec")
    bottom[...] = jnp.where(section > 0, below[0 : bottom.shape[0], :], 0.0)
    top[...] = jnp.where(section < lax.axis_size("sec") - 1, above[0 : top.shape[0], :], 0.0)
    two = 2 * width
    for k in range(comps * depth_z):
        low_out[2 * k : 2 * k + 2, :] = flow[k * width : k * width + 2, :]
        high_out[2 * k : 2 * k + 2, :] = flow[(k + 1) * width - 2 : (k + 1) * width, :]
    base = 2 * comps * depth_z
    for c in range(comps):
        low_out[base + 2 * c : base + 2 * c + 1, :] = bottom[c * two + width : c * two + width + 1, :]
        low_out[base + 2 * c + 1 : base + 2 * c + 2, :] = top[c * two : c * two + 1, :]
        high_out[base + 2 * c : base + 2 * c + 1, :] = bottom[(c + 1) * two - 1 : (c + 1) * two, :]
        high_out[base + 2 * c + 1 : base + 2 * c + 2, :] = top[c * two + width - 1 : c * two + width, :]
    base += 2 * comps
    for z in range(depth_z):
        low_out[base + z : base + z + 1, :] = viscosity[z * width : z * width + 1, :]
        high_out[base + z : base + z + 1, :] = viscosity[(z + 1) * width - 1 : (z + 1) * width, :]


def edges(comps, depth_z, width, flow, viscosity, below, above):
    depth = flow.shape[1]
    shape = jax.ShapeDtypeStruct((2 * comps * (depth_z + 1) + depth_z, depth), jnp.float32)
    halo = jax.ShapeDtypeStruct(((2 * comps + 1) * width, depth), jnp.float32)
    return pl.pallas_call(
        functools.partial(edge_kernel, comps, depth_z, width),
        out_shape=(shape, shape, halo, halo),
        in_specs=[VM] * 4,
        out_specs=(VM,) * 4,
        compiler_params=pltpu.CompilerParams(vmem_limit_bytes=24 * 1024 * 1024),
        name="edges",
    )(flow, viscosity, below, above)


def inner_kernel(comps, depth_z, width, flow, viscosity, below, above, first):
    two = 2 * width

    def own(z):
        if z < 0:
            return [below[c * two + (2 + z) * width : c * two + (3 + z) * width, :] for c in range(comps)]
        if z >= depth_z:
            return [above[c * two + (z - depth_z) * width : c * two + (z - depth_z + 1) * width, :] for c in range(comps)]
        return [flow[(c * depth_z + z) * width : (c * depth_z + z + 1) * width, :] for c in range(comps)]

    for z in range(-1, depth_z + 1):
        if z < 0:
            visc = below[comps * two :, :]
        elif z == depth_z:
            visc = above[comps * two :, :]
        else:
            visc = viscosity[z * width : (z + 1) * width, :]
        centers, change = tendency(own(z), own(z + 1), own(z - 1), visc, width)
        for c in range(comps):
            first[c, z + 1, 0:width, :] = centers[c] + change[c]


def inner(comps, depth_z, width, flow, viscosity, below, above):
    depth = flow.shape[1]
    return pl.pallas_call(
        functools.partial(inner_kernel, comps, depth_z, width),
        out_shape=jax.ShapeDtypeStruct((comps, depth_z + 2, width, depth), jnp.float32),
        in_specs=[VM] * 4,
        out_specs=VM,
        compiler_params=pltpu.CompilerParams(vmem_limit_bytes=24 * 1024 * 1024),
        cost_estimate=pl.CostEstimate(flops=10**7, bytes_accessed=2**22, transcendentals=0),
        name="inner",
    )(flow, viscosity, below, above)


def outer_kernel(comps, depth_z, width, flow, viscosity, below, above, first, left, right, inlet, second_out, inlet_now, strip, visc, started, table):
    depth = flow.shape[1]
    two = 2 * width
    rows = depth_z * width
    total = comps * rows
    base = 2 * comps * depth_z
    strip[...] = jnp.zeros_like(strip)
    visc[...] = jnp.zeros_like(visc)
    for c in range(comps):
        for z in range(-2, depth_z + 2):
            if z < 0:
                ref, spot = below, c * two + (2 + z) * width
            elif z >= depth_z:
                ref, spot = above, c * two + (z - depth_z) * width
            else:
                ref, spot = flow, (c * depth_z + z) * width
            strip[c, z + 2, 2:4, :] = ref[spot : spot + 2, :]
            strip[c, z + 2, 4:6, :] = ref[spot + width - 2 : spot + width, :]
            if 0 <= z < depth_z:
                k = 2 * (c * depth_z + z)
                strip[c, z + 2, 0:2, :] = left[k : k + 2, :]
                strip[c, z + 2, 6:8, :] = right[k : k + 2, :]
            elif z in (-1, depth_z):
                k = base + 2 * c + (z == depth_z)
                strip[c, z + 2, 1:2, :] = left[k : k + 1, :]
                strip[c, z + 2, 6:7, :] = right[k : k + 1, :]
    side = base + 2 * comps
    for z in range(-1, depth_z + 1):
        if z < 0:
            ref, spot = below, comps * two
        elif z == depth_z:
            ref, spot = above, comps * two
        else:
            ref, spot = viscosity, z * width
            visc[z + 1, 1:2, :] = left[side + z : side + z + 1, :]
            visc[z + 1, 6:7, :] = right[side + z : side + z + 1, :]
        visc[z + 1, 2:4, :] = ref[spot : spot + 2, :]
        visc[z + 1, 4:6, :] = ref[spot + width - 2 : spot + width, :]

    place = lax.broadcasted_iota(jnp.int32, (width, 1), 0)
    blank = jnp.zeros((6, depth), jnp.float32)

    def one(z, carry):
        plane, upper, lower = ([strip[c, z + 1 + d] for c in range(comps)] for d in (0, 1, -1))
        centers, change = tendency(plane, upper, lower, visc[z], 8)
        for c in range(comps):
            edge = centers[c] + change[c]
            mine = first[c, z]
            mine = jnp.where(place == 0, edge[2:3], mine)
            mine = jnp.where(place == width - 1, edge[5:6], mine)
            started[c, z, 0:width, :] = mine
            started[c, z, width : width + 8, :] = jnp.concatenate([edge[6:7], blank, edge[1:2]], axis=0)
        return carry

    lax.fori_loop(0, depth_z + 2, one, 0)

    def second(z, carry):
        plane = [started[c, z + 1] for c in range(comps)]
        upper, lower = ([started[c, z + 1 + d, 0:width, :] for c in range(comps)] for d in (1, -1))
        at = pl.multiple_of(z * width, width)
        centers, change = tendency(plane, upper, lower, viscosity[pl.ds(at, width), :], width)
        for c in range(comps):
            spot = pl.multiple_of((c * depth_z + z) * width, width)
            value = 0.5 * flow[pl.ds(spot, width), :] + 0.5 * (centers[c] + change[c])
            second_out[pl.ds(spot, width), :] = value
            high, low = halves(value)
            table[pl.ds(spot, width), :] = high
            table[pl.ds(total + spot, width), :] = low
        return carry

    lax.fori_loop(0, depth_z, second, 0)

    cells = inlet[0:1, :]
    picked = jnp.dot(table[...], column_hot(cells, depth), preferred_element_type=jnp.float32)
    row = lax.broadcasted_iota(jnp.int32, (rows, cells.shape[1]), 0) == (cells >> (depth.bit_length() - 1))
    for c in range(comps):
        both = picked[c * rows : (c + 1) * rows] + picked[total + c * rows : total + (c + 1) * rows]
        inlet_now[c : c + 1, :] = jnp.sum(jnp.where(row, both, 0.0), axis=0, keepdims=True)


def outer(comps, depth_z, width, flow, viscosity, below, above, first, left, right, inlet):
    depth = flow.shape[1]
    return pl.pallas_call(
        functools.partial(outer_kernel, comps, depth_z, width),
        out_shape=(
            jax.ShapeDtypeStruct(flow.shape, jnp.float32),
            jax.ShapeDtypeStruct((comps, inlet.shape[1]), jnp.float32),
        ),
        in_specs=[VM] * 8,
        out_specs=(VM, VM),
        scratch_shapes=[
            pltpu.VMEM((comps, depth_z + 4, 8, depth), jnp.float32),
            pltpu.VMEM((depth_z + 2, 8, depth), jnp.float32),
            pltpu.VMEM((comps, depth_z + 2, width + 8, depth), jnp.float32),
            pltpu.VMEM((2 * flow.shape[0], depth), jnp.bfloat16),
        ],
        compiler_params=pltpu.CompilerParams(vmem_limit_bytes=24 * 1024 * 1024),
        cost_estimate=pl.CostEstimate(flops=10**7, bytes_accessed=2**22, transcendentals=0),
        name="outer",
    )(flow, viscosity, below, above, first, left, right, inlet)


def on_device(
    flow_field,
    viscosity,
    port_plane,
    port_match,
    inlet_cell,
    inclusion_state,
    response_rate,
    inclusion_mass,
    anchor_cell,
    live_counts,
    arrival_cell,
):
    comps, depth_z, width, depth = flow_field.shape
    partners, cap = anchor_cell.shape[2:]
    sizes = (comps, depth_z, width)
    flow = flow_field.reshape(-1, depth)
    visc = viscosity.reshape(-1, depth)
    count = lax.axis_size("tile")
    forth = [(i, i + 1) for i in range(count - 1)]
    back = [(i + 1, i) for i in range(count - 1)]
    levels = lax.axis_size("sec")
    up = [(i, (i + 1) % levels) for i in range(levels)]
    down = [((i + 1) % levels, i) for i in range(levels)]
    over = [(i, (i + levels // 2) % levels) for i in range(levels)]

    low_cap, high_cap = caps(*sizes, flow, visc, port_plane)
    below = lax.ppermute(high_cap, "sec", up)
    above = lax.ppermute(low_cap, "sec", down)
    across = lax.ppermute(port_plane, "sec", over)
    counts = live_counts.reshape(-1)
    counts, low_cap, high_cap = lax.optimization_barrier((counts, low_cap, high_cap))
    sampled = sample(comps, counts, flow, anchor_cell.reshape(partners, cap))
    outgoing = slip(
        counts,
        sampled,
        inclusion_state.reshape(comps, partners, cap),
        response_rate.reshape(partners, cap),
        inclusion_mass.reshape(partners, cap),
        port_plane,
        above,
        across,
        below,
    )
    below, above, outgoing = lax.optimization_barrier((below, above, outgoing))
    arrived = lax.all_to_all(outgoing, "tile", split_axis=0, concat_axis=0, tiled=True)
    low_edge, high_edge, bottom, top = edges(*sizes, flow, visc, below, above)
    left = lax.ppermute(high_edge, "tile", forth)
    right = lax.ppermute(low_edge, "tile", back)
    inlet = jnp.pad(jnp.stack([inlet_cell, port_match]), ((0, 0), (0, cap - inlet_cell.shape[0])))
    first = inner(*sizes, flow, visc, bottom, top)
    second, inlet_now = outer(*sizes, flow, visc, bottom, top, first, left, right, inlet)
    flow_next, arrived_state = land(
        port_match, second, inlet_now, inlet, arrival_cell.reshape(partners, cap), arrived
    )
    return flow_next.reshape(flow_field.shape), arrived_state.reshape(inclusion_state.shape)


def solution(mesh):
    return jax.shard_map(
        on_device,
        mesh=mesh,
        in_specs=(
            P(None, "sec", "tile", None),
            P("sec", "tile", None),
            P(None, ("sec", "tile")),
            P(("sec", "tile")),
            P(("sec", "tile")),
            P(None, "sec", "tile", None, None),
            P("sec", "tile", None, None),
            P("sec", "tile", None, None),
            P("sec", "tile", None, None),
            P("sec", "tile", None),
            P("sec", "tile", None, None),
        ),
        out_specs=(P(None, "sec", "tile", None), P(None, "sec", "tile", None, None)),
        check_vma=False,
    )
```

```python
import functools

import jax
import jax.numpy as jnp
from jax import lax
from jax.experimental import pallas as pl
from jax.experimental.pallas import tpu as pltpu
from jax.sharding import PartitionSpec as P

VM = pl.BlockSpec(memory_space=pltpu.VMEM)
SM = pl.BlockSpec(memory_space=pltpu.SMEM)
HB = pl.BlockSpec(memory_space=pltpu.HBM)


def halves(value):
    high = value.astype(jnp.bfloat16)
    low = (value - high.astype(jnp.float32)).astype(jnp.bfloat16)
    return high, low


def column_hot(cells, depth):
    at = lax.broadcasted_iota(jnp.int32, (depth, cells.shape[1]), 0)
    return jnp.where(at == (cells & (depth - 1)), 1.0, 0.0).astype(jnp.bfloat16)


def sample_kernel(GP, counts, flow, anchor, sampled, table, packed):
    partners, cap = anchor.shape
    total, depth = flow.shape
    comps = sampled.shape[1]
    rows = total // comps
    shift = depth.bit_length() - 1
    cap_shift = cap.bit_length() - 1
    lane = lax.broadcasted_iota(jnp.int32, (1, cap), 1)
    packed[...] = jnp.zeros_like(packed)

    def pack(p, base):
        begin = base & (cap - 1)
        spot = base >> cap_shift
        turned = pltpu.roll(anchor[pl.ds(p, 1), :], begin, 1)
        pltpu.store(packed.at[pl.ds(spot, 1), :], turned, mask=lane >= begin)
        pltpu.store(packed.at[pl.ds(spot + 1, 1), :], turned, mask=lane < begin)
        return base + counts[p]

    used = lax.fori_loop(0, partners, pack, 0, unroll=8)
    high, low = halves(flow[...])
    table[0:total] = high
    table[total:] = low

    def group(g, carry):
        first = g * GP
        cells = jnp.concatenate([packed[pl.ds(first + i, 1), :] for i in range(GP)], axis=1)
        hot = column_hot(cells, depth)
        picked = jnp.dot(table[...], hot, preferred_element_type=jnp.float32)
        row = lax.broadcasted_iota(jnp.int32, (rows, cells.shape[1]), 0) == (cells >> shift)
        parts = []
        for c in range(comps):
            both = picked[c * rows : (c + 1) * rows] + picked[total + c * rows : total + (c + 1) * rows]
            parts.append(jnp.sum(jnp.where(row, both, 0.0), axis=0, keepdims=True))
        found = jnp.concatenate(parts, axis=0)
        for i in range(GP):
            sampled[first + i] = found[:, i * cap : (i + 1) * cap]
        return carry

    lax.fori_loop(0, (used + GP * cap - 1) // (GP * cap), group, 0)


def sample(comps, counts, flow, anchor, GP=4):
    partners, cap = anchor.shape
    return pl.pallas_call(
        functools.partial(sample_kernel, GP),
        out_shape=jax.ShapeDtypeStruct((partners + 8, comps, cap), jnp.float32),
        in_specs=[SM, VM, VM],
        out_specs=VM,
        scratch_shapes=[
            pltpu.VMEM((2 * flow.shape[0], flow.shape[1]), jnp.bfloat16),
            pltpu.VMEM((partners + 8, cap), jnp.int32),
        ],
        compiler_params=pltpu.CompilerParams(vmem_limit_bytes=24 * 1024 * 1024),
        cost_estimate=pl.CostEstimate(flops=2 * 8192 * 512 * 1024, bytes_accessed=2**21, transcendentals=0),
        name="sample",
    )(counts, flow, anchor)


chunks = 4


def slip_kernel(counts, sampled, state, rate, mass, ports, above, across, below, far, out, whole, out_sems):
    comps, partners, cap = state.shape
    per = ports.shape[1]
    cap_shift = cap.bit_length() - 1
    last = above.shape[0] - 8
    lane = lax.broadcasted_iota(jnp.int32, (1, cap), 1)
    whole[:, 0:per] = ports[...]
    whole[:, per : 2 * per] = above[last : last + comps, 0:per]
    whole[:, 2 * per : 3 * per] = across[...]
    whole[:, 3 * per :] = below[last : last + comps, 0:per]

    def finish(p, base):
        n = counts[p]
        begin = base & (cap - 1)
        spot = base >> cap_shift
        both = jnp.where(lane >= begin, sampled[spot], sampled[spot + 1])
        value = pltpu.roll(both, (cap - begin) & (cap - 1), 1)
        own = jnp.concatenate([state[c, pl.ds(p, 1), :] for c in range(comps)], axis=0)
        r = rate[pl.ds(p, 1), :]
        drop = r * (own - value)
        live = lane < n
        out[3 * p] = jnp.where(live, own - drop, 0.0)
        out[3 * p + 1] = jnp.where(live, mass[pl.ds(p, 1), :] * drop, 0.0)
        out[3 * p + 2] = whole[...]
        return base + n

    block = partners // chunks
    base = 0
    copies = []
    for i in range(chunks):
        base = lax.fori_loop(i * block, (i + 1) * block, finish, base, unroll=8)
        part = pl.ds(3 * i * block, 3 * block)
        copies.append(pltpu.make_async_copy(out.at[part], far.at[part], out_sems.at[i]))
        copies[i].start()
    for copy in copies:
        copy.wait()


def slip(counts, sampled, state, rate, mass, ports, above, across, below):
    comps, partners, cap = state.shape
    return pl.pallas_call(
        slip_kernel,
        out_shape=jax.ShapeDtypeStruct((partners * 3, comps, cap), jnp.float32),
        in_specs=[SM] + [VM] * 8,
        out_specs=HB,
        scratch_shapes=[
            pltpu.VMEM((partners * 3, comps, cap), jnp.float32),
            pltpu.VMEM((comps, cap), jnp.float32),
            pltpu.SemaphoreType.DMA((chunks,)),
        ],
        compiler_params=pltpu.CompilerParams(vmem_limit_bytes=24 * 1024 * 1024),
        cost_estimate=pl.CostEstimate(flops=2 * 10**6, bytes_accessed=2**20, transcendentals=0),
        name="slip",
    )(counts, sampled, state, rate, mass, ports, above, across, below)


def land_kernel(GP, match, second, inlet_now, inlet, arrival, arrived, flow_out, state_out, last_ref, last, packed, sem):
    comps, partners, cap = state_out.shape
    total, depth = second.shape
    rows = total // comps
    shift = depth.bit_length() - 1
    cap_shift = cap.bit_length() - 1
    entries = match.shape[0]
    per = entries
    nt = (((1,), (1,)), ((), ()))
    slot = lax.broadcasted_iota(jnp.int32, (1, cap), 1)

    def ends(p, carry):
        moved = arrived[3 * p]
        gift = arrived[3 * p + 1]
        for c in range(comps):
            state_out[c, pl.ds(p, 1), :] = moved[c : c + 1]
        biggest = jnp.max(jnp.abs(gift), axis=0, keepdims=True)
        last_ref[pl.ds(p, 1), :] = jnp.where(biggest > 0.0, slot + 1, 0)
        return carry

    lax.fori_loop(0, partners, ends, 0, unroll=8)
    last_ref[partners:, :] = jnp.zeros_like(last_ref[partners:, :])
    top = jnp.max(last_ref[...].T, axis=0, keepdims=True)
    last_ref[0:1, :] = top
    fetch = pltpu.make_async_copy(last_ref.at[0:1, :], last, sem)
    fetch.start()

    def spread(cells, values):
        row = lax.broadcasted_iota(jnp.int32, (rows, cells.shape[1]), 0) == (cells >> shift)
        high, low = halves(values)
        parts = []
        for part in (high.astype(jnp.float32), low.astype(jnp.float32)):
            for c in range(comps):
                parts.append(jnp.where(row, part[c : c + 1], 0.0).astype(jnp.bfloat16))
        return jnp.concatenate(parts, axis=0)

    def product(cells, values):
        both = lax.dot_general(spread(cells, values), column_hot(cells, depth), nt, preferred_element_type=jnp.float32)
        return both[:total] + both[total:]

    section = lax.axis_index("sec")
    sections = cap // per
    target = jnp.zeros((comps, cap), jnp.float32)
    for k in range(entries):
        port = match[k]
        device = port // entries
        place = (device // partners + sections - section) % sections * per + port % entries
        turned = pltpu.roll(arrived[3 * (device % partners) + 2], (k + cap - place) % cap, 1)
        target = jnp.where(slot == k, turned, target)
    change = jnp.where(slot < entries, 0.5 * (target - inlet_now[...]), 0.0)
    flow_out[...] = second[...] + product(inlet[0:1, :], change)
    packed[...] = jnp.zeros_like(packed)
    fetch.wait()

    def pack(p, base):
        begin = base & (cap - 1)
        spot = base >> cap_shift
        cells = arrival[pl.ds(p, 1), :].astype(jnp.float32)
        both = jnp.concatenate([arrived[3 * p + 1], jnp.broadcast_to(cells, (8 - comps, cap))], axis=0)
        turned = pltpu.roll(both, begin, 1)
        wide = lax.broadcasted_iota(jnp.int32, (8, cap), 1)
        pltpu.store(packed.at[spot], turned, mask=wide >= begin)
        pltpu.store(packed.at[spot + 1], turned, mask=wide < begin)
        return base + last[0, p]

    used = lax.fori_loop(0, partners, pack, 0, unroll=8)

    def group(g, carry):
        first = g * GP
        both = jnp.concatenate([packed[first + i] for i in range(GP)], axis=1)
        flow_out[...] += product(both[comps : comps + 1].astype(jnp.int32), both[:comps])
        return carry

    lax.fori_loop(0, (used + GP * cap - 1) // (GP * cap), group, 0)


def land(match, second, inlet_now, inlet, arrival, arrived, GP=8):
    partners, cap = arrival.shape
    comps = arrived.shape[1]
    return pl.pallas_call(
        functools.partial(land_kernel, GP),
        out_shape=(
            jax.ShapeDtypeStruct(second.shape, jnp.float32),
            jax.ShapeDtypeStruct((comps, partners, cap), jnp.float32),
        ),
        in_specs=[SM] + [VM] * 5,
        out_specs=(VM, VM),
        scratch_shapes=[
            pltpu.VMEM((cap, cap), jnp.int32),
            pltpu.SMEM((1, cap), jnp.int32),
            pltpu.VMEM((partners + 8, 8, cap), jnp.float32),
            pltpu.SemaphoreType.DMA,
        ],
        compiler_params=pltpu.CompilerParams(vmem_limit_bytes=24 * 1024 * 1024),
        cost_estimate=pl.CostEstimate(flops=2 * 8192 * 512 * 1024, bytes_accessed=2**21, transcendentals=0),
        name="land",
    )(match, second, inlet_now, inlet, arrival, arrived)


def tendency(plane, upper, lower, viscosity, keep):
    place = lax.broadcasted_iota(jnp.int32, (1, viscosity.shape[1]), 1)
    depth = viscosity.shape[1]
    centers, laps, dz, dx, dy = [], [], [], [], []
    for c in range(len(plane)):
        whole = plane[c]
        center = whole[:keep]
        up_x = pltpu.roll(whole, whole.shape[0] - 1, 0)[:keep]
        low_x = pltpu.roll(whole, 1, 0)[:keep]
        up_y = jnp.where(place == depth - 1, 0.0, pltpu.roll(center, depth - 1, 1))
        low_y = jnp.where(place == 0, 0.0, pltpu.roll(center, 1, 1))
        centers.append(center)
        laps.append((upper[c] + lower[c]) + (up_x + low_x) + (up_y + low_y) - 6.0 * center)
        dz.append(upper[c] - lower[c])
        dx.append(up_x - low_x)
        dy.append(up_y - low_y)
    strain = sum(d[c] * d[c] for c in range(3) for d in (dz, dx, dy)) * 0.25
    eddy = viscosity * (1.0 + strain / (1.0 + strain))
    out = []
    for c in range(len(plane)):
        carried = centers[0] * dz[c] + centers[1] * dx[c] + centers[2] * dy[c]
        out.append(0.5 * (eddy * laps[c]) - 0.25 * carried)
    return centers, out


def cap_kernel(comps, depth_z, width, flow, viscosity, ports, low_out, high_out, sems):
    copies = []

    def copy(source, target):
        copies.append(pltpu.make_async_copy(source, target, sems.at[len(copies)]))
        copies[-1].start()

    two = 2 * width
    last = (depth_z - 1) * width
    for c in range(comps):
        base = c * depth_z * width
        copy(flow.at[base : base + two, :], low_out.at[c * two : (c + 1) * two, :])
        copy(flow.at[base + last - width : base + last + width, :], high_out.at[c * two : (c + 1) * two, :])
    base = comps * two
    copy(viscosity.at[0:width, :], low_out.at[base : base + width, :])
    copy(viscosity.at[last : last + width, :], high_out.at[base : base + width, :])
    for out in (low_out, high_out):
        out[base + width :, :] = jnp.zeros((8, out.shape[1]), jnp.float32)
        out[base + width : base + width + comps, 0 : ports.shape[1]] = ports[...]
    for started in copies:
        started.wait()


def caps(comps, depth_z, width, flow, viscosity, ports):
    shape = jax.ShapeDtypeStruct((2 * comps * width + width + 8, flow.shape[1]), jnp.float32)
    return pl.pallas_call(
        functools.partial(cap_kernel, comps, depth_z, width),
        out_shape=(shape, shape),
        in_specs=[HB, HB, VM],
        out_specs=(VM, VM),
        scratch_shapes=[pltpu.SemaphoreType.DMA((2 * comps + 2,))],
        compiler_params=pltpu.CompilerParams(vmem_limit_bytes=60 * 1024 * 1024),
        name="caps",
    )(flow, viscosity, ports)


def edge_kernel(comps, depth_z, width, flow, viscosity, below, above, low_out, high_out, bottom, top):
    section = lax.axis_index("sec")
    bottom[...] = jnp.where(section > 0, below[0 : bottom.shape[0], :], 0.0)
    top[...] = jnp.where(section < lax.axis_size("sec") - 1, above[0 : top.shape[0], :], 0.0)
    two = 2 * width
    for k in range(comps * depth_z):
        low_out[2 * k : 2 * k + 2, :] = flow[k * width : k * width + 2, :]
        high_out[2 * k : 2 * k + 2, :] = flow[(k + 1) * width - 2 : (k + 1) * width, :]
    base = 2 * comps * depth_z
    for c in range(comps):
        low_out[base + 2 * c : base + 2 * c + 1, :] = bottom[c * two + width : c * two + width + 1, :]
        low_out[base + 2 * c + 1 : base + 2 * c + 2, :] = top[c * two : c * two + 1, :]
        high_out[base + 2 * c : base + 2 * c + 1, :] = bottom[(c + 1) * two - 1 : (c + 1) * two, :]
        high_out[base + 2 * c + 1 : base + 2 * c + 2, :] = top[c * two + width - 1 : c * two + width, :]
    base += 2 * comps
    for z in range(depth_z):
        low_out[base + z : base + z + 1, :] = viscosity[z * width : z * width + 1, :]
        high_out[base + z : base + z + 1, :] = viscosity[(z + 1) * width - 1 : (z + 1) * width, :]


def edges(comps, depth_z, width, flow, viscosity, below, above):
    depth = flow.shape[1]
    shape = jax.ShapeDtypeStruct((2 * comps * (depth_z + 1) + depth_z, depth), jnp.float32)
    halo = jax.ShapeDtypeStruct(((2 * comps + 1) * width, depth), jnp.float32)
    return pl.pallas_call(
        functools.partial(edge_kernel, comps, depth_z, width),
        out_shape=(shape, shape, halo, halo),
        in_specs=[VM] * 4,
        out_specs=(VM,) * 4,
        compiler_params=pltpu.CompilerParams(vmem_limit_bytes=24 * 1024 * 1024),
        name="edges",
    )(flow, viscosity, below, above)


def inner_kernel(comps, depth_z, width, flow, viscosity, below, above, first):
    two = 2 * width

    def own(z):
        if z < 0:
            return [below[c * two + (2 + z) * width : c * two + (3 + z) * width, :] for c in range(comps)]
        if z >= depth_z:
            return [above[c * two + (z - depth_z) * width : c * two + (z - depth_z + 1) * width, :] for c in range(comps)]
        return [flow[(c * depth_z + z) * width : (c * depth_z + z + 1) * width, :] for c in range(comps)]

    for z in range(-1, depth_z + 1):
        if z < 0:
            visc = below[comps * two :, :]
        elif z == depth_z:
            visc = above[comps * two :, :]
        else:
            visc = viscosity[z * width : (z + 1) * width, :]
        centers, change = tendency(own(z), own(z + 1), own(z - 1), visc, width)
        for c in range(comps):
            first[c, z + 1, 0:width, :] = centers[c] + change[c]


def inner(comps, depth_z, width, flow, viscosity, below, above):
    depth = flow.shape[1]
    return pl.pallas_call(
        functools.partial(inner_kernel, comps, depth_z, width),
        out_shape=jax.ShapeDtypeStruct((comps, depth_z + 2, width, depth), jnp.float32),
        in_specs=[VM] * 4,
        out_specs=VM,
        compiler_params=pltpu.CompilerParams(vmem_limit_bytes=24 * 1024 * 1024),
        cost_estimate=pl.CostEstimate(flops=10**7, bytes_accessed=2**22, transcendentals=0),
        name="inner",
    )(flow, viscosity, below, above)


def outer_kernel(comps, depth_z, width, flow, viscosity, below, above, first, left, right, inlet, second_out, inlet_now, strip, visc, started, table):
    depth = flow.shape[1]
    two = 2 * width
    rows = depth_z * width
    total = comps * rows
    base = 2 * comps * depth_z
    strip[...] = jnp.zeros_like(strip)
    visc[...] = jnp.zeros_like(visc)
    for c in range(comps):
        for z in range(-2, depth_z + 2):
            if z < 0:
                ref, spot = below, c * two + (2 + z) * width
            elif z >= depth_z:
                ref, spot = above, c * two + (z - depth_z) * width
            else:
                ref, spot = flow, (c * depth_z + z) * width
            strip[c, z + 2, 2:4, :] = ref[spot : spot + 2, :]
            strip[c, z + 2, 4:6, :] = ref[spot + width - 2 : spot + width, :]
            if 0 <= z < depth_z:
                k = 2 * (c * depth_z + z)
                strip[c, z + 2, 0:2, :] = left[k : k + 2, :]
                strip[c, z + 2, 6:8, :] = right[k : k + 2, :]
            elif z in (-1, depth_z):
                k = base + 2 * c + (z == depth_z)
                strip[c, z + 2, 1:2, :] = left[k : k + 1, :]
                strip[c, z + 2, 6:7, :] = right[k : k + 1, :]
    side = base + 2 * comps
    for z in range(-1, depth_z + 1):
        if z < 0:
            ref, spot = below, comps * two
        elif z == depth_z:
            ref, spot = above, comps * two
        else:
            ref, spot = viscosity, z * width
            visc[z + 1, 1:2, :] = left[side + z : side + z + 1, :]
            visc[z + 1, 6:7, :] = right[side + z : side + z + 1, :]
        visc[z + 1, 2:4, :] = ref[spot : spot + 2, :]
        visc[z + 1, 4:6, :] = ref[spot + width - 2 : spot + width, :]

    place = lax.broadcasted_iota(jnp.int32, (width, 1), 0)
    blank = jnp.zeros((6, depth), jnp.float32)

    def one(z, carry):
        plane, upper, lower = ([strip[c, z + 1 + d] for c in range(comps)] for d in (0, 1, -1))
        centers, change = tendency(plane, upper, lower, visc[z], 8)
        for c in range(comps):
            edge = centers[c] + change[c]
            mine = first[c, z]
            mine = jnp.where(place == 0, edge[2:3], mine)
            mine = jnp.where(place == width - 1, edge[5:6], mine)
            started[c, z, 0:width, :] = mine
            started[c, z, width : width + 8, :] = jnp.concatenate([edge[6:7], blank, edge[1:2]], axis=0)
        return carry

    lax.fori_loop(0, depth_z + 2, one, 0)

    def second(z, carry):
        plane = [started[c, z + 1] for c in range(comps)]
        upper, lower = ([started[c, z + 1 + d, 0:width, :] for c in range(comps)] for d in (1, -1))
        at = pl.multiple_of(z * width, width)
        centers, change = tendency(plane, upper, lower, viscosity[pl.ds(at, width), :], width)
        for c in range(comps):
            spot = pl.multiple_of((c * depth_z + z) * width, width)
            value = 0.5 * flow[pl.ds(spot, width), :] + 0.5 * (centers[c] + change[c])
            second_out[pl.ds(spot, width), :] = value
            high, low = halves(value)
            table[pl.ds(spot, width), :] = high
            table[pl.ds(total + spot, width), :] = low
        return carry

    lax.fori_loop(0, depth_z, second, 0)

    cells = inlet[0:1, :]
    picked = jnp.dot(table[...], column_hot(cells, depth), preferred_element_type=jnp.float32)
    row = lax.broadcasted_iota(jnp.int32, (rows, cells.shape[1]), 0) == (cells >> (depth.bit_length() - 1))
    for c in range(comps):
        both = picked[c * rows : (c + 1) * rows] + picked[total + c * rows : total + (c + 1) * rows]
        inlet_now[c : c + 1, :] = jnp.sum(jnp.where(row, both, 0.0), axis=0, keepdims=True)


def outer(comps, depth_z, width, flow, viscosity, below, above, first, left, right, inlet):
    depth = flow.shape[1]
    return pl.pallas_call(
        functools.partial(outer_kernel, comps, depth_z, width),
        out_shape=(
            jax.ShapeDtypeStruct(flow.shape, jnp.float32),
            jax.ShapeDtypeStruct((comps, inlet.shape[1]), jnp.float32),
        ),
        in_specs=[VM] * 8,
        out_specs=(VM, VM),
        scratch_shapes=[
            pltpu.VMEM((comps, depth_z + 4, 8, depth), jnp.float32),
            pltpu.VMEM((depth_z + 2, 8, depth), jnp.float32),
            pltpu.VMEM((comps, depth_z + 2, width + 8, depth), jnp.float32),
            pltpu.VMEM((2 * flow.shape[0], depth), jnp.bfloat16),
        ],
        compiler_params=pltpu.CompilerParams(vmem_limit_bytes=24 * 1024 * 1024),
        cost_estimate=pl.CostEstimate(flops=10**7, bytes_accessed=2**22, transcendentals=0),
        name="outer",
    )(flow, viscosity, below, above, first, left, right, inlet)


def on_device(
    flow_field,
    viscosity,
    port_plane,
    port_match,
    inlet_cell,
    inclusion_state,
    response_rate,
    inclusion_mass,
    anchor_cell,
    live_counts,
    arrival_cell,
):
    comps, depth_z, width, depth = flow_field.shape
    partners, cap = anchor_cell.shape[2:]
    sizes = (comps, depth_z, width)
    flow = flow_field.reshape(-1, depth)
    visc = viscosity.reshape(-1, depth)
    count = lax.axis_size("tile")
    forth = [(i, i + 1) for i in range(count - 1)]
    back = [(i + 1, i) for i in range(count - 1)]
    levels = lax.axis_size("sec")
    up = [(i, (i + 1) % levels) for i in range(levels)]
    down = [((i + 1) % levels, i) for i in range(levels)]
    over = [(i, (i + levels // 2) % levels) for i in range(levels)]

    low_cap, high_cap = caps(*sizes, flow, visc, port_plane)
    below = lax.ppermute(high_cap, "sec", up)
    above = lax.ppermute(low_cap, "sec", down)
    across = lax.ppermute(port_plane, "sec", over)
    counts = live_counts.reshape(-1)
    counts, low_cap, high_cap = lax.optimization_barrier((counts, low_cap, high_cap))
    sampled = sample(comps, counts, flow, anchor_cell.reshape(partners, cap))
    outgoing = slip(
        counts,
        sampled,
        inclusion_state.reshape(comps, partners, cap),
        response_rate.reshape(partners, cap),
        inclusion_mass.reshape(partners, cap),
        port_plane,
        above,
        across,
        below,
    )
    below, above, outgoing = lax.optimization_barrier((below, above, outgoing))
    arrived = lax.all_to_all(outgoing, "tile", split_axis=0, concat_axis=0, tiled=True)
    low_edge, high_edge, bottom, top = edges(*sizes, flow, visc, below, above)
    left = lax.ppermute(high_edge, "tile", forth)
    right = lax.ppermute(low_edge, "tile", back)
    inlet = jnp.pad(jnp.stack([inlet_cell, port_match]), ((0, 0), (0, cap - inlet_cell.shape[0])))
    first = inner(*sizes, flow, visc, bottom, top)
    second, inlet_now = outer(*sizes, flow, visc, bottom, top, first, left, right, inlet)
    flow_next, arrived_state = land(
        port_match, second, inlet_now, inlet, arrival_cell.reshape(partners, cap), arrived
    )
    return flow_next.reshape(flow_field.shape), arrived_state.reshape(inclusion_state.shape)


def solution(mesh):
    return jax.shard_map(
        on_device,
        mesh=mesh,
        in_specs=(
            P(None, "sec", "tile", None),
            P("sec", "tile", None),
            P(None, ("sec", "tile")),
            P(("sec", "tile")),
            P(("sec", "tile")),
            P(None, "sec", "tile", None, None),
            P("sec", "tile", None, None),
            P("sec", "tile", None, None),
            P("sec", "tile", None, None),
            P("sec", "tile", None),
            P("sec", "tile", None, None),
        ),
        out_specs=(P(None, "sec", "tile", None), P(None, "sec", "tile", None, None)),
        check_vma=False,
    )
```

```python
import functools

import jax
import jax.numpy as jnp
from jax import lax
from jax.experimental import pallas as pl
from jax.experimental.pallas import tpu as pltpu
from jax.sharding import PartitionSpec as P

VM = pl.BlockSpec(memory_space=pltpu.VMEM)
SM = pl.BlockSpec(memory_space=pltpu.SMEM)
HB = pl.BlockSpec(memory_space=pltpu.HBM)


def halves(value):
    high = value.astype(jnp.bfloat16)
    low = (value - high.astype(jnp.float32)).astype(jnp.bfloat16)
    return high, low


def column_hot(cells, depth):
    at = lax.broadcasted_iota(jnp.int32, (depth, cells.shape[1]), 0)
    return jnp.where(at == (cells & (depth - 1)), 1.0, 0.0).astype(jnp.bfloat16)


def sample_kernel(GP, counts, flow, anchor, sampled, table, packed):
    partners, cap = anchor.shape
    total, depth = flow.shape
    comps = sampled.shape[1]
    rows = total // comps
    shift = depth.bit_length() - 1
    cap_shift = cap.bit_length() - 1
    lane = lax.broadcasted_iota(jnp.int32, (1, cap), 1)
    packed[...] = jnp.zeros_like(packed)

    def pack(p, base):
        begin = base & (cap - 1)
        spot = base >> cap_shift
        turned = pltpu.roll(anchor[pl.ds(p, 1), :], begin, 1)
        pltpu.store(packed.at[pl.ds(spot, 1), :], turned, mask=lane >= begin)
        pltpu.store(packed.at[pl.ds(spot + 1, 1), :], turned, mask=lane < begin)
        return base + counts[p]

    used = lax.fori_loop(0, partners, pack, 0, unroll=8)
    high, low = halves(flow[...])
    table[0:total] = high
    table[total:] = low

    def group(g, carry):
        first = g * GP
        cells = jnp.concatenate([packed[pl.ds(first + i, 1), :] for i in range(GP)], axis=1)
        hot = column_hot(cells, depth)
        picked = jnp.dot(table[...], hot, preferred_element_type=jnp.float32)
        row = lax.broadcasted_iota(jnp.int32, (rows, cells.shape[1]), 0) == (cells >> shift)
        parts = []
        for c in range(comps):
            both = picked[c * rows : (c + 1) * rows] + picked[total + c * rows : total + (c + 1) * rows]
            parts.append(jnp.sum(jnp.where(row, both, 0.0), axis=0, keepdims=True))
        found = jnp.concatenate(parts, axis=0)
        for i in range(GP):
            sampled[first + i] = found[:, i * cap : (i + 1) * cap]
        return carry

    lax.fori_loop(0, (used + GP * cap - 1) // (GP * cap), group, 0)


def sample(comps, counts, flow, anchor, GP=4):
    partners, cap = anchor.shape
    return pl.pallas_call(
        functools.partial(sample_kernel, GP),
        out_shape=jax.ShapeDtypeStruct((partners + 8, comps, cap), jnp.float32),
        in_specs=[SM, VM, VM],
        out_specs=VM,
        scratch_shapes=[
            pltpu.VMEM((2 * flow.shape[0], flow.shape[1]), jnp.bfloat16),
            pltpu.VMEM((partners + 8, cap), jnp.int32),
        ],
        compiler_params=pltpu.CompilerParams(vmem_limit_bytes=24 * 1024 * 1024),
        cost_estimate=pl.CostEstimate(flops=2 * 8192 * 512 * 1024, bytes_accessed=2**21, transcendentals=0),
        name="sample",
    )(counts, flow, anchor)


chunks = 4


def slip_kernel(counts, sampled, state, rate, mass, ports, above, across, below, far, out, whole, out_sems):
    comps, partners, cap = state.shape
    per = ports.shape[1]
    cap_shift = cap.bit_length() - 1
    last = above.shape[0] - 8
    lane = lax.broadcasted_iota(jnp.int32, (1, cap), 1)
    whole[:, 0:per] = ports[...]
    whole[:, per : 2 * per] = above[last : last + comps, 0:per]
    whole[:, 2 * per : 3 * per] = across[...]
    whole[:, 3 * per :] = below[last : last + comps, 0:per]

    def finish(p, base):
        n = counts[p]
        begin = base & (cap - 1)
        spot = base >> cap_shift
        both = jnp.where(lane >= begin, sampled[spot], sampled[spot + 1])
        value = pltpu.roll(both, (cap - begin) & (cap - 1), 1)
        own = jnp.concatenate([state[c, pl.ds(p, 1), :] for c in range(comps)], axis=0)
        r = rate[pl.ds(p, 1), :]
        drop = r * (own - value)
        live = lane < n
        out[3 * p] = jnp.where(live, own - drop, 0.0)
        out[3 * p + 1] = jnp.where(live, mass[pl.ds(p, 1), :] * drop, 0.0)
        out[3 * p + 2] = whole[...]
        return base + n

    block = partners // chunks
    base = 0
    copies = []
    for i in range(chunks):
        base = lax.fori_loop(i * block, (i + 1) * block, finish, base, unroll=8)
        part = pl.ds(3 * i * block, 3 * block)
        copies.append(pltpu.make_async_copy(out.at[part], far.at[part], out_sems.at[i]))
        copies[i].start()
    for copy in copies:
        copy.wait()


def slip(counts, sampled, state, rate, mass, ports, above, across, below):
    comps, partners, cap = state.shape
    return pl.pallas_call(
        slip_kernel,
        out_shape=jax.ShapeDtypeStruct((partners * 3, comps, cap), jnp.float32),
        in_specs=[SM] + [VM] * 8,
        out_specs=HB,
        scratch_shapes=[
            pltpu.VMEM((partners * 3, comps, cap), jnp.float32),
            pltpu.VMEM((comps, cap), jnp.float32),
            pltpu.SemaphoreType.DMA((chunks,)),
        ],
        compiler_params=pltpu.CompilerParams(vmem_limit_bytes=24 * 1024 * 1024),
        cost_estimate=pl.CostEstimate(flops=2 * 10**6, bytes_accessed=2**20, transcendentals=0),
        name="slip",
    )(counts, sampled, state, rate, mass, ports, above, across, below)


def land_kernel(GP, match, second, inlet_now, inlet, arrival, arrived, flow_out, state_out, last_ref, last, packed, sem):
    comps, partners, cap = state_out.shape
    total, depth = second.shape
    rows = total // comps
    shift = depth.bit_length() - 1
    cap_shift = cap.bit_length() - 1
    entries = match.shape[0]
    per = entries
    nt = (((1,), (1,)), ((), ()))
    slot = lax.broadcasted_iota(jnp.int32, (1, cap), 1)

    def ends(p, carry):
        moved = arrived[3 * p]
        gift = arrived[3 * p + 1]
        for c in range(comps):
            state_out[c, pl.ds(p, 1), :] = moved[c : c + 1]
        biggest = jnp.max(jnp.abs(gift), axis=0, keepdims=True)
        last_ref[pl.ds(p, 1), :] = jnp.where(biggest > 0.0, slot + 1, 0)
        return carry

    lax.fori_loop(0, partners, ends, 0, unroll=8)
    last_ref[partners:, :] = jnp.zeros_like(last_ref[partners:, :])
    top = jnp.max(last_ref[...].T, axis=0, keepdims=True)
    last_ref[0:1, :] = top
    fetch = pltpu.make_async_copy(last_ref.at[0:1, :], last, sem)
    fetch.start()

    def spread(cells, values):
        row = lax.broadcasted_iota(jnp.int32, (rows, cells.shape[1]), 0) == (cells >> shift)
        high, low = halves(values)
        parts = []
        for part in (high.astype(jnp.float32), low.astype(jnp.float32)):
            for c in range(comps):
                parts.append(jnp.where(row, part[c : c + 1], 0.0).astype(jnp.bfloat16))
        return jnp.concatenate(parts, axis=0)

    def product(cells, values):
        both = lax.dot_general(spread(cells, values), column_hot(cells, depth), nt, preferred_element_type=jnp.float32)
        return both[:total] + both[total:]

    section = lax.axis_index("sec")
    sections = cap // per
    target = jnp.zeros((comps, cap), jnp.float32)
    for k in range(entries):
        port = match[k]
        device = port // entries
        place = (device // partners + sections - section) % sections * per + port % entries
        turned = pltpu.roll(arrived[3 * (device % partners) + 2], (k + cap - place) % cap, 1)
        target = jnp.where(slot == k, turned, target)
    change = jnp.where(slot < entries, 0.5 * (target - inlet_now[...]), 0.0)
    flow_out[...] = second[...] + product(inlet[0:1, :], change)
    packed[...] = jnp.zeros_like(packed)
    fetch.wait()

    def pack(p, base):
        begin = base & (cap - 1)
        spot = base >> cap_shift
        cells = arrival[pl.ds(p, 1), :].astype(jnp.float32)
        both = jnp.concatenate([arrived[3 * p + 1], jnp.broadcast_to(cells, (8 - comps, cap))], axis=0)
        turned = pltpu.roll(both, begin, 1)
        wide = lax.broadcasted_iota(jnp.int32, (8, cap), 1)
        pltpu.store(packed.at[spot], turned, mask=wide >= begin)
        pltpu.store(packed.at[spot + 1], turned, mask=wide < begin)
        return base + last[0, p]

    used = lax.fori_loop(0, partners, pack, 0, unroll=8)

    def group(g, carry):
        first = g * GP
        both = jnp.concatenate([packed[first + i] for i in range(GP)], axis=1)
        flow_out[...] += product(both[comps : comps + 1].astype(jnp.int32), both[:comps])
        return carry

    lax.fori_loop(0, (used + GP * cap - 1) // (GP * cap), group, 0)


def land(match, second, inlet_now, inlet, arrival, arrived, GP=8):
    partners, cap = arrival.shape
    comps = arrived.shape[1]
    return pl.pallas_call(
        functools.partial(land_kernel, GP),
        out_shape=(
            jax.ShapeDtypeStruct(second.shape, jnp.float32),
            jax.ShapeDtypeStruct((comps, partners, cap), jnp.float32),
        ),
        in_specs=[SM] + [VM] * 5,
        out_specs=(VM, VM),
        scratch_shapes=[
            pltpu.VMEM((cap, cap), jnp.int32),
            pltpu.SMEM((1, cap), jnp.int32),
            pltpu.VMEM((partners + 8, 8, cap), jnp.float32),
            pltpu.SemaphoreType.DMA,
        ],
        compiler_params=pltpu.CompilerParams(vmem_limit_bytes=24 * 1024 * 1024),
        cost_estimate=pl.CostEstimate(flops=2 * 8192 * 512 * 1024, bytes_accessed=2**21, transcendentals=0),
        name="land",
    )(match, second, inlet_now, inlet, arrival, arrived)


def tendency(plane, upper, lower, viscosity, keep):
    place = lax.broadcasted_iota(jnp.int32, (1, viscosity.shape[1]), 1)
    depth = viscosity.shape[1]
    centers, laps, dz, dx, dy = [], [], [], [], []
    for c in range(len(plane)):
        whole = plane[c]
        center = whole[:keep]
        up_x = pltpu.roll(whole, whole.shape[0] - 1, 0)[:keep]
        low_x = pltpu.roll(whole, 1, 0)[:keep]
        up_y = jnp.where(place == depth - 1, 0.0, pltpu.roll(center, depth - 1, 1))
        low_y = jnp.where(place == 0, 0.0, pltpu.roll(center, 1, 1))
        centers.append(center)
        laps.append((upper[c] + lower[c]) + (up_x + low_x) + (up_y + low_y) - 6.0 * center)
        dz.append(upper[c] - lower[c])
        dx.append(up_x - low_x)
        dy.append(up_y - low_y)
    strain = sum(d[c] * d[c] for c in range(3) for d in (dz, dx, dy)) * 0.25
    eddy = viscosity * (1.0 + strain / (1.0 + strain))
    out = []
    for c in range(len(plane)):
        carried = centers[0] * dz[c] + centers[1] * dx[c] + centers[2] * dy[c]
        out.append(0.5 * (eddy * laps[c]) - 0.25 * carried)
    return centers, out


def rim_kernel(comps, depth_z, width, flow, viscosity, ports, low_edge, high_edge, low_cap, high_cap):
    for k in range(comps * depth_z):
        low_edge[2 * k : 2 * k + 2, :] = flow[k * width : k * width + 2, :]
        high_edge[2 * k : 2 * k + 2, :] = flow[(k + 1) * width - 2 : (k + 1) * width, :]
    base = 2 * comps * depth_z
    for z in range(depth_z):
        low_edge[base + z : base + z + 1, :] = viscosity[z * width : z * width + 1, :]
        high_edge[base + z : base + z + 1, :] = viscosity[(z + 1) * width - 1 : (z + 1) * width, :]
    two = 2 * width
    last = depth_z * width
    for c in range(comps):
        low_cap[c * two : (c + 1) * two, :] = flow[c * last : c * last + two, :]
        high_cap[c * two : (c + 1) * two, :] = flow[(c + 1) * last - two : (c + 1) * last, :]
    base = comps * two
    low_cap[base : base + width, :] = viscosity[0:width, :]
    high_cap[base : base + width, :] = viscosity[last - width : last, :]
    for out in (low_cap, high_cap):
        out[base + width :, :] = jnp.zeros((8, out.shape[1]), jnp.float32)
        out[base + width : base + width + comps, 0 : ports.shape[1]] = ports[...]


def rims(comps, depth_z, width, flow, viscosity, ports):
    depth = flow.shape[1]
    edge = jax.ShapeDtypeStruct(((2 * comps + 1) * depth_z, depth), jnp.float32)
    cap = jax.ShapeDtypeStruct((2 * comps * width + width + 8, depth), jnp.float32)
    return pl.pallas_call(
        functools.partial(rim_kernel, comps, depth_z, width),
        out_shape=(edge, edge, cap, cap),
        in_specs=[VM] * 3,
        out_specs=(VM,) * 4,
        compiler_params=pltpu.CompilerParams(vmem_limit_bytes=60 * 1024 * 1024),
        name="rims",
    )(flow, viscosity, ports)


def corner_kernel(comps, depth_z, below, above, left, right, low_out, high_out, bottom, top):
    section = lax.axis_index("sec")
    bottom[...] = jnp.where(section > 0, below[0 : bottom.shape[0], :], 0.0)
    top[...] = jnp.where(section < lax.axis_size("sec") - 1, above[0 : top.shape[0], :], 0.0)
    for c in range(comps):
        for out, z in ((low_out, 0), (high_out, depth_z - 1)):
            k = 2 * (c * depth_z + z)
            out[c : c + 1, :] = left[k + 1 : k + 2, :]
            out[comps + c : comps + c + 1, :] = right[k : k + 1, :]


def corners(comps, depth_z, width, below, above, left, right):
    depth = below.shape[1]
    shape = jax.ShapeDtypeStruct((2 * comps, depth), jnp.float32)
    halo = jax.ShapeDtypeStruct(((2 * comps + 1) * width, depth), jnp.float32)
    return pl.pallas_call(
        functools.partial(corner_kernel, comps, depth_z),
        out_shape=(shape, shape, halo, halo),
        in_specs=[VM] * 4,
        out_specs=(VM,) * 4,
        compiler_params=pltpu.CompilerParams(vmem_limit_bytes=24 * 1024 * 1024),
        name="corners",
    )(below, above, left, right)


def inner_kernel(comps, depth_z, width, flow, viscosity, below, above, first):
    two = 2 * width

    def own(z):
        if z < 0:
            return [below[c * two + (2 + z) * width : c * two + (3 + z) * width, :] for c in range(comps)]
        if z >= depth_z:
            return [above[c * two + (z - depth_z) * width : c * two + (z - depth_z + 1) * width, :] for c in range(comps)]
        return [flow[(c * depth_z + z) * width : (c * depth_z + z + 1) * width, :] for c in range(comps)]

    for z in range(-1, depth_z + 1):
        if z < 0:
            visc = below[comps * two :, :]
        elif z == depth_z:
            visc = above[comps * two :, :]
        else:
            visc = viscosity[z * width : (z + 1) * width, :]
        centers, change = tendency(own(z), own(z + 1), own(z - 1), visc, width)
        for c in range(comps):
            first[c, z + 1, 0:width, :] = centers[c] + change[c]


def inner(comps, depth_z, width, flow, viscosity, below, above):
    depth = flow.shape[1]
    return pl.pallas_call(
        functools.partial(inner_kernel, comps, depth_z, width),
        out_shape=jax.ShapeDtypeStruct((comps, depth_z + 2, width, depth), jnp.float32),
        in_specs=[VM] * 4,
        out_specs=VM,
        compiler_params=pltpu.CompilerParams(vmem_limit_bytes=24 * 1024 * 1024),
        cost_estimate=pl.CostEstimate(flops=10**7, bytes_accessed=2**22, transcendentals=0),
        name="inner",
    )(flow, viscosity, below, above)


def outer_kernel(comps, depth_z, width, flow, viscosity, below, above, first, left, right, low_corner, high_corner, inlet, second_out, inlet_now, strip, visc, started, table):
    depth = flow.shape[1]
    two = 2 * width
    rows = depth_z * width
    total = comps * rows
    base = 2 * comps * depth_z
    strip[...] = jnp.zeros_like(strip)
    visc[...] = jnp.zeros_like(visc)
    for c in range(comps):
        for z in range(-2, depth_z + 2):
            if z < 0:
                ref, spot = below, c * two + (2 + z) * width
            elif z >= depth_z:
                ref, spot = above, c * two + (z - depth_z) * width
            else:
                ref, spot = flow, (c * depth_z + z) * width
            strip[c, z + 2, 2:4, :] = ref[spot : spot + 2, :]
            strip[c, z + 2, 4:6, :] = ref[spot + width - 2 : spot + width, :]
            if 0 <= z < depth_z:
                k = 2 * (c * depth_z + z)
                strip[c, z + 2, 0:2, :] = left[k : k + 2, :]
                strip[c, z + 2, 6:8, :] = right[k : k + 2, :]
            elif z in (-1, depth_z):
                corner = low_corner if z < 0 else high_corner
                strip[c, z + 2, 1:2, :] = corner[c : c + 1, :]
                strip[c, z + 2, 6:7, :] = corner[comps + c : comps + c + 1, :]
    for z in range(-1, depth_z + 1):
        if z < 0:
            ref, spot = below, comps * two
        elif z == depth_z:
            ref, spot = above, comps * two
        else:
            ref, spot = viscosity, z * width
            visc[z + 1, 1:2, :] = left[base + z : base + z + 1, :]
            visc[z + 1, 6:7, :] = right[base + z : base + z + 1, :]
        visc[z + 1, 2:4, :] = ref[spot : spot + 2, :]
        visc[z + 1, 4:6, :] = ref[spot + width - 2 : spot + width, :]

    place = lax.broadcasted_iota(jnp.int32, (width, 1), 0)
    blank = jnp.zeros((6, depth), jnp.float32)

    def one(z, carry):
        plane, upper, lower = ([strip[c, z + 1 + d] for c in range(comps)] for d in (0, 1, -1))
        centers, change = tendency(plane, upper, lower, visc[z], 8)
        for c in range(comps):
            edge = centers[c] + change[c]
            mine = first[c, z]
            mine = jnp.where(place == 0, edge[2:3], mine)
            mine = jnp.where(place == width - 1, edge[5:6], mine)
            started[c, z, 0:width, :] = mine
            started[c, z, width : width + 8, :] = jnp.concatenate([edge[6:7], blank, edge[1:2]], axis=0)
        return carry

    lax.fori_loop(0, depth_z + 2, one, 0)

    def second(z, carry):
        plane = [started[c, z + 1] for c in range(comps)]
        upper, lower = ([started[c, z + 1 + d, 0:width, :] for c in range(comps)] for d in (1, -1))
        at = pl.multiple_of(z * width, width)
        centers, change = tendency(plane, upper, lower, viscosity[pl.ds(at, width), :], width)
        for c in range(comps):
            spot = pl.multiple_of((c * depth_z + z) * width, width)
            value = 0.5 * flow[pl.ds(spot, width), :] + 0.5 * (centers[c] + change[c])
            second_out[pl.ds(spot, width), :] = value
            high, low = halves(value)
            table[pl.ds(spot, width), :] = high
            table[pl.ds(total + spot, width), :] = low
        return carry

    lax.fori_loop(0, depth_z, second, 0)

    cells = inlet[0:1, :]
    picked = jnp.dot(table[...], column_hot(cells, depth), preferred_element_type=jnp.float32)
    row = lax.broadcasted_iota(jnp.int32, (rows, cells.shape[1]), 0) == (cells >> (depth.bit_length() - 1))
    for c in range(comps):
        both = picked[c * rows : (c + 1) * rows] + picked[total + c * rows : total + (c + 1) * rows]
        inlet_now[c : c + 1, :] = jnp.sum(jnp.where(row, both, 0.0), axis=0, keepdims=True)


def outer(comps, depth_z, width, flow, viscosity, below, above, first, left, right, low_corner, high_corner, inlet):
    depth = flow.shape[1]
    return pl.pallas_call(
        functools.partial(outer_kernel, comps, depth_z, width),
        out_shape=(
            jax.ShapeDtypeStruct(flow.shape, jnp.float32),
            jax.ShapeDtypeStruct((comps, inlet.shape[1]), jnp.float32),
        ),
        in_specs=[VM] * 10,
        out_specs=(VM, VM),
        scratch_shapes=[
            pltpu.VMEM((comps, depth_z + 4, 8, depth), jnp.float32),
            pltpu.VMEM((depth_z + 2, 8, depth), jnp.float32),
            pltpu.VMEM((comps, depth_z + 2, width + 8, depth), jnp.float32),
            pltpu.VMEM((2 * flow.shape[0], depth), jnp.bfloat16),
        ],
        compiler_params=pltpu.CompilerParams(vmem_limit_bytes=24 * 1024 * 1024),
        cost_estimate=pl.CostEstimate(flops=10**7, bytes_accessed=2**22, transcendentals=0),
        name="outer",
    )(flow, viscosity, below, above, first, left, right, low_corner, high_corner, inlet)


def on_device(
    flow_field,
    viscosity,
    port_plane,
    port_match,
    inlet_cell,
    inclusion_state,
    response_rate,
    inclusion_mass,
    anchor_cell,
    live_counts,
    arrival_cell,
):
    comps, depth_z, width, depth = flow_field.shape
    partners, cap = anchor_cell.shape[2:]
    sizes = (comps, depth_z, width)
    flow = flow_field.reshape(-1, depth)
    visc = viscosity.reshape(-1, depth)
    count = lax.axis_size("tile")
    forth = [(i, i + 1) for i in range(count - 1)]
    back = [(i + 1, i) for i in range(count - 1)]
    levels = lax.axis_size("sec")
    up = [(i, (i + 1) % levels) for i in range(levels)]
    down = [((i + 1) % levels, i) for i in range(levels)]
    over = [(i, (i + levels // 2) % levels) for i in range(levels)]

    low_edge, high_edge, low_cap, high_cap = rims(*sizes, flow, visc, port_plane)
    left = lax.ppermute(high_edge, "tile", forth)
    right = lax.ppermute(low_edge, "tile", back)
    below = lax.ppermute(high_cap, "sec", up)
    above = lax.ppermute(low_cap, "sec", down)
    across = lax.ppermute(port_plane, "sec", over)
    counts = live_counts.reshape(-1)
    counts, low_cap, high_cap = lax.optimization_barrier((counts, low_cap, high_cap))
    sampled = sample(comps, counts, flow, anchor_cell.reshape(partners, cap))
    outgoing = slip(
        counts,
        sampled,
        inclusion_state.reshape(comps, partners, cap),
        response_rate.reshape(partners, cap),
        inclusion_mass.reshape(partners, cap),
        port_plane,
        above,
        across,
        below,
    )
    left, right, below, above, outgoing = lax.optimization_barrier((left, right, below, above, outgoing))
    arrived = lax.all_to_all(outgoing, "tile", split_axis=0, concat_axis=0, tiled=True)
    low_out, high_out, bottom, top = corners(*sizes, below, above, left, right)
    low_corner = lax.ppermute(high_out, "sec", up[:-1])
    high_corner = lax.ppermute(low_out, "sec", down[:-1])
    inlet = jnp.pad(inlet_cell.reshape(1, -1), ((0, 0), (0, cap - inlet_cell.shape[0])))
    first = inner(*sizes, flow, visc, bottom, top)
    second, inlet_now = outer(*sizes, flow, visc, bottom, top, first, left, right, low_corner, high_corner, inlet)
    flow_next, arrived_state = land(
        port_match, second, inlet_now, inlet, arrival_cell.reshape(partners, cap), arrived
    )
    return flow_next.reshape(flow_field.shape), arrived_state.reshape(inclusion_state.shape)


def solution(mesh):
    return jax.shard_map(
        on_device,
        mesh=mesh,
        in_specs=(
            P(None, "sec", "tile", None),
            P("sec", "tile", None),
            P(None, ("sec", "tile")),
            P(("sec", "tile")),
            P(("sec", "tile")),
            P(None, "sec", "tile", None, None),
            P("sec", "tile", None, None),
            P("sec", "tile", None, None),
            P("sec", "tile", None, None),
            P("sec", "tile", None),
            P("sec", "tile", None, None),
        ),
        out_specs=(P(None, "sec", "tile", None), P(None, "sec", "tile", None, None)),
        check_vma=False,
    )
```

```python
import functools

import jax
import jax.numpy as jnp
from jax import lax
from jax.experimental import pallas as pl
from jax.experimental.pallas import tpu as pltpu
from jax.sharding import PartitionSpec as P

VM = pl.BlockSpec(memory_space=pltpu.VMEM)
SM = pl.BlockSpec(memory_space=pltpu.SMEM)
HB = pl.BlockSpec(memory_space=pltpu.HBM)


def halves(value):
    high = value.astype(jnp.bfloat16)
    low = (value - high.astype(jnp.float32)).astype(jnp.bfloat16)
    return high, low


def column_hot(cells, depth):
    at = lax.broadcasted_iota(jnp.int32, (depth, cells.shape[1]), 0)
    return jnp.where(at == (cells & (depth - 1)), 1.0, 0.0).astype(jnp.bfloat16)


def sample_kernel(GP, counts, flow, anchor, sampled, table, packed):
    partners, cap = anchor.shape
    total, depth = flow.shape
    comps = sampled.shape[1]
    rows = total // comps
    shift = depth.bit_length() - 1
    cap_shift = cap.bit_length() - 1
    lane = lax.broadcasted_iota(jnp.int32, (1, cap), 1)
    packed[...] = jnp.zeros_like(packed)

    def pack(p, base):
        begin = base & (cap - 1)
        spot = base >> cap_shift
        turned = pltpu.roll(anchor[pl.ds(p, 1), :], begin, 1)
        pltpu.store(packed.at[pl.ds(spot, 1), :], turned, mask=lane >= begin)
        pltpu.store(packed.at[pl.ds(spot + 1, 1), :], turned, mask=lane < begin)
        return base + counts[p]

    used = lax.fori_loop(0, partners, pack, 0, unroll=8)
    high, low = halves(flow[...])
    table[0:total] = high
    table[total:] = low

    def group(g, carry):
        first = g * GP
        cells = jnp.concatenate([packed[pl.ds(first + i, 1), :] for i in range(GP)], axis=1)
        hot = column_hot(cells, depth)
        picked = jnp.dot(table[...], hot, preferred_element_type=jnp.float32)
        row = lax.broadcasted_iota(jnp.int32, (rows, cells.shape[1]), 0) == (cells >> shift)
        parts = []
        for c in range(comps):
            both = picked[c * rows : (c + 1) * rows] + picked[total + c * rows : total + (c + 1) * rows]
            parts.append(jnp.sum(jnp.where(row, both, 0.0), axis=0, keepdims=True))
        found = jnp.concatenate(parts, axis=0)
        for i in range(GP):
            sampled[first + i] = found[:, i * cap : (i + 1) * cap]
        return carry

    lax.fori_loop(0, (used + GP * cap - 1) // (GP * cap), group, 0)


def sample(comps, counts, flow, anchor, GP=4):
    partners, cap = anchor.shape
    return pl.pallas_call(
        functools.partial(sample_kernel, GP),
        out_shape=jax.ShapeDtypeStruct((partners + 8, comps, cap), jnp.float32),
        in_specs=[SM, VM, VM],
        out_specs=VM,
        scratch_shapes=[
            pltpu.VMEM((2 * flow.shape[0], flow.shape[1]), jnp.bfloat16),
            pltpu.VMEM((partners + 8, cap), jnp.int32),
        ],
        compiler_params=pltpu.CompilerParams(vmem_limit_bytes=24 * 1024 * 1024),
        cost_estimate=pl.CostEstimate(flops=2 * 8192 * 512 * 1024, bytes_accessed=2**21, transcendentals=0),
        name="sample",
    )(counts, flow, anchor)


chunks = 4


def slip_kernel(counts, sampled, state, rate, mass, ports, above, across, below, far, out, whole, out_sems):
    comps, partners, cap = state.shape
    per = ports.shape[1]
    cap_shift = cap.bit_length() - 1
    last = above.shape[0] - 8
    lane = lax.broadcasted_iota(jnp.int32, (1, cap), 1)
    whole[:, 0:per] = ports[...]
    whole[:, per : 2 * per] = above[last : last + comps, 0:per]
    whole[:, 2 * per : 3 * per] = across[...]
    whole[:, 3 * per :] = below[last : last + comps, 0:per]

    def finish(p, base):
        n = counts[p]
        begin = base & (cap - 1)
        spot = base >> cap_shift
        both = jnp.where(lane >= begin, sampled[spot], sampled[spot + 1])
        value = pltpu.roll(both, (cap - begin) & (cap - 1), 1)
        own = jnp.concatenate([state[c, pl.ds(p, 1), :] for c in range(comps)], axis=0)
        r = rate[pl.ds(p, 1), :]
        drop = r * (own - value)
        live = lane < n
        out[3 * p] = jnp.where(live, own - drop, 0.0)
        out[3 * p + 1] = jnp.where(live, mass[pl.ds(p, 1), :] * drop, 0.0)
        out[3 * p + 2] = whole[...]
        return base + n

    block = partners // chunks
    base = 0
    copies = []
    for i in range(chunks):
        base = lax.fori_loop(i * block, (i + 1) * block, finish, base, unroll=8)
        part = pl.ds(3 * i * block, 3 * block)
        copies.append(pltpu.make_async_copy(out.at[part], far.at[part], out_sems.at[i]))
        copies[i].start()
    for copy in copies:
        copy.wait()


def slip(counts, sampled, state, rate, mass, ports, above, across, below):
    comps, partners, cap = state.shape
    return pl.pallas_call(
        slip_kernel,
        out_shape=jax.ShapeDtypeStruct((partners * 3, comps, cap), jnp.float32),
        in_specs=[SM] + [VM] * 8,
        out_specs=HB,
        scratch_shapes=[
            pltpu.VMEM((partners * 3, comps, cap), jnp.float32),
            pltpu.VMEM((comps, cap), jnp.float32),
            pltpu.SemaphoreType.DMA((chunks,)),
        ],
        compiler_params=pltpu.CompilerParams(vmem_limit_bytes=24 * 1024 * 1024),
        cost_estimate=pl.CostEstimate(flops=2 * 10**6, bytes_accessed=2**20, transcendentals=0),
        name="slip",
    )(counts, sampled, state, rate, mass, ports, above, across, below)


def land_kernel(GP, match, second, inlet_now, inlet, arrival, arrived, flow_far, state_far, flow_out, state_out, last_ref, last, packed, sem, out_sems):
    comps, partners, cap = state_out.shape
    total, depth = second.shape
    rows = total // comps
    shift = depth.bit_length() - 1
    cap_shift = cap.bit_length() - 1
    entries = match.shape[0]
    per = entries
    nt = (((1,), (1,)), ((), ()))
    slot = lax.broadcasted_iota(jnp.int32, (1, cap), 1)

    def ends(p, carry):
        moved = arrived[3 * p]
        gift = arrived[3 * p + 1]
        for c in range(comps):
            state_out[c, pl.ds(p, 1), :] = moved[c : c + 1]
        biggest = jnp.max(jnp.abs(gift), axis=0, keepdims=True)
        last_ref[pl.ds(p, 1), :] = jnp.where(biggest > 0.0, slot + 1, 0)
        return carry

    lax.fori_loop(0, partners, ends, 0, unroll=8)
    last_ref[partners:, :] = jnp.zeros_like(last_ref[partners:, :])
    top = jnp.max(last_ref[...].T, axis=0, keepdims=True)
    last_ref[0:1, :] = top
    fetch = pltpu.make_async_copy(last_ref.at[0:1, :], last, sem)
    fetch.start()
    state_copy = pltpu.make_async_copy(state_out, state_far, out_sems.at[2])
    state_copy.start()
    flow_out[...] = second[...]

    def add(cells, values, spot):
        row = lax.broadcasted_iota(jnp.int32, (rows, cells.shape[1]), 0) == (cells >> shift)
        high, low = halves(values)
        parts = []
        for part in (high.astype(jnp.float32), low.astype(jnp.float32)):
            for c in range(values.shape[0]):
                parts.append(jnp.where(row, part[c : c + 1], 0.0).astype(jnp.bfloat16))
        both = lax.dot_general(
            jnp.concatenate(parts, axis=0), column_hot(cells, depth), nt, preferred_element_type=jnp.float32
        )
        half = values.shape[0] * rows
        flow_out[spot : spot + half, :] += both[:half] + both[half:]

    section = lax.axis_index("sec")
    sections = cap // per
    target = jnp.zeros((comps, cap), jnp.float32)
    for k in range(entries):
        port = match[k]
        device = port // entries
        place = (device // partners + sections - section) % sections * per + port % entries
        turned = pltpu.roll(arrived[3 * (device % partners) + 2], (k + cap - place) % cap, 1)
        target = jnp.where(slot == k, turned, target)
    change = jnp.where(slot < entries, 0.5 * (target - inlet_now[...]), 0.0)
    packed[...] = jnp.zeros_like(packed)
    fetch.wait()

    def pack(p, base):
        begin = base & (cap - 1)
        spot = base >> cap_shift
        cells = arrival[pl.ds(p, 1), :].astype(jnp.float32)
        both = jnp.concatenate([arrived[3 * p + 1], jnp.broadcast_to(cells, (8 - comps, cap))], axis=0)
        turned = pltpu.roll(both, begin, 1)
        wide = lax.broadcasted_iota(jnp.int32, (8, cap), 1)
        pltpu.store(packed.at[spot], turned, mask=wide >= begin)
        pltpu.store(packed.at[spot + 1], turned, mask=wide < begin)
        return base + last[0, p]

    used = lax.fori_loop(0, partners, pack, 0, unroll=8)

    spare = (used + cap - 1) >> cap_shift
    cells = jnp.broadcast_to(inlet[0:1, :].astype(jnp.float32), (8 - comps, cap))
    packed[spare] = jnp.concatenate([change, cells], axis=0)

    def load(g):
        both = jnp.concatenate([packed[g * GP + i] for i in range(GP)], axis=1)
        return both[comps : comps + 1].astype(jnp.int32), both[:comps]

    def group(g, carry):
        cells, values = load(g)
        add(cells, values, 0)
        return carry

    final = spare // GP
    lax.fori_loop(0, final, group, 0)
    cells, values = load(final)
    half = comps // 2
    copies = []
    for i in range(2):
        part = pl.ds(i * half * rows, half * rows)
        add(cells, values[i * half : (i + 1) * half], i * half * rows)
        copies.append(pltpu.make_async_copy(flow_out.at[part, :], flow_far.at[part, :], out_sems.at[i]))
        copies[i].start()
    for copy in copies:
        copy.wait()
    state_copy.wait()


def land(match, second, inlet_now, inlet, arrival, arrived, GP=4):
    partners, cap = arrival.shape
    comps = arrived.shape[1]
    return pl.pallas_call(
        functools.partial(land_kernel, GP),
        out_shape=(
            jax.ShapeDtypeStruct(second.shape, jnp.float32),
            jax.ShapeDtypeStruct((comps, partners, cap), jnp.float32),
        ),
        in_specs=[SM] + [VM] * 5,
        out_specs=(HB, HB),
        scratch_shapes=[
            pltpu.VMEM(second.shape, jnp.float32),
            pltpu.VMEM((comps, partners, cap), jnp.float32),
            pltpu.VMEM((cap, cap), jnp.int32),
            pltpu.SMEM((1, cap), jnp.int32),
            pltpu.VMEM((partners + 8, 8, cap), jnp.float32),
            pltpu.SemaphoreType.DMA,
            pltpu.SemaphoreType.DMA((3,)),
        ],
        compiler_params=pltpu.CompilerParams(vmem_limit_bytes=24 * 1024 * 1024),
        cost_estimate=pl.CostEstimate(flops=2 * 8192 * 512 * 1024, bytes_accessed=2**21, transcendentals=0),
        name="land",
    )(match, second, inlet_now, inlet, arrival, arrived)


def tendency(plane, upper, lower, viscosity, keep):
    place = lax.broadcasted_iota(jnp.int32, (1, viscosity.shape[1]), 1)
    depth = viscosity.shape[1]
    centers, laps, dz, dx, dy = [], [], [], [], []
    for c in range(len(plane)):
        whole = plane[c]
        center = whole[:keep]
        up_x = pltpu.roll(whole, whole.shape[0] - 1, 0)[:keep]
        low_x = pltpu.roll(whole, 1, 0)[:keep]
        up_y = jnp.where(place == depth - 1, 0.0, pltpu.roll(center, depth - 1, 1))
        low_y = jnp.where(place == 0, 0.0, pltpu.roll(center, 1, 1))
        centers.append(center)
        laps.append((upper[c] + lower[c]) + (up_x + low_x) + (up_y + low_y) - 6.0 * center)
        dz.append(upper[c] - lower[c])
        dx.append(up_x - low_x)
        dy.append(up_y - low_y)
    strain = sum(d[c] * d[c] for c in range(3) for d in (dz, dx, dy)) * 0.25
    eddy = viscosity * (1.0 + strain / (1.0 + strain))
    out = []
    for c in range(len(plane)):
        carried = centers[0] * dz[c] + centers[1] * dx[c] + centers[2] * dy[c]
        out.append(0.5 * (eddy * laps[c]) - 0.25 * carried)
    return centers, out


def cap_kernel(comps, depth_z, width, flow, viscosity, ports, low_out, high_out, sems):
    copies = []

    def copy(source, target):
        copies.append(pltpu.make_async_copy(source, target, sems.at[len(copies)]))
        copies[-1].start()

    two = 2 * width
    last = (depth_z - 1) * width
    for c in range(comps):
        base = c * depth_z * width
        copy(flow.at[base : base + two, :], low_out.at[c * two : (c + 1) * two, :])
        copy(flow.at[base + last - width : base + last + width, :], high_out.at[c * two : (c + 1) * two, :])
    base = comps * two
    copy(viscosity.at[0:width, :], low_out.at[base : base + width, :])
    copy(viscosity.at[last : last + width, :], high_out.at[base : base + width, :])
    for out in (low_out, high_out):
        out[base + width :, :] = jnp.zeros((8, out.shape[1]), jnp.float32)
        out[base + width : base + width + comps, 0 : ports.shape[1]] = ports[...]
    for started in copies:
        started.wait()


def caps(comps, depth_z, width, flow, viscosity, ports):
    shape = jax.ShapeDtypeStruct((2 * comps * width + width + 8, flow.shape[1]), jnp.float32)
    return pl.pallas_call(
        functools.partial(cap_kernel, comps, depth_z, width),
        out_shape=(shape, shape),
        in_specs=[HB, HB, VM],
        out_specs=(VM, VM),
        scratch_shapes=[pltpu.SemaphoreType.DMA((2 * comps + 2,))],
        compiler_params=pltpu.CompilerParams(vmem_limit_bytes=60 * 1024 * 1024),
        name="caps",
    )(flow, viscosity, ports)


def edge_kernel(comps, depth_z, width, flow, viscosity, below, above, low_out, high_out, bottom, top):
    section = lax.axis_index("sec")
    bottom[...] = jnp.where(section > 0, below[0 : bottom.shape[0], :], 0.0)
    top[...] = jnp.where(section < lax.axis_size("sec") - 1, above[0 : top.shape[0], :], 0.0)
    two = 2 * width
    for k in range(comps * depth_z):
        low_out[2 * k : 2 * k + 2, :] = flow[k * width : k * width + 2, :]
        high_out[2 * k : 2 * k + 2, :] = flow[(k + 1) * width - 2 : (k + 1) * width, :]
    base = 2 * comps * depth_z
    for c in range(comps):
        low_out[base + 2 * c : base + 2 * c + 1, :] = bottom[c * two + width : c * two + width + 1, :]
        low_out[base + 2 * c + 1 : base + 2 * c + 2, :] = top[c * two : c * two + 1, :]
        high_out[base + 2 * c : base + 2 * c + 1, :] = bottom[(c + 1) * two - 1 : (c + 1) * two, :]
        high_out[base + 2 * c + 1 : base + 2 * c + 2, :] = top[c * two + width - 1 : c * two + width, :]
    base += 2 * comps
    for z in range(depth_z):
        low_out[base + z : base + z + 1, :] = viscosity[z * width : z * width + 1, :]
        high_out[base + z : base + z + 1, :] = viscosity[(z + 1) * width - 1 : (z + 1) * width, :]


def edges(comps, depth_z, width, flow, viscosity, below, above):
    depth = flow.shape[1]
    shape = jax.ShapeDtypeStruct((2 * comps * (depth_z + 1) + depth_z, depth), jnp.float32)
    halo = jax.ShapeDtypeStruct(((2 * comps + 1) * width, depth), jnp.float32)
    return pl.pallas_call(
        functools.partial(edge_kernel, comps, depth_z, width),
        out_shape=(shape, shape, halo, halo),
        in_specs=[VM] * 4,
        out_specs=(VM,) * 4,
        compiler_params=pltpu.CompilerParams(vmem_limit_bytes=24 * 1024 * 1024),
        name="edges",
    )(flow, viscosity, below, above)


def inner_kernel(comps, depth_z, width, flow, viscosity, below, above, first, middle):
    two = 2 * width

    def own(z):
        if z < 0:
            return [below[c * two + (2 + z) * width : c * two + (3 + z) * width, :] for c in range(comps)]
        if z >= depth_z:
            return [above[c * two + (z - depth_z) * width : c * two + (z - depth_z + 1) * width, :] for c in range(comps)]
        return [flow[(c * depth_z + z) * width : (c * depth_z + z + 1) * width, :] for c in range(comps)]

    for z in range(-1, depth_z + 1):
        if z < 0:
            visc = below[comps * two :, :]
        elif z == depth_z:
            visc = above[comps * two :, :]
        else:
            visc = viscosity[z * width : (z + 1) * width, :]
        centers, change = tendency(own(z), own(z + 1), own(z - 1), visc, width)
        for c in range(comps):
            first[c, z + 1, 0:width, :] = centers[c] + change[c]

    def second(z, carry):
        plane, upper, lower = ([first[c, z + 1 + d] for c in range(comps)] for d in (0, 1, -1))
        at = pl.multiple_of(z * width, width)
        centers, change = tendency(plane, upper, lower, viscosity[pl.ds(at, width), :], width)
        for c in range(comps):
            spot = pl.multiple_of((c * depth_z + z) * width, width)
            middle[pl.ds(spot, width), :] = 0.5 * flow[pl.ds(spot, width), :] + 0.5 * (centers[c] + change[c])
        return carry

    lax.fori_loop(0, depth_z, second, 0)


def inner(comps, depth_z, width, flow, viscosity, below, above):
    depth = flow.shape[1]
    return pl.pallas_call(
        functools.partial(inner_kernel, comps, depth_z, width),
        out_shape=(
            jax.ShapeDtypeStruct((comps, depth_z + 2, width, depth), jnp.float32),
            jax.ShapeDtypeStruct(flow.shape, jnp.float32),
        ),
        in_specs=[VM] * 4,
        out_specs=(VM, VM),
        compiler_params=pltpu.CompilerParams(vmem_limit_bytes=24 * 1024 * 1024),
        cost_estimate=pl.CostEstimate(flops=10**7, bytes_accessed=2**22, transcendentals=0),
        name="inner",
    )(flow, viscosity, below, above)


def outer_kernel(comps, depth_z, width, flow, viscosity, below, above, first, middle, left, right, inlet, second_out, inlet_now, strip, visc, started, table):
    depth = flow.shape[1]
    two = 2 * width
    rows = depth_z * width
    total = comps * rows
    base = 2 * comps * depth_z
    strip[...] = jnp.zeros_like(strip)
    visc[...] = jnp.zeros_like(visc)
    for c in range(comps):
        for z in range(-2, depth_z + 2):
            if z < 0:
                ref, spot = below, c * two + (2 + z) * width
            elif z >= depth_z:
                ref, spot = above, c * two + (z - depth_z) * width
            else:
                ref, spot = flow, (c * depth_z + z) * width
            strip[c, z + 2, 2:4, :] = ref[spot : spot + 2, :]
            strip[c, z + 2, 4:6, :] = ref[spot + width - 2 : spot + width, :]
            if 0 <= z < depth_z:
                k = 2 * (c * depth_z + z)
                strip[c, z + 2, 0:2, :] = left[k : k + 2, :]
                strip[c, z + 2, 6:8, :] = right[k : k + 2, :]
            elif z in (-1, depth_z):
                k = base + 2 * c + (z == depth_z)
                strip[c, z + 2, 1:2, :] = left[k : k + 1, :]
                strip[c, z + 2, 6:7, :] = right[k : k + 1, :]
    side = base + 2 * comps
    for z in range(-1, depth_z + 1):
        if z < 0:
            ref, spot = below, comps * two
        elif z == depth_z:
            ref, spot = above, comps * two
        else:
            ref, spot = viscosity, z * width
            visc[z + 1, 1:2, :] = left[side + z : side + z + 1, :]
            visc[z + 1, 6:7, :] = right[side + z : side + z + 1, :]
        visc[z + 1, 2:4, :] = ref[spot : spot + 2, :]
        visc[z + 1, 4:6, :] = ref[spot + width - 2 : spot + width, :]

    place = lax.broadcasted_iota(jnp.int32, (8, 1), 0)

    def apart(value):
        return jnp.where(place < 4, pltpu.roll(value, 7, 0), pltpu.roll(value, 1, 0))

    def one(z, carry):
        plane, upper, lower = ([strip[c, z + 1 + d] for c in range(comps)] for d in (0, 1, -1))
        centers, change = tendency(plane, upper, lower, visc[z], 8)
        for c in range(comps):
            ends = apart(centers[c] + change[c])
            near = jnp.where(place < 4, pltpu.roll(first[c, z, 0:8, :], 1, 0), pltpu.roll(first[c, z, width - 8 : width, :], 7, 0))
            started[c, z] = jnp.where((place < 2) | (place > 5), ends, near)
        return carry

    lax.fori_loop(0, depth_z + 2, one, 0, unroll=2)

    def second(z, carry):
        plane, upper, lower = ([started[c, z + 1 + d] for c in range(comps)] for d in (0, 1, -1))
        centers, change = tendency(plane, upper, lower, apart(visc[z + 1]), 8)
        for c in range(comps):
            spot = pl.multiple_of((c * depth_z + z) * width, width)
            edge = 0.5 * apart(strip[c, z + 2]) + 0.5 * (centers[c] + change[c])
            mine = middle[pl.ds(spot, width), :]
            top = jnp.where(place < 2, pltpu.roll(edge, 7, 0), mine[0:8])
            end = jnp.where(place > 5, pltpu.roll(edge, 1, 0), mine[width - 8 :])
            value = jnp.concatenate([top, mine[8 : width - 8], end] if width > 16 else [top, end], axis=0)
            second_out[pl.ds(spot, width), :] = value
            high, low = halves(value)
            table[pl.ds(spot, width), :] = high
            table[pl.ds(total + spot, width), :] = low
        return carry

    lax.fori_loop(0, depth_z, second, 0, unroll=2)

    cells = inlet[0:1, :]
    picked = jnp.dot(table[...], column_hot(cells, depth), preferred_element_type=jnp.float32)
    row = lax.broadcasted_iota(jnp.int32, (rows, cells.shape[1]), 0) == (cells >> (depth.bit_length() - 1))
    for c in range(comps):
        both = picked[c * rows : (c + 1) * rows] + picked[total + c * rows : total + (c + 1) * rows]
        inlet_now[c : c + 1, :] = jnp.sum(jnp.where(row, both, 0.0), axis=0, keepdims=True)


def outer(comps, depth_z, width, flow, viscosity, below, above, first, middle, left, right, inlet):
    depth = flow.shape[1]
    return pl.pallas_call(
        functools.partial(outer_kernel, comps, depth_z, width),
        out_shape=(
            jax.ShapeDtypeStruct(flow.shape, jnp.float32),
            jax.ShapeDtypeStruct((comps, inlet.shape[1]), jnp.float32),
        ),
        in_specs=[VM] * 9,
        out_specs=(VM, VM),
        scratch_shapes=[
            pltpu.VMEM((comps, depth_z + 4, 8, depth), jnp.float32),
            pltpu.VMEM((depth_z + 2, 8, depth), jnp.float32),
            pltpu.VMEM((comps, depth_z + 2, 8, depth), jnp.float32),
            pltpu.VMEM((2 * flow.shape[0], depth), jnp.bfloat16),
        ],
        compiler_params=pltpu.CompilerParams(vmem_limit_bytes=24 * 1024 * 1024),
        cost_estimate=pl.CostEstimate(flops=10**7, bytes_accessed=2**22, transcendentals=0),
        name="outer",
    )(flow, viscosity, below, above, first, middle, left, right, inlet)


def on_device(
    flow_field,
    viscosity,
    port_plane,
    port_match,
    inlet_cell,
    inclusion_state,
    response_rate,
    inclusion_mass,
    anchor_cell,
    live_counts,
    arrival_cell,
):
    comps, depth_z, width, depth = flow_field.shape
    partners, cap = anchor_cell.shape[2:]
    sizes = (comps, depth_z, width)
    flow = flow_field.reshape(-1, depth)
    visc = viscosity.reshape(-1, depth)
    count = lax.axis_size("tile")
    forth = [(i, i + 1) for i in range(count - 1)]
    back = [(i + 1, i) for i in range(count - 1)]
    levels = lax.axis_size("sec")
    up = [(i, (i + 1) % levels) for i in range(levels)]
    down = [((i + 1) % levels, i) for i in range(levels)]
    over = [(i, (i + levels // 2) % levels) for i in range(levels)]

    low_cap, high_cap = caps(*sizes, flow, visc, port_plane)
    below = lax.ppermute(high_cap, "sec", up)
    above = lax.ppermute(low_cap, "sec", down)
    across = lax.ppermute(port_plane, "sec", over)
    counts = live_counts.reshape(-1)
    counts, low_cap, high_cap = lax.optimization_barrier((counts, low_cap, high_cap))
    sampled = sample(comps, counts, flow, anchor_cell.reshape(partners, cap))
    outgoing = slip(
        counts,
        sampled,
        inclusion_state.reshape(comps, partners, cap),
        response_rate.reshape(partners, cap),
        inclusion_mass.reshape(partners, cap),
        port_plane,
        above,
        across,
        below,
    )
    below, above, outgoing = lax.optimization_barrier((below, above, outgoing))
    arrived = lax.all_to_all(outgoing, "tile", split_axis=0, concat_axis=0, tiled=True)
    low_edge, high_edge, bottom, top = edges(*sizes, flow, visc, below, above)
    left = lax.ppermute(high_edge, "tile", forth)
    right = lax.ppermute(low_edge, "tile", back)
    inlet = jnp.pad(inlet_cell.reshape(1, -1), ((0, 0), (0, cap - inlet_cell.shape[0])))
    first, middle = inner(*sizes, flow, visc, bottom, top)
    second, inlet_now = outer(*sizes, flow, visc, bottom, top, first, middle, left, right, inlet)
    flow_next, arrived_state = land(
        port_match, second, inlet_now, inlet, arrival_cell.reshape(partners, cap), arrived
    )
    return flow_next.reshape(flow_field.shape), arrived_state.reshape(inclusion_state.shape)


def solution(mesh):
    return jax.shard_map(
        on_device,
        mesh=mesh,
        in_specs=(
            P(None, "sec", "tile", None),
            P("sec", "tile", None),
            P(None, ("sec", "tile")),
            P(("sec", "tile")),
            P(("sec", "tile")),
            P(None, "sec", "tile", None, None),
            P("sec", "tile", None, None),
            P("sec", "tile", None, None),
            P("sec", "tile", None, None),
            P("sec", "tile", None),
            P("sec", "tile", None, None),
        ),
        out_specs=(P(None, "sec", "tile", None), P(None, "sec", "tile", None, None)),
        check_vma=False,
    )
```

```python
import functools

import jax
import jax.numpy as jnp
from jax import lax
from jax.experimental import pallas as pl
from jax.experimental.pallas import tpu as pltpu
from jax.sharding import PartitionSpec as P

VM = pl.BlockSpec(memory_space=pltpu.VMEM)
SM = pl.BlockSpec(memory_space=pltpu.SMEM)
HB = pl.BlockSpec(memory_space=pltpu.HBM)


def halves(value):
    high = value.astype(jnp.bfloat16)
    low = (value - high.astype(jnp.float32)).astype(jnp.bfloat16)
    return high, low


def column_hot(cells, depth):
    at = lax.broadcasted_iota(jnp.int32, (depth, cells.shape[1]), 0)
    return jnp.where(at == (cells & (depth - 1)), 1.0, 0.0).astype(jnp.bfloat16)


def sample_kernel(GP, counts, flow, anchor, sampled, table, packed):
    partners, cap = anchor.shape
    total, depth = flow.shape
    comps = sampled.shape[1]
    rows = total // comps
    shift = depth.bit_length() - 1
    cap_shift = cap.bit_length() - 1
    lane = lax.broadcasted_iota(jnp.int32, (1, cap), 1)
    packed[...] = jnp.zeros_like(packed)

    def pack(p, base):
        begin = base & (cap - 1)
        spot = base >> cap_shift
        turned = pltpu.roll(anchor[pl.ds(p, 1), :], begin, 1)
        pltpu.store(packed.at[pl.ds(spot, 1), :], turned, mask=lane >= begin)
        pltpu.store(packed.at[pl.ds(spot + 1, 1), :], turned, mask=lane < begin)
        return base + counts[p]

    used = lax.fori_loop(0, partners, pack, 0, unroll=8)
    high, low = halves(flow[...])
    table[0:total] = high
    table[total:] = low

    def group(g, carry):
        first = g * GP
        cells = jnp.concatenate([packed[pl.ds(first + i, 1), :] for i in range(GP)], axis=1)
        hot = column_hot(cells, depth)
        picked = jnp.dot(table[...], hot, preferred_element_type=jnp.float32)
        row = lax.broadcasted_iota(jnp.int32, (rows, cells.shape[1]), 0) == (cells >> shift)
        parts = []
        for c in range(comps):
            both = picked[c * rows : (c + 1) * rows] + picked[total + c * rows : total + (c + 1) * rows]
            parts.append(jnp.sum(jnp.where(row, both, 0.0), axis=0, keepdims=True))
        found = jnp.concatenate(parts, axis=0)
        for i in range(GP):
            sampled[first + i] = found[:, i * cap : (i + 1) * cap]
        return carry

    lax.fori_loop(0, (used + GP * cap - 1) // (GP * cap), group, 0)


def sample(comps, counts, flow, anchor, GP=4):
    partners, cap = anchor.shape
    return pl.pallas_call(
        functools.partial(sample_kernel, GP),
        out_shape=jax.ShapeDtypeStruct((partners + 8, comps, cap), jnp.float32),
        in_specs=[SM, VM, VM],
        out_specs=VM,
        scratch_shapes=[
            pltpu.VMEM((2 * flow.shape[0], flow.shape[1]), jnp.bfloat16),
            pltpu.VMEM((partners + 8, cap), jnp.int32),
        ],
        compiler_params=pltpu.CompilerParams(vmem_limit_bytes=24 * 1024 * 1024),
        cost_estimate=pl.CostEstimate(flops=2 * 8192 * 512 * 1024, bytes_accessed=2**21, transcendentals=0),
        name="sample",
    )(counts, flow, anchor)


chunks = 4


def slip_kernel(counts, sampled, state, rate, mass, ports, above, across, below, far, out, whole, out_sems):
    comps, partners, cap = state.shape
    per = ports.shape[1]
    cap_shift = cap.bit_length() - 1
    last = above.shape[0] - 8
    lane = lax.broadcasted_iota(jnp.int32, (1, cap), 1)
    whole[:, 0:per] = ports[...]
    whole[:, per : 2 * per] = above[last : last + comps, 0:per]
    whole[:, 2 * per : 3 * per] = across[...]
    whole[:, 3 * per :] = below[last : last + comps, 0:per]

    def finish(p, base):
        n = counts[p]
        begin = base & (cap - 1)
        spot = base >> cap_shift
        both = jnp.where(lane >= begin, sampled[spot], sampled[spot + 1])
        value = pltpu.roll(both, (cap - begin) & (cap - 1), 1)
        own = jnp.concatenate([state[c, pl.ds(p, 1), :] for c in range(comps)], axis=0)
        r = rate[pl.ds(p, 1), :]
        drop = r * (own - value)
        live = lane < n
        out[3 * p] = jnp.where(live, own - drop, 0.0)
        out[3 * p + 1] = jnp.where(live, mass[pl.ds(p, 1), :] * drop, 0.0)
        out[3 * p + 2] = whole[...]
        return base + n

    block = partners // chunks
    base = 0
    copies = []
    for i in range(chunks):
        base = lax.fori_loop(i * block, (i + 1) * block, finish, base, unroll=8)
        part = pl.ds(3 * i * block, 3 * block)
        copies.append(pltpu.make_async_copy(out.at[part], far.at[part], out_sems.at[i]))
        copies[i].start()
    for copy in copies:
        copy.wait()


def slip(counts, sampled, state, rate, mass, ports, above, across, below):
    comps, partners, cap = state.shape
    return pl.pallas_call(
        slip_kernel,
        out_shape=jax.ShapeDtypeStruct((partners * 3, comps, cap), jnp.float32),
        in_specs=[SM] + [VM] * 8,
        out_specs=HB,
        scratch_shapes=[
            pltpu.VMEM((partners * 3, comps, cap), jnp.float32),
            pltpu.VMEM((comps, cap), jnp.float32),
            pltpu.SemaphoreType.DMA((chunks,)),
        ],
        compiler_params=pltpu.CompilerParams(vmem_limit_bytes=24 * 1024 * 1024),
        cost_estimate=pl.CostEstimate(flops=2 * 10**6, bytes_accessed=2**20, transcendentals=0),
        name="slip",
    )(counts, sampled, state, rate, mass, ports, above, across, below)


def land_kernel(GP, match, second, inlet_now, inlet, arrival, arrived, flow_far, state_far, flow_out, state_out, last_ref, last, packed, sem, out_sems):
    comps, partners, cap = state_out.shape
    total, depth = second.shape
    rows = total // comps
    shift = depth.bit_length() - 1
    cap_shift = cap.bit_length() - 1
    entries = match.shape[0]
    per = entries
    nt = (((1,), (1,)), ((), ()))
    slot = lax.broadcasted_iota(jnp.int32, (1, cap), 1)

    def ends(p, carry):
        moved = arrived[3 * p]
        gift = arrived[3 * p + 1]
        for c in range(comps):
            state_out[c, pl.ds(p, 1), :] = moved[c : c + 1]
        biggest = jnp.max(jnp.abs(gift), axis=0, keepdims=True)
        last_ref[pl.ds(p, 1), :] = jnp.where(biggest > 0.0, slot + 1, 0)
        return carry

    lax.fori_loop(0, partners, ends, 0, unroll=8)
    last_ref[partners:, :] = jnp.zeros_like(last_ref[partners:, :])
    top = jnp.max(last_ref[...].T, axis=0, keepdims=True)
    last_ref[0:1, :] = top
    fetch = pltpu.make_async_copy(last_ref.at[0:1, :], last, sem)
    fetch.start()
    state_copy = pltpu.make_async_copy(state_out, state_far, out_sems.at[2])
    state_copy.start()
    flow_out[...] = second[...]

    def add(cells, values, spot):
        row = lax.broadcasted_iota(jnp.int32, (rows, cells.shape[1]), 0) == (cells >> shift)
        high, low = halves(values)
        parts = []
        for part in (high.astype(jnp.float32), low.astype(jnp.float32)):
            for c in range(values.shape[0]):
                parts.append(jnp.where(row, part[c : c + 1], 0.0).astype(jnp.bfloat16))
        both = lax.dot_general(
            jnp.concatenate(parts, axis=0), column_hot(cells, depth), nt, preferred_element_type=jnp.float32
        )
        half = values.shape[0] * rows
        flow_out[spot : spot + half, :] += both[:half] + both[half:]

    section = lax.axis_index("sec")
    sections = cap // per
    target = jnp.zeros((comps, cap), jnp.float32)
    for k in range(entries):
        port = match[k]
        device = port // entries
        place = (device // partners + sections - section) % sections * per + port % entries
        turned = pltpu.roll(arrived[3 * (device % partners) + 2], (k + cap - place) % cap, 1)
        target = jnp.where(slot == k, turned, target)
    change = jnp.where(slot < entries, 0.5 * (target - inlet_now[...]), 0.0)
    packed[...] = jnp.zeros_like(packed)
    fetch.wait()

    def pack(p, base):
        begin = base & (cap - 1)
        spot = base >> cap_shift
        cells = arrival[pl.ds(p, 1), :].astype(jnp.float32)
        both = jnp.concatenate([arrived[3 * p + 1], jnp.broadcast_to(cells, (8 - comps, cap))], axis=0)
        turned = pltpu.roll(both, begin, 1)
        wide = lax.broadcasted_iota(jnp.int32, (8, cap), 1)
        pltpu.store(packed.at[spot], turned, mask=wide >= begin)
        pltpu.store(packed.at[spot + 1], turned, mask=wide < begin)
        return base + last[0, p]

    used = lax.fori_loop(0, partners, pack, 0, unroll=8)

    spare = (used + cap - 1) >> cap_shift
    cells = jnp.broadcast_to(inlet[0:1, :].astype(jnp.float32), (8 - comps, cap))
    packed[spare] = jnp.concatenate([change, cells], axis=0)

    def load(g):
        both = jnp.concatenate([packed[g * GP + i] for i in range(GP)], axis=1)
        return both[comps : comps + 1].astype(jnp.int32), both[:comps]

    def group(g, carry):
        cells, values = load(g)
        add(cells, values, 0)
        return carry

    final = spare // GP
    lax.fori_loop(0, final, group, 0)
    cells, values = load(final)
    half = comps // 2
    copies = []
    for i in range(2):
        part = pl.ds(i * half * rows, half * rows)
        add(cells, values[i * half : (i + 1) * half], i * half * rows)
        copies.append(pltpu.make_async_copy(flow_out.at[part, :], flow_far.at[part, :], out_sems.at[i]))
        copies[i].start()
    for copy in copies:
        copy.wait()
    state_copy.wait()


def land(match, second, inlet_now, inlet, arrival, arrived, GP=4):
    partners, cap = arrival.shape
    comps = arrived.shape[1]
    return pl.pallas_call(
        functools.partial(land_kernel, GP),
        out_shape=(
            jax.ShapeDtypeStruct(second.shape, jnp.float32),
            jax.ShapeDtypeStruct((comps, partners, cap), jnp.float32),
        ),
        in_specs=[SM] + [VM] * 5,
        out_specs=(HB, HB),
        scratch_shapes=[
            pltpu.VMEM(second.shape, jnp.float32),
            pltpu.VMEM((comps, partners, cap), jnp.float32),
            pltpu.VMEM((cap, cap), jnp.int32),
            pltpu.SMEM((1, cap), jnp.int32),
            pltpu.VMEM((partners + 8, 8, cap), jnp.float32),
            pltpu.SemaphoreType.DMA,
            pltpu.SemaphoreType.DMA((3,)),
        ],
        compiler_params=pltpu.CompilerParams(vmem_limit_bytes=24 * 1024 * 1024),
        cost_estimate=pl.CostEstimate(flops=2 * 8192 * 512 * 1024, bytes_accessed=2**21, transcendentals=0),
        name="land",
    )(match, second, inlet_now, inlet, arrival, arrived)


def tendency(plane, upper, lower, viscosity, keep):
    place = lax.broadcasted_iota(jnp.int32, (1, viscosity.shape[1]), 1)
    depth = viscosity.shape[1]
    centers, laps, dz, dx, dy = [], [], [], [], []
    for c in range(len(plane)):
        whole = plane[c]
        center = whole[:keep]
        up_x = pltpu.roll(whole, whole.shape[0] - 1, 0)[:keep]
        low_x = pltpu.roll(whole, 1, 0)[:keep]
        up_y = jnp.where(place == depth - 1, 0.0, pltpu.roll(center, depth - 1, 1))
        low_y = jnp.where(place == 0, 0.0, pltpu.roll(center, 1, 1))
        centers.append(center)
        laps.append((upper[c] + lower[c]) + (up_x + low_x) + (up_y + low_y) - 6.0 * center)
        dz.append(upper[c] - lower[c])
        dx.append(up_x - low_x)
        dy.append(up_y - low_y)
    strain = sum(d[c] * d[c] for c in range(3) for d in (dz, dx, dy)) * 0.25
    eddy = viscosity * (1.0 + strain / (1.0 + strain))
    out = []
    for c in range(len(plane)):
        carried = centers[0] * dz[c] + centers[1] * dx[c] + centers[2] * dy[c]
        out.append(0.5 * (eddy * laps[c]) - 0.25 * carried)
    return centers, out


def rim_kernel(comps, depth_z, width, flow, viscosity, ports, high_edge, low_cap, high_cap):
    for k in range(comps * depth_z):
        high_edge[2 * k : 2 * k + 2, :] = flow[(k + 1) * width - 2 : (k + 1) * width, :]
    base = 2 * comps * depth_z
    for z in range(depth_z):
        high_edge[base + z : base + z + 1, :] = viscosity[(z + 1) * width - 1 : (z + 1) * width, :]
    two = 2 * width
    last = depth_z * width
    for c in range(comps):
        low_cap[c * two : (c + 1) * two, :] = flow[c * last : c * last + two, :]
        high_cap[c * two : (c + 1) * two, :] = flow[(c + 1) * last - two : (c + 1) * last, :]
    base = comps * two
    low_cap[base : base + width, :] = viscosity[0:width, :]
    high_cap[base : base + width, :] = viscosity[last - width : last, :]
    for out in (low_cap, high_cap):
        out[base + width :, :] = jnp.zeros((8, out.shape[1]), jnp.float32)
        out[base + width : base + width + comps, 0 : ports.shape[1]] = ports[...]


def rims(comps, depth_z, width, flow, viscosity, ports):
    depth = flow.shape[1]
    edge = jax.ShapeDtypeStruct(((2 * comps + 1) * depth_z, depth), jnp.float32)
    cap = jax.ShapeDtypeStruct((2 * comps * width + width + 8, depth), jnp.float32)
    return pl.pallas_call(
        functools.partial(rim_kernel, comps, depth_z, width),
        out_shape=(edge, cap, cap),
        in_specs=[VM] * 3,
        out_specs=(VM,) * 3,
        compiler_params=pltpu.CompilerParams(vmem_limit_bytes=60 * 1024 * 1024),
        name="rims",
    )(flow, viscosity, ports)


def edge_kernel(comps, depth_z, width, flow, viscosity, below, above, low_out, corner, bottom, top):
    section = lax.axis_index("sec")
    bottom[...] = jnp.where(section > 0, below[0 : bottom.shape[0], :], 0.0)
    top[...] = jnp.where(section < lax.axis_size("sec") - 1, above[0 : top.shape[0], :], 0.0)
    two = 2 * width
    for k in range(comps * depth_z):
        low_out[2 * k : 2 * k + 2, :] = flow[k * width : k * width + 2, :]
    base = 2 * comps * depth_z
    for c in range(comps):
        low_out[base + 2 * c : base + 2 * c + 1, :] = bottom[c * two + width : c * two + width + 1, :]
        low_out[base + 2 * c + 1 : base + 2 * c + 2, :] = top[c * two : c * two + 1, :]
        corner[2 * c : 2 * c + 1, :] = bottom[(c + 1) * two - 1 : (c + 1) * two, :]
        corner[2 * c + 1 : 2 * c + 2, :] = top[c * two + width - 1 : c * two + width, :]
    base += 2 * comps
    for z in range(depth_z):
        low_out[base + z : base + z + 1, :] = viscosity[z * width : z * width + 1, :]


def edges(comps, depth_z, width, flow, viscosity, below, above):
    depth = flow.shape[1]
    shape = jax.ShapeDtypeStruct((2 * comps * (depth_z + 1) + depth_z, depth), jnp.float32)
    small = jax.ShapeDtypeStruct((2 * comps, depth), jnp.float32)
    halo = jax.ShapeDtypeStruct(((2 * comps + 1) * width, depth), jnp.float32)
    return pl.pallas_call(
        functools.partial(edge_kernel, comps, depth_z, width),
        out_shape=(shape, small, halo, halo),
        in_specs=[VM] * 4,
        out_specs=(VM,) * 4,
        compiler_params=pltpu.CompilerParams(vmem_limit_bytes=24 * 1024 * 1024),
        name="edges",
    )(flow, viscosity, below, above)


def inner_kernel(comps, depth_z, width, flow, viscosity, below, above, first, middle):
    two = 2 * width

    def own(z):
        if z < 0:
            return [below[c * two + (2 + z) * width : c * two + (3 + z) * width, :] for c in range(comps)]
        if z >= depth_z:
            return [above[c * two + (z - depth_z) * width : c * two + (z - depth_z + 1) * width, :] for c in range(comps)]
        return [flow[(c * depth_z + z) * width : (c * depth_z + z + 1) * width, :] for c in range(comps)]

    for z in range(-1, depth_z + 1):
        if z < 0:
            visc = below[comps * two :, :]
        elif z == depth_z:
            visc = above[comps * two :, :]
        else:
            visc = viscosity[z * width : (z + 1) * width, :]
        centers, change = tendency(own(z), own(z + 1), own(z - 1), visc, width)
        for c in range(comps):
            first[c, z + 1, 0:width, :] = centers[c] + change[c]

    def second(z, carry):
        plane, upper, lower = ([first[c, z + 1 + d] for c in range(comps)] for d in (0, 1, -1))
        at = pl.multiple_of(z * width, width)
        centers, change = tendency(plane, upper, lower, viscosity[pl.ds(at, width), :], width)
        for c in range(comps):
            spot = pl.multiple_of((c * depth_z + z) * width, width)
            middle[pl.ds(spot, width), :] = 0.5 * flow[pl.ds(spot, width), :] + 0.5 * (centers[c] + change[c])
        return carry

    lax.fori_loop(0, depth_z, second, 0)


def inner(comps, depth_z, width, flow, viscosity, below, above):
    depth = flow.shape[1]
    return pl.pallas_call(
        functools.partial(inner_kernel, comps, depth_z, width),
        out_shape=(
            jax.ShapeDtypeStruct((comps, depth_z + 2, width, depth), jnp.float32),
            jax.ShapeDtypeStruct(flow.shape, jnp.float32),
        ),
        in_specs=[VM] * 4,
        out_specs=(VM, VM),
        compiler_params=pltpu.CompilerParams(vmem_limit_bytes=24 * 1024 * 1024),
        cost_estimate=pl.CostEstimate(flops=10**7, bytes_accessed=2**22, transcendentals=0),
        name="inner",
    )(flow, viscosity, below, above)


def outer_kernel(comps, depth_z, width, flow, viscosity, below, above, first, middle, left, corner, right, inlet, second_out, inlet_now, strip, visc, started, table):
    depth = flow.shape[1]
    two = 2 * width
    rows = depth_z * width
    total = comps * rows
    base = 2 * comps * depth_z
    strip[...] = jnp.zeros_like(strip)
    visc[...] = jnp.zeros_like(visc)
    for c in range(comps):
        for z in range(-2, depth_z + 2):
            if z < 0:
                ref, spot = below, c * two + (2 + z) * width
            elif z >= depth_z:
                ref, spot = above, c * two + (z - depth_z) * width
            else:
                ref, spot = flow, (c * depth_z + z) * width
            strip[c, z + 2, 2:4, :] = ref[spot : spot + 2, :]
            strip[c, z + 2, 4:6, :] = ref[spot + width - 2 : spot + width, :]
            if 0 <= z < depth_z:
                k = 2 * (c * depth_z + z)
                strip[c, z + 2, 0:2, :] = left[k : k + 2, :]
                strip[c, z + 2, 6:8, :] = right[k : k + 2, :]
            elif z in (-1, depth_z):
                k = base + 2 * c + (z == depth_z)
                j = k - base
                strip[c, z + 2, 1:2, :] = corner[j : j + 1, :]
                strip[c, z + 2, 6:7, :] = right[k : k + 1, :]
    side = base + 2 * comps
    for z in range(-1, depth_z + 1):
        if z < 0:
            ref, spot = below, comps * two
        elif z == depth_z:
            ref, spot = above, comps * two
        else:
            ref, spot = viscosity, z * width
            visc[z + 1, 1:2, :] = left[base + z : base + z + 1, :]
            visc[z + 1, 6:7, :] = right[side + z : side + z + 1, :]
        visc[z + 1, 2:4, :] = ref[spot : spot + 2, :]
        visc[z + 1, 4:6, :] = ref[spot + width - 2 : spot + width, :]

    place = lax.broadcasted_iota(jnp.int32, (8, 1), 0)

    def apart(value):
        return jnp.where(place < 4, pltpu.roll(value, 7, 0), pltpu.roll(value, 1, 0))

    def one(z, carry):
        plane, upper, lower = ([strip[c, z + 1 + d] for c in range(comps)] for d in (0, 1, -1))
        centers, change = tendency(plane, upper, lower, visc[z], 8)
        for c in range(comps):
            ends = apart(centers[c] + change[c])
            near = jnp.where(place < 4, pltpu.roll(first[c, z, 0:8, :], 1, 0), pltpu.roll(first[c, z, width - 8 : width, :], 7, 0))
            started[c, z] = jnp.where((place < 2) | (place > 5), ends, near)
        return carry

    lax.fori_loop(0, depth_z + 2, one, 0, unroll=2)

    def second(z, carry):
        plane, upper, lower = ([started[c, z + 1 + d] for c in range(comps)] for d in (0, 1, -1))
        centers, change = tendency(plane, upper, lower, apart(visc[z + 1]), 8)
        for c in range(comps):
            spot = pl.multiple_of((c * depth_z + z) * width, width)
            edge = 0.5 * apart(strip[c, z + 2]) + 0.5 * (centers[c] + change[c])
            mine = middle[pl.ds(spot, width), :]
            top = jnp.where(place < 2, pltpu.roll(edge, 7, 0), mine[0:8])
            end = jnp.where(place > 5, pltpu.roll(edge, 1, 0), mine[width - 8 :])
            value = jnp.concatenate([top, mine[8 : width - 8], end] if width > 16 else [top, end], axis=0)
            second_out[pl.ds(spot, width), :] = value
            high, low = halves(value)
            table[pl.ds(spot, width), :] = high
            table[pl.ds(total + spot, width), :] = low
        return carry

    lax.fori_loop(0, depth_z, second, 0, unroll=2)

    cells = inlet[0:1, :]
    picked = jnp.dot(table[...], column_hot(cells, depth), preferred_element_type=jnp.float32)
    row = lax.broadcasted_iota(jnp.int32, (rows, cells.shape[1]), 0) == (cells >> (depth.bit_length() - 1))
    for c in range(comps):
        both = picked[c * rows : (c + 1) * rows] + picked[total + c * rows : total + (c + 1) * rows]
        inlet_now[c : c + 1, :] = jnp.sum(jnp.where(row, both, 0.0), axis=0, keepdims=True)


def outer(comps, depth_z, width, flow, viscosity, below, above, first, middle, left, corner, right, inlet):
    depth = flow.shape[1]
    return pl.pallas_call(
        functools.partial(outer_kernel, comps, depth_z, width),
        out_shape=(
            jax.ShapeDtypeStruct(flow.shape, jnp.float32),
            jax.ShapeDtypeStruct((comps, inlet.shape[1]), jnp.float32),
        ),
        in_specs=[VM] * 10,
        out_specs=(VM, VM),
        scratch_shapes=[
            pltpu.VMEM((comps, depth_z + 4, 8, depth), jnp.float32),
            pltpu.VMEM((depth_z + 2, 8, depth), jnp.float32),
            pltpu.VMEM((comps, depth_z + 2, 8, depth), jnp.float32),
            pltpu.VMEM((2 * flow.shape[0], depth), jnp.bfloat16),
        ],
        compiler_params=pltpu.CompilerParams(vmem_limit_bytes=24 * 1024 * 1024),
        cost_estimate=pl.CostEstimate(flops=10**7, bytes_accessed=2**22, transcendentals=0),
        name="outer",
    )(flow, viscosity, below, above, first, middle, left, corner, right, inlet)


def on_device(
    flow_field,
    viscosity,
    port_plane,
    port_match,
    inlet_cell,
    inclusion_state,
    response_rate,
    inclusion_mass,
    anchor_cell,
    live_counts,
    arrival_cell,
):
    comps, depth_z, width, depth = flow_field.shape
    partners, cap = anchor_cell.shape[2:]
    sizes = (comps, depth_z, width)
    flow = flow_field.reshape(-1, depth)
    visc = viscosity.reshape(-1, depth)
    count = lax.axis_size("tile")
    forth = [(i, i + 1) for i in range(count - 1)]
    back = [(i + 1, i) for i in range(count - 1)]
    levels = lax.axis_size("sec")
    up = [(i, (i + 1) % levels) for i in range(levels)]
    down = [((i + 1) % levels, i) for i in range(levels)]
    over = [(i, (i + levels // 2) % levels) for i in range(levels)]

    high_edge, low_cap, high_cap = rims(*sizes, flow, visc, port_plane)
    left = lax.ppermute(high_edge, "tile", forth)
    below = lax.ppermute(high_cap, "sec", up)
    above = lax.ppermute(low_cap, "sec", down)
    across = lax.ppermute(port_plane, "sec", over)
    counts = live_counts.reshape(-1)
    counts, low_cap, high_cap = lax.optimization_barrier((counts, low_cap, high_cap))
    sampled = sample(comps, counts, flow, anchor_cell.reshape(partners, cap))
    outgoing = slip(
        counts,
        sampled,
        inclusion_state.reshape(comps, partners, cap),
        response_rate.reshape(partners, cap),
        inclusion_mass.reshape(partners, cap),
        port_plane,
        above,
        across,
        below,
    )
    left, below, above, outgoing = lax.optimization_barrier((left, below, above, outgoing))
    arrived = lax.all_to_all(outgoing, "tile", split_axis=0, concat_axis=0, tiled=True)
    low_edge, corner, bottom, top = edges(*sizes, flow, visc, below, above)
    right = lax.ppermute(low_edge, "tile", back)
    corner = lax.ppermute(corner, "tile", forth)
    inlet = jnp.pad(inlet_cell.reshape(1, -1), ((0, 0), (0, cap - inlet_cell.shape[0])))
    first, middle = inner(*sizes, flow, visc, bottom, top)
    second, inlet_now = outer(*sizes, flow, visc, bottom, top, first, middle, left, corner, right, inlet)
    flow_next, arrived_state = land(
        port_match, second, inlet_now, inlet, arrival_cell.reshape(partners, cap), arrived
    )
    return flow_next.reshape(flow_field.shape), arrived_state.reshape(inclusion_state.shape)


def solution(mesh):
    return jax.shard_map(
        on_device,
        mesh=mesh,
        in_specs=(
            P(None, "sec", "tile", None),
            P("sec", "tile", None),
            P(None, ("sec", "tile")),
            P(("sec", "tile")),
            P(("sec", "tile")),
            P(None, "sec", "tile", None, None),
            P("sec", "tile", None, None),
            P("sec", "tile", None, None),
            P("sec", "tile", None, None),
            P("sec", "tile", None),
            P("sec", "tile", None, None),
        ),
        out_specs=(P(None, "sec", "tile", None), P(None, "sec", "tile", None, None)),
        check_vma=False,
    )
```

```python
import functools

import jax
import jax.numpy as jnp
from jax import lax
from jax.experimental import pallas as pl
from jax.experimental.pallas import tpu as pltpu
from jax.sharding import PartitionSpec as P

VM = pl.BlockSpec(memory_space=pltpu.VMEM)
SM = pl.BlockSpec(memory_space=pltpu.SMEM)
HB = pl.BlockSpec(memory_space=pltpu.HBM)


def halves(value):
    high = value.astype(jnp.bfloat16)
    low = (value - high.astype(jnp.float32)).astype(jnp.bfloat16)
    return high, low


def column_hot(cells, depth):
    at = lax.broadcasted_iota(jnp.int32, (depth, cells.shape[1]), 0)
    return jnp.where(at == (cells & (depth - 1)), 1.0, 0.0).astype(jnp.bfloat16)


def sample_kernel(GP, counts, flow, anchor, sampled, table, packed):
    partners, cap = anchor.shape
    total, depth = flow.shape
    comps = sampled.shape[1]
    rows = total // comps
    shift = depth.bit_length() - 1
    cap_shift = cap.bit_length() - 1
    lane = lax.broadcasted_iota(jnp.int32, (1, cap), 1)
    packed[...] = jnp.zeros_like(packed)

    def pack(p, base):
        begin = base & (cap - 1)
        spot = base >> cap_shift
        turned = pltpu.roll(anchor[pl.ds(p, 1), :], begin, 1)
        pltpu.store(packed.at[pl.ds(spot, 1), :], turned, mask=lane >= begin)
        pltpu.store(packed.at[pl.ds(spot + 1, 1), :], turned, mask=lane < begin)
        return base + counts[p]

    used = lax.fori_loop(0, partners, pack, 0, unroll=8)
    high, low = halves(flow[...])
    table[0:total] = high
    table[total:] = low

    def group(g, carry):
        first = g * GP
        cells = jnp.concatenate([packed[pl.ds(first + i, 1), :] for i in range(GP)], axis=1)
        hot = column_hot(cells, depth)
        picked = jnp.dot(table[...], hot, preferred_element_type=jnp.float32)
        row = lax.broadcasted_iota(jnp.int32, (rows, cells.shape[1]), 0) == (cells >> shift)
        parts = []
        for c in range(comps):
            both = picked[c * rows : (c + 1) * rows] + picked[total + c * rows : total + (c + 1) * rows]
            parts.append(jnp.sum(jnp.where(row, both, 0.0), axis=0, keepdims=True))
        found = jnp.concatenate(parts, axis=0)
        for i in range(GP):
            sampled[first + i] = found[:, i * cap : (i + 1) * cap]
        return carry

    lax.fori_loop(0, (used + GP * cap - 1) // (GP * cap), group, 0)


def sample(comps, counts, flow, anchor, GP=4):
    partners, cap = anchor.shape
    return pl.pallas_call(
        functools.partial(sample_kernel, GP),
        out_shape=jax.ShapeDtypeStruct((partners + 8, comps, cap), jnp.float32),
        in_specs=[SM, VM, VM],
        out_specs=VM,
        scratch_shapes=[
            pltpu.VMEM((2 * flow.shape[0], flow.shape[1]), jnp.bfloat16),
            pltpu.VMEM((partners + 8, cap), jnp.int32),
        ],
        compiler_params=pltpu.CompilerParams(vmem_limit_bytes=24 * 1024 * 1024),
        cost_estimate=pl.CostEstimate(flops=2 * 8192 * 512 * 1024, bytes_accessed=2**21, transcendentals=0),
        name="sample",
    )(counts, flow, anchor)


chunks = 4


def slip_kernel(counts, sampled, state, rate, mass, ports, above, across, below, wrapped, far, out, whole, out_sems):
    comps, partners, cap = state.shape
    per = ports.shape[1]
    cap_shift = cap.bit_length() - 1
    last = above.shape[0] - 8
    lane = lax.broadcasted_iota(jnp.int32, (1, cap), 1)
    whole[:, 0:per] = ports[...]
    section = lax.axis_index("sec")
    top = lax.axis_size("sec") - 1
    whole[:, per : 2 * per] = jnp.where(section < top, above[last : last + comps, 0:per], wrapped[...])
    whole[:, 2 * per : 3 * per] = across[...]
    whole[:, 3 * per :] = jnp.where(section > 0, below[last : last + comps, 0:per], wrapped[...])

    def finish(p, base):
        n = counts[p]
        begin = base & (cap - 1)
        spot = base >> cap_shift
        both = jnp.where(lane >= begin, sampled[spot], sampled[spot + 1])
        value = pltpu.roll(both, (cap - begin) & (cap - 1), 1)
        own = jnp.concatenate([state[c, pl.ds(p, 1), :] for c in range(comps)], axis=0)
        r = rate[pl.ds(p, 1), :]
        drop = r * (own - value)
        live = lane < n
        out[3 * p] = jnp.where(live, own - drop, 0.0)
        out[3 * p + 1] = jnp.where(live, mass[pl.ds(p, 1), :] * drop, 0.0)
        out[3 * p + 2] = whole[...]
        return base + n

    block = partners // chunks
    base = 0
    copies = []
    for i in range(chunks):
        base = lax.fori_loop(i * block, (i + 1) * block, finish, base, unroll=8)
        part = pl.ds(3 * i * block, 3 * block)
        copies.append(pltpu.make_async_copy(out.at[part], far.at[part], out_sems.at[i]))
        copies[i].start()
    for copy in copies:
        copy.wait()


def slip(counts, sampled, state, rate, mass, ports, above, across, below, wrapped):
    comps, partners, cap = state.shape
    return pl.pallas_call(
        slip_kernel,
        out_shape=jax.ShapeDtypeStruct((partners * 3, comps, cap), jnp.float32),
        in_specs=[SM] + [VM] * 9,
        out_specs=HB,
        scratch_shapes=[
            pltpu.VMEM((partners * 3, comps, cap), jnp.float32),
            pltpu.VMEM((comps, cap), jnp.float32),
            pltpu.SemaphoreType.DMA((chunks,)),
        ],
        compiler_params=pltpu.CompilerParams(vmem_limit_bytes=24 * 1024 * 1024),
        cost_estimate=pl.CostEstimate(flops=2 * 10**6, bytes_accessed=2**20, transcendentals=0),
        name="slip",
    )(counts, sampled, state, rate, mass, ports, above, across, below, wrapped)


def land_kernel(GP, match, second, inlet_now, inlet, arrival, arrived, flow_far, state_far, flow_out, state_out, last_ref, last, packed, sem, out_sems):
    comps, partners, cap = state_out.shape
    total, depth = second.shape
    rows = total // comps
    shift = depth.bit_length() - 1
    cap_shift = cap.bit_length() - 1
    entries = match.shape[0]
    per = entries
    nt = (((1,), (1,)), ((), ()))
    slot = lax.broadcasted_iota(jnp.int32, (1, cap), 1)

    def ends(p, carry):
        moved = arrived[3 * p]
        gift = arrived[3 * p + 1]
        for c in range(comps):
            state_out[c, pl.ds(p, 1), :] = moved[c : c + 1]
        biggest = jnp.max(jnp.abs(gift), axis=0, keepdims=True)
        last_ref[pl.ds(p, 1), :] = jnp.where(biggest > 0.0, slot + 1, 0)
        return carry

    lax.fori_loop(0, partners, ends, 0, unroll=8)
    last_ref[partners:, :] = jnp.zeros_like(last_ref[partners:, :])
    top = jnp.max(last_ref[...].T, axis=0, keepdims=True)
    last_ref[0:1, :] = top
    fetch = pltpu.make_async_copy(last_ref.at[0:1, :], last, sem)
    fetch.start()
    state_copy = pltpu.make_async_copy(state_out, state_far, out_sems.at[2])
    state_copy.start()
    flow_out[...] = second[...]

    def add(cells, values, spot):
        row = lax.broadcasted_iota(jnp.int32, (rows, cells.shape[1]), 0) == (cells >> shift)
        high, low = halves(values)
        parts = []
        for part in (high.astype(jnp.float32), low.astype(jnp.float32)):
            for c in range(values.shape[0]):
                parts.append(jnp.where(row, part[c : c + 1], 0.0).astype(jnp.bfloat16))
        both = lax.dot_general(
            jnp.concatenate(parts, axis=0), column_hot(cells, depth), nt, preferred_element_type=jnp.float32
        )
        half = values.shape[0] * rows
        flow_out[spot : spot + half, :] += both[:half] + both[half:]

    section = lax.axis_index("sec")
    sections = cap // per
    target = jnp.zeros((comps, cap), jnp.float32)
    for k in range(entries):
        port = match[k]
        device = port // entries
        place = (device // partners + sections - section) % sections * per + port % entries
        turned = pltpu.roll(arrived[3 * (device % partners) + 2], (k + cap - place) % cap, 1)
        target = jnp.where(slot == k, turned, target)
    change = jnp.where(slot < entries, 0.5 * (target - inlet_now[...]), 0.0)
    packed[...] = jnp.zeros_like(packed)
    fetch.wait()

    def pack(p, base):
        begin = base & (cap - 1)
        spot = base >> cap_shift
        cells = arrival[pl.ds(p, 1), :].astype(jnp.float32)
        both = jnp.concatenate([arrived[3 * p + 1], jnp.broadcast_to(cells, (8 - comps, cap))], axis=0)
        turned = pltpu.roll(both, begin, 1)
        wide = lax.broadcasted_iota(jnp.int32, (8, cap), 1)
        pltpu.store(packed.at[spot], turned, mask=wide >= begin)
        pltpu.store(packed.at[spot + 1], turned, mask=wide < begin)
        return base + last[0, p]

    used = lax.fori_loop(0, partners, pack, 0, unroll=8)

    spare = (used + cap - 1) >> cap_shift
    cells = jnp.broadcast_to(inlet[0:1, :].astype(jnp.float32), (8 - comps, cap))
    packed[spare] = jnp.concatenate([change, cells], axis=0)

    def load(g):
        both = jnp.concatenate([packed[g * GP + i] for i in range(GP)], axis=1)
        return both[comps : comps + 1].astype(jnp.int32), both[:comps]

    def group(g, carry):
        cells, values = load(g)
        add(cells, values, 0)
        return carry

    final = spare // GP
    lax.fori_loop(0, final, group, 0)
    cells, values = load(final)
    half = comps // 2
    copies = []
    for i in range(2):
        part = pl.ds(i * half * rows, half * rows)
        add(cells, values[i * half : (i + 1) * half], i * half * rows)
        copies.append(pltpu.make_async_copy(flow_out.at[part, :], flow_far.at[part, :], out_sems.at[i]))
        copies[i].start()
    for copy in copies:
        copy.wait()
    state_copy.wait()


def land(match, second, inlet_now, inlet, arrival, arrived, GP=4):
    partners, cap = arrival.shape
    comps = arrived.shape[1]
    return pl.pallas_call(
        functools.partial(land_kernel, GP),
        out_shape=(
            jax.ShapeDtypeStruct(second.shape, jnp.float32),
            jax.ShapeDtypeStruct((comps, partners, cap), jnp.float32),
        ),
        in_specs=[SM] + [VM] * 5,
        out_specs=(HB, HB),
        scratch_shapes=[
            pltpu.VMEM(second.shape, jnp.float32),
            pltpu.VMEM((comps, partners, cap), jnp.float32),
            pltpu.VMEM((cap, cap), jnp.int32),
            pltpu.SMEM((1, cap), jnp.int32),
            pltpu.VMEM((partners + 8, 8, cap), jnp.float32),
            pltpu.SemaphoreType.DMA,
            pltpu.SemaphoreType.DMA((3,)),
        ],
        compiler_params=pltpu.CompilerParams(vmem_limit_bytes=24 * 1024 * 1024),
        cost_estimate=pl.CostEstimate(flops=2 * 8192 * 512 * 1024, bytes_accessed=2**21, transcendentals=0),
        name="land",
    )(match, second, inlet_now, inlet, arrival, arrived)


def tendency(plane, upper, lower, viscosity, keep):
    place = lax.broadcasted_iota(jnp.int32, (1, viscosity.shape[1]), 1)
    depth = viscosity.shape[1]
    centers, laps, dz, dx, dy = [], [], [], [], []
    for c in range(len(plane)):
        whole = plane[c]
        center = whole[:keep]
        up_x = pltpu.roll(whole, whole.shape[0] - 1, 0)[:keep]
        low_x = pltpu.roll(whole, 1, 0)[:keep]
        up_y = jnp.where(place == depth - 1, 0.0, pltpu.roll(center, depth - 1, 1))
        low_y = jnp.where(place == 0, 0.0, pltpu.roll(center, 1, 1))
        centers.append(center)
        laps.append((upper[c] + lower[c]) + (up_x + low_x) + (up_y + low_y) - 6.0 * center)
        dz.append(upper[c] - lower[c])
        dx.append(up_x - low_x)
        dy.append(up_y - low_y)
    strain = sum(d[c] * d[c] for c in range(3) for d in (dz, dx, dy)) * 0.25
    eddy = viscosity * (1.0 + strain / (1.0 + strain))
    out = []
    for c in range(len(plane)):
        carried = centers[0] * dz[c] + centers[1] * dx[c] + centers[2] * dy[c]
        out.append(0.5 * (eddy * laps[c]) - 0.25 * carried)
    return centers, out


def cap_kernel(comps, depth_z, width, flow, viscosity, ports, low_cap, high_cap):
    two = 2 * width
    last = depth_z * width
    for c in range(comps):
        low_cap[c * two : (c + 1) * two, :] = flow[c * last : c * last + two, :]
        high_cap[c * two : (c + 1) * two, :] = flow[(c + 1) * last - two : (c + 1) * last, :]
    base = comps * two
    low_cap[base : base + width, :] = viscosity[0:width, :]
    high_cap[base : base + width, :] = viscosity[last - width : last, :]
    for out in (low_cap, high_cap):
        out[base + width :, :] = jnp.zeros((8, out.shape[1]), jnp.float32)
        out[base + width : base + width + comps, 0 : ports.shape[1]] = ports[...]


def caps(comps, depth_z, width, flow, viscosity, ports):
    depth = flow.shape[1]
    cap = jax.ShapeDtypeStruct((2 * comps * width + width + 8, depth), jnp.float32)
    return pl.pallas_call(
        functools.partial(cap_kernel, comps, depth_z, width),
        out_shape=(cap, cap),
        in_specs=[VM] * 3,
        out_specs=(VM, VM),
        compiler_params=pltpu.CompilerParams(vmem_limit_bytes=60 * 1024 * 1024),
        name="caps",
    )(flow, viscosity, ports)


def edge_kernel(comps, depth_z, width, flow, viscosity, below, above, low_out, high_out):
    two = 2 * width
    for k in range(comps * depth_z):
        low_out[2 * k : 2 * k + 2, :] = flow[k * width : k * width + 2, :]
        high_out[2 * k : 2 * k + 2, :] = flow[(k + 1) * width - 2 : (k + 1) * width, :]
    base = 2 * comps * depth_z
    for c in range(comps):
        low_out[base + 2 * c : base + 2 * c + 1, :] = below[c * two + width : c * two + width + 1, :]
        low_out[base + 2 * c + 1 : base + 2 * c + 2, :] = above[c * two : c * two + 1, :]
        high_out[base + 2 * c : base + 2 * c + 1, :] = below[(c + 1) * two - 1 : (c + 1) * two, :]
        high_out[base + 2 * c + 1 : base + 2 * c + 2, :] = above[c * two + width - 1 : c * two + width, :]
    base += 2 * comps
    for z in range(depth_z):
        low_out[base + z : base + z + 1, :] = viscosity[z * width : z * width + 1, :]
        high_out[base + z : base + z + 1, :] = viscosity[(z + 1) * width - 1 : (z + 1) * width, :]


def edges(comps, depth_z, width, flow, viscosity, below, above):
    depth = flow.shape[1]
    shape = jax.ShapeDtypeStruct((2 * comps * (depth_z + 1) + depth_z, depth), jnp.float32)
    return pl.pallas_call(
        functools.partial(edge_kernel, comps, depth_z, width),
        out_shape=(shape, shape),
        in_specs=[VM] * 4,
        out_specs=(VM, VM),
        compiler_params=pltpu.CompilerParams(vmem_limit_bytes=24 * 1024 * 1024),
        name="edges",
    )(flow, viscosity, below, above)


def inner_kernel(comps, depth_z, width, flow, viscosity, below, above, first, middle):
    two = 2 * width

    def own(z):
        if z < 0:
            return [below[c * two + (2 + z) * width : c * two + (3 + z) * width, :] for c in range(comps)]
        if z >= depth_z:
            return [above[c * two + (z - depth_z) * width : c * two + (z - depth_z + 1) * width, :] for c in range(comps)]
        return [flow[(c * depth_z + z) * width : (c * depth_z + z + 1) * width, :] for c in range(comps)]

    for z in range(-1, depth_z + 1):
        if z < 0:
            visc = below[comps * two : comps * two + width, :]
        elif z == depth_z:
            visc = above[comps * two : comps * two + width, :]
        else:
            visc = viscosity[z * width : (z + 1) * width, :]
        centers, change = tendency(own(z), own(z + 1), own(z - 1), visc, width)
        for c in range(comps):
            first[c, z + 1, 0:width, :] = centers[c] + change[c]

    def second(z, carry):
        plane, upper, lower = ([first[c, z + 1 + d] for c in range(comps)] for d in (0, 1, -1))
        at = pl.multiple_of(z * width, width)
        centers, change = tendency(plane, upper, lower, viscosity[pl.ds(at, width), :], width)
        for c in range(comps):
            spot = pl.multiple_of((c * depth_z + z) * width, width)
            middle[pl.ds(spot, width), :] = 0.5 * flow[pl.ds(spot, width), :] + 0.5 * (centers[c] + change[c])
        return carry

    lax.fori_loop(0, depth_z, second, 0)


def inner(comps, depth_z, width, flow, viscosity, below, above):
    depth = flow.shape[1]
    return pl.pallas_call(
        functools.partial(inner_kernel, comps, depth_z, width),
        out_shape=(
            jax.ShapeDtypeStruct((comps, depth_z + 2, width, depth), jnp.float32),
            jax.ShapeDtypeStruct(flow.shape, jnp.float32),
        ),
        in_specs=[VM] * 4,
        out_specs=(VM, VM),
        compiler_params=pltpu.CompilerParams(vmem_limit_bytes=24 * 1024 * 1024),
        cost_estimate=pl.CostEstimate(flops=10**7, bytes_accessed=2**22, transcendentals=0),
        name="inner",
    )(flow, viscosity, below, above)


def outer_kernel(comps, depth_z, width, flow, viscosity, below, above, first, middle, left, right, inlet, second_out, inlet_now, strip, visc, started, table):
    depth = flow.shape[1]
    two = 2 * width
    rows = depth_z * width
    total = comps * rows
    base = 2 * comps * depth_z
    strip[...] = jnp.zeros_like(strip)
    visc[...] = jnp.zeros_like(visc)
    for c in range(comps):
        for z in range(-2, depth_z + 2):
            if z < 0:
                ref, spot = below, c * two + (2 + z) * width
            elif z >= depth_z:
                ref, spot = above, c * two + (z - depth_z) * width
            else:
                ref, spot = flow, (c * depth_z + z) * width
            strip[c, z + 2, 2:4, :] = ref[spot : spot + 2, :]
            strip[c, z + 2, 4:6, :] = ref[spot + width - 2 : spot + width, :]
            if 0 <= z < depth_z:
                k = 2 * (c * depth_z + z)
                strip[c, z + 2, 0:2, :] = left[k : k + 2, :]
                strip[c, z + 2, 6:8, :] = right[k : k + 2, :]
            elif z in (-1, depth_z):
                k = base + 2 * c + (z == depth_z)
                strip[c, z + 2, 1:2, :] = left[k : k + 1, :]
                strip[c, z + 2, 6:7, :] = right[k : k + 1, :]
    side = base + 2 * comps
    for z in range(-1, depth_z + 1):
        if z < 0:
            ref, spot = below, comps * two
        elif z == depth_z:
            ref, spot = above, comps * two
        else:
            ref, spot = viscosity, z * width
            visc[z + 1, 1:2, :] = left[side + z : side + z + 1, :]
            visc[z + 1, 6:7, :] = right[side + z : side + z + 1, :]
        visc[z + 1, 2:4, :] = ref[spot : spot + 2, :]
        visc[z + 1, 4:6, :] = ref[spot + width - 2 : spot + width, :]

    place = lax.broadcasted_iota(jnp.int32, (8, 1), 0)

    def apart(value):
        return jnp.where(place < 4, pltpu.roll(value, 7, 0), pltpu.roll(value, 1, 0))

    def one(z, carry):
        plane, upper, lower = ([strip[c, z + 1 + d] for c in range(comps)] for d in (0, 1, -1))
        centers, change = tendency(plane, upper, lower, visc[z], 8)
        for c in range(comps):
            ends = apart(centers[c] + change[c])
            near = jnp.where(place < 4, pltpu.roll(first[c, z, 0:8, :], 1, 0), pltpu.roll(first[c, z, width - 8 : width, :], 7, 0))
            started[c, z] = jnp.where((place < 2) | (place > 5), ends, near)
        return carry

    lax.fori_loop(0, depth_z + 2, one, 0, unroll=2)

    def second(z, carry):
        plane, upper, lower = ([started[c, z + 1 + d] for c in range(comps)] for d in (0, 1, -1))
        centers, change = tendency(plane, upper, lower, apart(visc[z + 1]), 8)
        for c in range(comps):
            spot = pl.multiple_of((c * depth_z + z) * width, width)
            edge = 0.5 * apart(strip[c, z + 2]) + 0.5 * (centers[c] + change[c])
            mine = middle[pl.ds(spot, width), :]
            top = jnp.where(place < 2, pltpu.roll(edge, 7, 0), mine[0:8])
            end = jnp.where(place > 5, pltpu.roll(edge, 1, 0), mine[width - 8 :])
            value = jnp.concatenate([top, mine[8 : width - 8], end] if width > 16 else [top, end], axis=0)
            second_out[pl.ds(spot, width), :] = value
            high, low = halves(value)
            table[pl.ds(spot, width), :] = high
            table[pl.ds(total + spot, width), :] = low
        return carry

    lax.fori_loop(0, depth_z, second, 0, unroll=2)

    cells = inlet[0:1, :]
    picked = jnp.dot(table[...], column_hot(cells, depth), preferred_element_type=jnp.float32)
    row = lax.broadcasted_iota(jnp.int32, (rows, cells.shape[1]), 0) == (cells >> (depth.bit_length() - 1))
    for c in range(comps):
        both = picked[c * rows : (c + 1) * rows] + picked[total + c * rows : total + (c + 1) * rows]
        inlet_now[c : c + 1, :] = jnp.sum(jnp.where(row, both, 0.0), axis=0, keepdims=True)


def outer(comps, depth_z, width, flow, viscosity, below, above, first, middle, left, right, inlet):
    depth = flow.shape[1]
    return pl.pallas_call(
        functools.partial(outer_kernel, comps, depth_z, width),
        out_shape=(
            jax.ShapeDtypeStruct(flow.shape, jnp.float32),
            jax.ShapeDtypeStruct((comps, inlet.shape[1]), jnp.float32),
        ),
        in_specs=[VM] * 9,
        out_specs=(VM, VM),
        scratch_shapes=[
            pltpu.VMEM((comps, depth_z + 4, 8, depth), jnp.float32),
            pltpu.VMEM((depth_z + 2, 8, depth), jnp.float32),
            pltpu.VMEM((comps, depth_z + 2, 8, depth), jnp.float32),
            pltpu.VMEM((2 * flow.shape[0], depth), jnp.bfloat16),
        ],
        compiler_params=pltpu.CompilerParams(vmem_limit_bytes=24 * 1024 * 1024),
        cost_estimate=pl.CostEstimate(flops=10**7, bytes_accessed=2**22, transcendentals=0),
        name="outer",
    )(flow, viscosity, below, above, first, middle, left, right, inlet)


def on_device(
    flow_field,
    viscosity,
    port_plane,
    port_match,
    inlet_cell,
    inclusion_state,
    response_rate,
    inclusion_mass,
    anchor_cell,
    live_counts,
    arrival_cell,
):
    comps, depth_z, width, depth = flow_field.shape
    partners, cap = anchor_cell.shape[2:]
    sizes = (comps, depth_z, width)
    flow = flow_field.reshape(-1, depth)
    visc = viscosity.reshape(-1, depth)
    count = lax.axis_size("tile")
    forth = [(i, i + 1) for i in range(count - 1)]
    back = [(i + 1, i) for i in range(count - 1)]
    levels = lax.axis_size("sec")
    up = [(i, i + 1) for i in range(levels - 1)]
    down = [(i + 1, i) for i in range(levels - 1)]
    over = [(i, (i + levels // 2) % levels) for i in range(levels)]

    low_cap, high_cap = caps(*sizes, flow, visc, port_plane)
    below = lax.ppermute(high_cap, "sec", up)
    above = lax.ppermute(low_cap, "sec", down)
    across = lax.ppermute(port_plane, "sec", over)
    wrapped = lax.ppermute(port_plane, "sec", [(0, levels - 1), (levels - 1, 0)])
    counts = live_counts.reshape(-1)
    counts, low_cap, high_cap = lax.optimization_barrier((counts, low_cap, high_cap))
    sampled = sample(comps, counts, flow, anchor_cell.reshape(partners, cap))
    outgoing = slip(
        counts,
        sampled,
        inclusion_state.reshape(comps, partners, cap),
        response_rate.reshape(partners, cap),
        inclusion_mass.reshape(partners, cap),
        port_plane,
        above,
        across,
        below,
        wrapped,
    )
    below, above, outgoing = lax.optimization_barrier((below, above, outgoing))
    arrived = lax.all_to_all(outgoing, "tile", split_axis=0, concat_axis=0, tiled=True)
    low_edge, high_edge = edges(*sizes, flow, visc, below, above)
    left = lax.ppermute(high_edge, "tile", forth)
    right = lax.ppermute(low_edge, "tile", back)
    inlet = jnp.pad(inlet_cell.reshape(1, -1), ((0, 0), (0, cap - inlet_cell.shape[0])))
    first, middle = inner(*sizes, flow, visc, below, above)
    second, inlet_now = outer(*sizes, flow, visc, below, above, first, middle, left, right, inlet)
    flow_next, arrived_state = land(
        port_match, second, inlet_now, inlet, arrival_cell.reshape(partners, cap), arrived
    )
    return flow_next.reshape(flow_field.shape), arrived_state.reshape(inclusion_state.shape)


def solution(mesh):
    return jax.shard_map(
        on_device,
        mesh=mesh,
        in_specs=(
            P(None, "sec", "tile", None),
            P("sec", "tile", None),
            P(None, ("sec", "tile")),
            P(("sec", "tile")),
            P(("sec", "tile")),
            P(None, "sec", "tile", None, None),
            P("sec", "tile", None, None),
            P("sec", "tile", None, None),
            P("sec", "tile", None, None),
            P("sec", "tile", None),
            P("sec", "tile", None, None),
        ),
        out_specs=(P(None, "sec", "tile", None), P(None, "sec", "tile", None, None)),
        check_vma=False,
    )
```

```python
import functools

import jax
import jax.numpy as jnp
from jax import lax
from jax.experimental import pallas as pl
from jax.experimental.pallas import tpu as pltpu
from jax.sharding import PartitionSpec as P

VM = pl.BlockSpec(memory_space=pltpu.VMEM)
SM = pl.BlockSpec(memory_space=pltpu.SMEM)
HB = pl.BlockSpec(memory_space=pltpu.HBM)


def halves(value):
    high = value.astype(jnp.bfloat16)
    low = (value - high.astype(jnp.float32)).astype(jnp.bfloat16)
    return high, low


def column_hot(cells, depth):
    at = lax.broadcasted_iota(jnp.int32, (depth, cells.shape[1]), 0)
    return jnp.where(at == (cells & (depth - 1)), 1.0, 0.0).astype(jnp.bfloat16)


def sample_kernel(GP, counts, flow, anchor, sampled, table, packed):
    partners, cap = anchor.shape
    total, depth = flow.shape
    comps = sampled.shape[1]
    rows = total // comps
    shift = depth.bit_length() - 1
    cap_shift = cap.bit_length() - 1
    lane = lax.broadcasted_iota(jnp.int32, (1, cap), 1)
    packed[...] = jnp.zeros_like(packed)

    def pack(p, base):
        begin = base & (cap - 1)
        spot = base >> cap_shift
        turned = pltpu.roll(anchor[pl.ds(p, 1), :], begin, 1)
        pltpu.store(packed.at[pl.ds(spot, 1), :], turned, mask=lane >= begin)
        pltpu.store(packed.at[pl.ds(spot + 1, 1), :], turned, mask=lane < begin)
        return base + counts[p]

    used = lax.fori_loop(0, partners, pack, 0, unroll=8)
    high, low = halves(flow[...])
    table[0:total] = high
    table[total:] = low

    def group(g, carry):
        first = g * GP
        cells = jnp.concatenate([packed[pl.ds(first + i, 1), :] for i in range(GP)], axis=1)
        hot = column_hot(cells, depth)
        picked = jnp.dot(table[...], hot, preferred_element_type=jnp.float32)
        row = lax.broadcasted_iota(jnp.int32, (rows, cells.shape[1]), 0) == (cells >> shift)
        parts = []
        for c in range(comps):
            both = picked[c * rows : (c + 1) * rows] + picked[total + c * rows : total + (c + 1) * rows]
            parts.append(jnp.sum(jnp.where(row, both, 0.0), axis=0, keepdims=True))
        found = jnp.concatenate(parts, axis=0)
        for i in range(GP):
            sampled[first + i] = found[:, i * cap : (i + 1) * cap]
        return carry

    lax.fori_loop(0, (used + GP * cap - 1) // (GP * cap), group, 0)


def sample(comps, counts, flow, anchor, GP=4):
    partners, cap = anchor.shape
    return pl.pallas_call(
        functools.partial(sample_kernel, GP),
        out_shape=jax.ShapeDtypeStruct((partners + 8, comps, cap), jnp.float32),
        in_specs=[SM, VM, VM],
        out_specs=VM,
        scratch_shapes=[
            pltpu.VMEM((2 * flow.shape[0], flow.shape[1]), jnp.bfloat16),
            pltpu.VMEM((partners + 8, cap), jnp.int32),
        ],
        compiler_params=pltpu.CompilerParams(vmem_limit_bytes=24 * 1024 * 1024),
        cost_estimate=pl.CostEstimate(flops=2 * 8192 * 512 * 1024, bytes_accessed=2**21, transcendentals=0),
        name="sample",
    )(counts, flow, anchor)


chunks = 4


def slip_kernel(counts, sampled, state, rate, mass, ports, above, across, below, far, out, whole, out_sems):
    comps, partners, cap = state.shape
    per = ports.shape[1]
    cap_shift = cap.bit_length() - 1
    last = above.shape[0] - 8
    lane = lax.broadcasted_iota(jnp.int32, (1, cap), 1)
    whole[:, 0:per] = ports[...]
    whole[:, per : 2 * per] = above[last : last + comps, 0:per]
    whole[:, 2 * per : 3 * per] = across[...]
    whole[:, 3 * per :] = below[last : last + comps, 0:per]

    def finish(p, base):
        n = counts[p]
        begin = base & (cap - 1)
        spot = base >> cap_shift
        both = jnp.where(lane >= begin, sampled[spot], sampled[spot + 1])
        value = pltpu.roll(both, (cap - begin) & (cap - 1), 1)
        own = jnp.concatenate([state[c, pl.ds(p, 1), :] for c in range(comps)], axis=0)
        r = rate[pl.ds(p, 1), :]
        drop = r * (own - value)
        live = lane < n
        out[3 * p] = jnp.where(live, own - drop, 0.0)
        out[3 * p + 1] = jnp.where(live, mass[pl.ds(p, 1), :] * drop, 0.0)
        out[3 * p + 2] = whole[...]
        return base + n

    block = partners // chunks
    base = 0
    copies = []
    for i in range(chunks):
        base = lax.fori_loop(i * block, (i + 1) * block, finish, base, unroll=8)
        part = pl.ds(3 * i * block, 3 * block)
        copies.append(pltpu.make_async_copy(out.at[part], far.at[part], out_sems.at[i]))
        copies[i].start()
    for copy in copies:
        copy.wait()


def slip(counts, sampled, state, rate, mass, ports, above, across, below):
    comps, partners, cap = state.shape
    return pl.pallas_call(
        slip_kernel,
        out_shape=jax.ShapeDtypeStruct((partners * 3, comps, cap), jnp.float32),
        in_specs=[SM] + [VM] * 8,
        out_specs=HB,
        scratch_shapes=[
            pltpu.VMEM((partners * 3, comps, cap), jnp.float32),
            pltpu.VMEM((comps, cap), jnp.float32),
            pltpu.SemaphoreType.DMA((chunks,)),
        ],
        compiler_params=pltpu.CompilerParams(vmem_limit_bytes=24 * 1024 * 1024),
        cost_estimate=pl.CostEstimate(flops=2 * 10**6, bytes_accessed=2**20, transcendentals=0),
        name="slip",
    )(counts, sampled, state, rate, mass, ports, above, across, below)


def land_kernel(GP, match, second, inlet_now, inlet, arrival, arrived, flow_far, state_far, flow_out, state_out, last_ref, last, packed, sem, out_sems):
    comps, partners, cap = state_out.shape
    total, depth = second.shape
    rows = total // comps
    shift = depth.bit_length() - 1
    cap_shift = cap.bit_length() - 1
    entries = match.shape[0]
    per = entries
    nt = (((1,), (1,)), ((), ()))
    slot = lax.broadcasted_iota(jnp.int32, (1, cap), 1)

    def ends(p, carry):
        moved = arrived[3 * p]
        gift = arrived[3 * p + 1]
        for c in range(comps):
            state_out[c, pl.ds(p, 1), :] = moved[c : c + 1]
        biggest = jnp.max(jnp.abs(gift), axis=0, keepdims=True)
        last_ref[pl.ds(p, 1), :] = jnp.where(biggest > 0.0, slot + 1, 0)
        return carry

    lax.fori_loop(0, partners, ends, 0, unroll=8)
    last_ref[partners:, :] = jnp.zeros_like(last_ref[partners:, :])
    top = jnp.max(last_ref[...].T, axis=0, keepdims=True)
    last_ref[0:1, :] = top
    fetch = pltpu.make_async_copy(last_ref.at[0:1, :], last, sem)
    fetch.start()
    state_copy = pltpu.make_async_copy(state_out, state_far, out_sems.at[2])
    state_copy.start()
    flow_out[...] = second[...]

    def add(cells, values, spot):
        row = lax.broadcasted_iota(jnp.int32, (rows, cells.shape[1]), 0) == (cells >> shift)
        high, low = halves(values)
        parts = []
        for part in (high.astype(jnp.float32), low.astype(jnp.float32)):
            for c in range(values.shape[0]):
                parts.append(jnp.where(row, part[c : c + 1], 0.0).astype(jnp.bfloat16))
        both = lax.dot_general(
            jnp.concatenate(parts, axis=0), column_hot(cells, depth), nt, preferred_element_type=jnp.float32
        )
        half = values.shape[0] * rows
        flow_out[spot : spot + half, :] += both[:half] + both[half:]

    section = lax.axis_index("sec")
    sections = cap // per
    target = jnp.zeros((comps, cap), jnp.float32)
    for k in range(entries):
        port = match[k]
        device = port // entries
        place = (device // partners + sections - section) % sections * per + port % entries
        turned = pltpu.roll(arrived[3 * (device % partners) + 2], (k + cap - place) % cap, 1)
        target = jnp.where(slot == k, turned, target)
    change = jnp.where(slot < entries, 0.5 * (target - inlet_now[...]), 0.0)
    packed[...] = jnp.zeros_like(packed)
    fetch.wait()

    def pack(p, base):
        begin = base & (cap - 1)
        spot = base >> cap_shift
        cells = arrival[pl.ds(p, 1), :].astype(jnp.float32)
        both = jnp.concatenate([arrived[3 * p + 1], jnp.broadcast_to(cells, (8 - comps, cap))], axis=0)
        turned = pltpu.roll(both, begin, 1)
        wide = lax.broadcasted_iota(jnp.int32, (8, cap), 1)
        pltpu.store(packed.at[spot], turned, mask=wide >= begin)
        pltpu.store(packed.at[spot + 1], turned, mask=wide < begin)
        return base + last[0, p]

    used = lax.fori_loop(0, partners, pack, 0, unroll=8)

    spare = (used + cap - 1) >> cap_shift
    cells = jnp.broadcast_to(inlet[0:1, :].astype(jnp.float32), (8 - comps, cap))
    packed[spare] = jnp.concatenate([change, cells], axis=0)

    def load(g):
        both = jnp.concatenate([packed[g * GP + i] for i in range(GP)], axis=1)
        return both[comps : comps + 1].astype(jnp.int32), both[:comps]

    def group(g, carry):
        cells, values = load(g)
        add(cells, values, 0)
        return carry

    final = spare // GP
    lax.fori_loop(0, final, group, 0)
    cells, values = load(final)
    half = comps // 2
    copies = []
    for i in range(2):
        part = pl.ds(i * half * rows, half * rows)
        add(cells, values[i * half : (i + 1) * half], i * half * rows)
        copies.append(pltpu.make_async_copy(flow_out.at[part, :], flow_far.at[part, :], out_sems.at[i]))
        copies[i].start()
    for copy in copies:
        copy.wait()
    state_copy.wait()


def land(match, second, inlet_now, inlet, arrival, arrived, GP=4):
    partners, cap = arrival.shape
    comps = arrived.shape[1]
    return pl.pallas_call(
        functools.partial(land_kernel, GP),
        out_shape=(
            jax.ShapeDtypeStruct(second.shape, jnp.float32),
            jax.ShapeDtypeStruct((comps, partners, cap), jnp.float32),
        ),
        in_specs=[SM] + [VM] * 5,
        out_specs=(HB, HB),
        scratch_shapes=[
            pltpu.VMEM(second.shape, jnp.float32),
            pltpu.VMEM((comps, partners, cap), jnp.float32),
            pltpu.VMEM((cap, cap), jnp.int32),
            pltpu.SMEM((1, cap), jnp.int32),
            pltpu.VMEM((partners + 8, 8, cap), jnp.float32),
            pltpu.SemaphoreType.DMA,
            pltpu.SemaphoreType.DMA((3,)),
        ],
        compiler_params=pltpu.CompilerParams(vmem_limit_bytes=24 * 1024 * 1024),
        cost_estimate=pl.CostEstimate(flops=2 * 8192 * 512 * 1024, bytes_accessed=2**21, transcendentals=0),
        name="land",
    )(match, second, inlet_now, inlet, arrival, arrived)


def tendency(plane, upper, lower, viscosity, keep):
    place = lax.broadcasted_iota(jnp.int32, (1, viscosity.shape[1]), 1)
    depth = viscosity.shape[1]
    centers, laps, dz, dx, dy = [], [], [], [], []
    for c in range(len(plane)):
        whole = plane[c]
        center = whole[:keep]
        up_x = pltpu.roll(whole, whole.shape[0] - 1, 0)[:keep]
        low_x = pltpu.roll(whole, 1, 0)[:keep]
        up_y = jnp.where(place == depth - 1, 0.0, pltpu.roll(center, depth - 1, 1))
        low_y = jnp.where(place == 0, 0.0, pltpu.roll(center, 1, 1))
        centers.append(center)
        laps.append((upper[c] + lower[c]) + (up_x + low_x) + (up_y + low_y) - 6.0 * center)
        dz.append(upper[c] - lower[c])
        dx.append(up_x - low_x)
        dy.append(up_y - low_y)
    strain = sum(d[c] * d[c] for c in range(3) for d in (dz, dx, dy)) * 0.25
    eddy = viscosity * (1.0 + strain / (1.0 + strain))
    out = []
    for c in range(len(plane)):
        carried = centers[0] * dz[c] + centers[1] * dx[c] + centers[2] * dy[c]
        out.append(0.5 * (eddy * laps[c]) - 0.25 * carried)
    return centers, out


def cap_kernel(comps, depth_z, width, flow, viscosity, ports, low_cap, high_cap):
    two = 2 * width
    last = depth_z * width
    for c in range(comps):
        low_cap[c * two : (c + 1) * two, :] = flow[c * last : c * last + two, :]
        high_cap[c * two : (c + 1) * two, :] = flow[(c + 1) * last - two : (c + 1) * last, :]
    base = comps * two
    low_cap[base : base + width, :] = viscosity[0:width, :]
    high_cap[base : base + width, :] = viscosity[last - width : last, :]
    for out in (low_cap, high_cap):
        out[base + width :, :] = jnp.zeros((8, out.shape[1]), jnp.float32)
        out[base + width : base + width + comps, 0 : ports.shape[1]] = ports[...]


def caps(comps, depth_z, width, flow, viscosity, ports):
    depth = flow.shape[1]
    cap = jax.ShapeDtypeStruct((2 * comps * width + width + 8, depth), jnp.float32)
    return pl.pallas_call(
        functools.partial(cap_kernel, comps, depth_z, width),
        out_shape=(cap, cap),
        in_specs=[VM] * 3,
        out_specs=(VM, VM),
        compiler_params=pltpu.CompilerParams(vmem_limit_bytes=60 * 1024 * 1024),
        name="caps",
    )(flow, viscosity, ports)


def edge_kernel(comps, depth_z, width, flow, viscosity, below, above, low_out, high_out, bottom, top):
    section = lax.axis_index("sec")
    bottom[...] = jnp.where(section > 0, below[0 : bottom.shape[0], :], 0.0)
    top[...] = jnp.where(section < lax.axis_size("sec") - 1, above[0 : top.shape[0], :], 0.0)
    two = 2 * width
    for k in range(comps * depth_z):
        low_out[2 * k : 2 * k + 2, :] = flow[k * width : k * width + 2, :]
        high_out[2 * k : 2 * k + 2, :] = flow[(k + 1) * width - 2 : (k + 1) * width, :]
    base = 2 * comps * depth_z
    for c in range(comps):
        low_out[base + 2 * c : base + 2 * c + 1, :] = bottom[c * two + width : c * two + width + 1, :]
        low_out[base + 2 * c + 1 : base + 2 * c + 2, :] = top[c * two : c * two + 1, :]
        high_out[base + 2 * c : base + 2 * c + 1, :] = bottom[(c + 1) * two - 1 : (c + 1) * two, :]
        high_out[base + 2 * c + 1 : base + 2 * c + 2, :] = top[c * two + width - 1 : c * two + width, :]
    base += 2 * comps
    for z in range(depth_z):
        low_out[base + z : base + z + 1, :] = viscosity[z * width : z * width + 1, :]
        high_out[base + z : base + z + 1, :] = viscosity[(z + 1) * width - 1 : (z + 1) * width, :]


def edges(comps, depth_z, width, flow, viscosity, below, above):
    depth = flow.shape[1]
    shape = jax.ShapeDtypeStruct((2 * comps * (depth_z + 1) + depth_z, depth), jnp.float32)
    halo = jax.ShapeDtypeStruct(((2 * comps + 1) * width, depth), jnp.float32)
    return pl.pallas_call(
        functools.partial(edge_kernel, comps, depth_z, width),
        out_shape=(shape, shape, halo, halo),
        in_specs=[VM] * 4,
        out_specs=(VM,) * 4,
        compiler_params=pltpu.CompilerParams(vmem_limit_bytes=24 * 1024 * 1024),
        name="edges",
    )(flow, viscosity, below, above)


def inner_kernel(comps, depth_z, width, flow, viscosity, below, above, first, middle):
    two = 2 * width

    def own(z):
        if z < 0:
            return [below[c * two + (2 + z) * width : c * two + (3 + z) * width, :] for c in range(comps)]
        if z >= depth_z:
            return [above[c * two + (z - depth_z) * width : c * two + (z - depth_z + 1) * width, :] for c in range(comps)]
        return [flow[(c * depth_z + z) * width : (c * depth_z + z + 1) * width, :] for c in range(comps)]

    for z in range(-1, depth_z + 1):
        if z < 0:
            visc = below[comps * two :, :]
        elif z == depth_z:
            visc = above[comps * two :, :]
        else:
            visc = viscosity[z * width : (z + 1) * width, :]
        centers, change = tendency(own(z), own(z + 1), own(z - 1), visc, width)
        for c in range(comps):
            first[c, z + 1, 0:width, :] = centers[c] + change[c]

    def second(z, carry):
        plane, upper, lower = ([first[c, z + 1 + d] for c in range(comps)] for d in (0, 1, -1))
        at = pl.multiple_of(z * width, width)
        centers, change = tendency(plane, upper, lower, viscosity[pl.ds(at, width), :], width)
        for c in range(comps):
            spot = pl.multiple_of((c * depth_z + z) * width, width)
            middle[pl.ds(spot, width), :] = 0.5 * flow[pl.ds(spot, width), :] + 0.5 * (centers[c] + change[c])
        return carry

    lax.fori_loop(0, depth_z, second, 0)


def inner(comps, depth_z, width, flow, viscosity, below, above):
    depth = flow.shape[1]
    return pl.pallas_call(
        functools.partial(inner_kernel, comps, depth_z, width),
        out_shape=(
            jax.ShapeDtypeStruct((comps, depth_z + 2, width, depth), jnp.float32),
            jax.ShapeDtypeStruct(flow.shape, jnp.float32),
        ),
        in_specs=[VM] * 4,
        out_specs=(VM, VM),
        compiler_params=pltpu.CompilerParams(vmem_limit_bytes=24 * 1024 * 1024),
        cost_estimate=pl.CostEstimate(flops=10**7, bytes_accessed=2**22, transcendentals=0),
        name="inner",
    )(flow, viscosity, below, above)


def outer_kernel(comps, depth_z, width, flow, viscosity, below, above, first, middle, left, right, inlet, second_out, inlet_now, strip, visc, started, table):
    depth = flow.shape[1]
    two = 2 * width
    rows = depth_z * width
    total = comps * rows
    base = 2 * comps * depth_z
    tile = lax.axis_index("tile")

    def from_left(spot, count):
        return jnp.where(tile > 0, left[spot : spot + count, :], 0.0)

    def from_right(spot, count):
        return jnp.where(tile < lax.axis_size("tile") - 1, right[spot : spot + count, :], 0.0)

    strip[...] = jnp.zeros_like(strip)
    visc[...] = jnp.zeros_like(visc)
    for c in range(comps):
        for z in range(-2, depth_z + 2):
            if z < 0:
                ref, spot = below, c * two + (2 + z) * width
            elif z >= depth_z:
                ref, spot = above, c * two + (z - depth_z) * width
            else:
                ref, spot = flow, (c * depth_z + z) * width
            strip[c, z + 2, 2:4, :] = ref[spot : spot + 2, :]
            strip[c, z + 2, 4:6, :] = ref[spot + width - 2 : spot + width, :]
            if 0 <= z < depth_z:
                k = 2 * (c * depth_z + z)
                strip[c, z + 2, 0:2, :] = from_left(k, 2)
                strip[c, z + 2, 6:8, :] = from_right(k, 2)
            elif z in (-1, depth_z):
                k = base + 2 * c + (z == depth_z)
                strip[c, z + 2, 1:2, :] = from_left(k, 1)
                strip[c, z + 2, 6:7, :] = from_right(k, 1)
    side = base + 2 * comps
    for z in range(-1, depth_z + 1):
        if z < 0:
            ref, spot = below, comps * two
        elif z == depth_z:
            ref, spot = above, comps * two
        else:
            ref, spot = viscosity, z * width
            visc[z + 1, 1:2, :] = from_left(side + z, 1)
            visc[z + 1, 6:7, :] = from_right(side + z, 1)
        visc[z + 1, 2:4, :] = ref[spot : spot + 2, :]
        visc[z + 1, 4:6, :] = ref[spot + width - 2 : spot + width, :]

    place = lax.broadcasted_iota(jnp.int32, (8, 1), 0)

    def apart(value):
        return jnp.where(place < 4, pltpu.roll(value, 7, 0), pltpu.roll(value, 1, 0))

    def one(z, carry):
        plane, upper, lower = ([strip[c, z + 1 + d] for c in range(comps)] for d in (0, 1, -1))
        centers, change = tendency(plane, upper, lower, visc[z], 8)
        for c in range(comps):
            ends = apart(centers[c] + change[c])
            near = jnp.where(place < 4, pltpu.roll(first[c, z, 0:8, :], 1, 0), pltpu.roll(first[c, z, width - 8 : width, :], 7, 0))
            started[c, z] = jnp.where((place < 2) | (place > 5), ends, near)
        return carry

    lax.fori_loop(0, depth_z + 2, one, 0, unroll=2)

    def second(z, carry):
        plane, upper, lower = ([started[c, z + 1 + d] for c in range(comps)] for d in (0, 1, -1))
        centers, change = tendency(plane, upper, lower, apart(visc[z + 1]), 8)
        for c in range(comps):
            spot = pl.multiple_of((c * depth_z + z) * width, width)
            edge = 0.5 * apart(strip[c, z + 2]) + 0.5 * (centers[c] + change[c])
            mine = middle[pl.ds(spot, width), :]
            top = jnp.where(place < 2, pltpu.roll(edge, 7, 0), mine[0:8])
            end = jnp.where(place > 5, pltpu.roll(edge, 1, 0), mine[width - 8 :])
            value = jnp.concatenate([top, mine[8 : width - 8], end] if width > 16 else [top, end], axis=0)
            second_out[pl.ds(spot, width), :] = value
            high, low = halves(value)
            table[pl.ds(spot, width), :] = high
            table[pl.ds(total + spot, width), :] = low
        return carry

    lax.fori_loop(0, depth_z, second, 0, unroll=2)

    cells = inlet[0:1, :]
    picked = jnp.dot(table[...], column_hot(cells, depth), preferred_element_type=jnp.float32)
    row = lax.broadcasted_iota(jnp.int32, (rows, cells.shape[1]), 0) == (cells >> (depth.bit_length() - 1))
    for c in range(comps):
        both = picked[c * rows : (c + 1) * rows] + picked[total + c * rows : total + (c + 1) * rows]
        inlet_now[c : c + 1, :] = jnp.sum(jnp.where(row, both, 0.0), axis=0, keepdims=True)


def outer(comps, depth_z, width, flow, viscosity, below, above, first, middle, left, right, inlet):
    depth = flow.shape[1]
    return pl.pallas_call(
        functools.partial(outer_kernel, comps, depth_z, width),
        out_shape=(
            jax.ShapeDtypeStruct(flow.shape, jnp.float32),
            jax.ShapeDtypeStruct((comps, inlet.shape[1]), jnp.float32),
        ),
        in_specs=[VM] * 9,
        out_specs=(VM, VM),
        scratch_shapes=[
            pltpu.VMEM((comps, depth_z + 4, 8, depth), jnp.float32),
            pltpu.VMEM((depth_z + 2, 8, depth), jnp.float32),
            pltpu.VMEM((comps, depth_z + 2, 8, depth), jnp.float32),
            pltpu.VMEM((2 * flow.shape[0], depth), jnp.bfloat16),
        ],
        compiler_params=pltpu.CompilerParams(vmem_limit_bytes=24 * 1024 * 1024),
        cost_estimate=pl.CostEstimate(flops=10**7, bytes_accessed=2**22, transcendentals=0),
        name="outer",
    )(flow, viscosity, below, above, first, middle, left, right, inlet)


def on_device(
    flow_field,
    viscosity,
    port_plane,
    port_match,
    inlet_cell,
    inclusion_state,
    response_rate,
    inclusion_mass,
    anchor_cell,
    live_counts,
    arrival_cell,
):
    comps, depth_z, width, depth = flow_field.shape
    partners, cap = anchor_cell.shape[2:]
    sizes = (comps, depth_z, width)
    flow = flow_field.reshape(-1, depth)
    visc = viscosity.reshape(-1, depth)
    count = lax.axis_size("tile")
    forth = [(i, (i + 1) % count) for i in range(count)]
    back = [((i + 1) % count, i) for i in range(count)]
    levels = lax.axis_size("sec")
    up = [(i, (i + 1) % levels) for i in range(levels)]
    down = [((i + 1) % levels, i) for i in range(levels)]
    over = [(i, (i + levels // 2) % levels) for i in range(levels)]

    low_cap, high_cap = caps(*sizes, flow, visc, port_plane)
    below = lax.ppermute(high_cap, "sec", up)
    above = lax.ppermute(low_cap, "sec", down)
    across = lax.ppermute(port_plane, "sec", over)
    counts = live_counts.reshape(-1)
    counts, low_cap, high_cap = lax.optimization_barrier((counts, low_cap, high_cap))
    sampled = sample(comps, counts, flow, anchor_cell.reshape(partners, cap))
    outgoing = slip(
        counts,
        sampled,
        inclusion_state.reshape(comps, partners, cap),
        response_rate.reshape(partners, cap),
        inclusion_mass.reshape(partners, cap),
        port_plane,
        above,
        across,
        below,
    )
    below, above, outgoing = lax.optimization_barrier((below, above, outgoing))
    arrived = lax.all_to_all(outgoing, "tile", split_axis=0, concat_axis=0, tiled=True)
    low_edge, high_edge, bottom, top = edges(*sizes, flow, visc, below, above)
    left = lax.ppermute(high_edge, "tile", forth)
    right = lax.ppermute(low_edge, "tile", back)
    inlet = jnp.pad(inlet_cell.reshape(1, -1), ((0, 0), (0, cap - inlet_cell.shape[0])))
    first, middle = inner(*sizes, flow, visc, bottom, top)
    second, inlet_now = outer(*sizes, flow, visc, bottom, top, first, middle, left, right, inlet)
    flow_next, arrived_state = land(
        port_match, second, inlet_now, inlet, arrival_cell.reshape(partners, cap), arrived
    )
    return flow_next.reshape(flow_field.shape), arrived_state.reshape(inclusion_state.shape)


def solution(mesh):
    return jax.shard_map(
        on_device,
        mesh=mesh,
        in_specs=(
            P(None, "sec", "tile", None),
            P("sec", "tile", None),
            P(None, ("sec", "tile")),
            P(("sec", "tile")),
            P(("sec", "tile")),
            P(None, "sec", "tile", None, None),
            P("sec", "tile", None, None),
            P("sec", "tile", None, None),
            P("sec", "tile", None, None),
            P("sec", "tile", None),
            P("sec", "tile", None, None),
        ),
        out_specs=(P(None, "sec", "tile", None), P(None, "sec", "tile", None, None)),
        check_vma=False,
    )
```

```python
import functools

import jax
import jax.numpy as jnp
from jax import lax
from jax.experimental import pallas as pl
from jax.experimental.pallas import tpu as pltpu
from jax.sharding import PartitionSpec as P

VM = pl.BlockSpec(memory_space=pltpu.VMEM)
SM = pl.BlockSpec(memory_space=pltpu.SMEM)
HB = pl.BlockSpec(memory_space=pltpu.HBM)


def halves(value):
    high = value.astype(jnp.bfloat16)
    low = (value - high.astype(jnp.float32)).astype(jnp.bfloat16)
    return high, low


def column_hot(cells, depth):
    at = lax.broadcasted_iota(jnp.int32, (depth, cells.shape[1]), 0)
    return jnp.where(at == (cells & (depth - 1)), 1.0, 0.0).astype(jnp.bfloat16)


def sample_kernel(GP, counts, flow, anchor, sampled, table, packed):
    partners, cap = anchor.shape
    total, depth = flow.shape
    comps = sampled.shape[1]
    rows = total // comps
    shift = depth.bit_length() - 1
    cap_shift = cap.bit_length() - 1
    lane = lax.broadcasted_iota(jnp.int32, (1, cap), 1)
    packed[...] = jnp.zeros_like(packed)

    def pack(p, base):
        begin = base & (cap - 1)
        spot = base >> cap_shift
        turned = pltpu.roll(anchor[pl.ds(p, 1), :], begin, 1)
        pltpu.store(packed.at[pl.ds(spot, 1), :], turned, mask=lane >= begin)
        pltpu.store(packed.at[pl.ds(spot + 1, 1), :], turned, mask=lane < begin)
        return base + counts[p]

    used = lax.fori_loop(0, partners, pack, 0, unroll=8)
    high, low = halves(flow[...])
    table[0:total] = high
    table[total:] = low

    def group(g, carry):
        first = g * GP
        cells = jnp.concatenate([packed[pl.ds(first + i, 1), :] for i in range(GP)], axis=1)
        hot = column_hot(cells, depth)
        picked = jnp.dot(table[...], hot, preferred_element_type=jnp.float32)
        row = lax.broadcasted_iota(jnp.int32, (rows, cells.shape[1]), 0) == (cells >> shift)
        parts = []
        for c in range(comps):
            both = picked[c * rows : (c + 1) * rows] + picked[total + c * rows : total + (c + 1) * rows]
            parts.append(jnp.sum(jnp.where(row, both, 0.0), axis=0, keepdims=True))
        found = jnp.concatenate(parts, axis=0)
        for i in range(GP):
            sampled[first + i] = found[:, i * cap : (i + 1) * cap]
        return carry

    lax.fori_loop(0, (used + GP * cap - 1) // (GP * cap), group, 0)


def sample(comps, counts, flow, anchor, GP=4):
    partners, cap = anchor.shape
    return pl.pallas_call(
        functools.partial(sample_kernel, GP),
        out_shape=jax.ShapeDtypeStruct((partners + 8, comps, cap), jnp.float32),
        in_specs=[SM, VM, VM],
        out_specs=VM,
        scratch_shapes=[
            pltpu.VMEM((2 * flow.shape[0], flow.shape[1]), jnp.bfloat16),
            pltpu.VMEM((partners + 8, cap), jnp.int32),
        ],
        compiler_params=pltpu.CompilerParams(vmem_limit_bytes=24 * 1024 * 1024),
        cost_estimate=pl.CostEstimate(flops=2 * 8192 * 512 * 1024, bytes_accessed=2**21, transcendentals=0),
        name="sample",
    )(counts, flow, anchor)


chunks = 4


def slip_kernel(counts, sampled, state, rate, mass, ports, above, across, below, far, out, whole, out_sems):
    comps, partners, cap = state.shape
    per = ports.shape[1]
    cap_shift = cap.bit_length() - 1
    last = above.shape[0] - 8
    lane = lax.broadcasted_iota(jnp.int32, (1, cap), 1)
    whole[:, 0:per] = ports[...]
    whole[:, per : 2 * per] = above[last : last + comps, 0:per]
    whole[:, 2 * per : 3 * per] = across[...]
    whole[:, 3 * per :] = below[last : last + comps, 0:per]

    def finish(p, base):
        n = counts[p]
        begin = base & (cap - 1)
        spot = base >> cap_shift
        both = jnp.where(lane >= begin, sampled[spot], sampled[spot + 1])
        value = pltpu.roll(both, (cap - begin) & (cap - 1), 1)
        own = jnp.concatenate([state[c, pl.ds(p, 1), :] for c in range(comps)], axis=0)
        r = rate[pl.ds(p, 1), :]
        drop = r * (own - value)
        live = lane < n
        out[3 * p] = jnp.where(live, own - drop, 0.0)
        out[3 * p + 1] = jnp.where(live, mass[pl.ds(p, 1), :] * drop, 0.0)
        out[3 * p + 2] = whole[...]
        return base + n

    block = partners // chunks
    base = 0
    copies = []
    for i in range(chunks):
        base = lax.fori_loop(i * block, (i + 1) * block, finish, base, unroll=8)
        part = pl.ds(3 * i * block, 3 * block)
        copies.append(pltpu.make_async_copy(out.at[part], far.at[part], out_sems.at[i]))
        copies[i].start()
    for copy in copies:
        copy.wait()


def slip(counts, sampled, state, rate, mass, ports, above, across, below):
    comps, partners, cap = state.shape
    return pl.pallas_call(
        slip_kernel,
        out_shape=jax.ShapeDtypeStruct((partners * 3, comps, cap), jnp.float32),
        in_specs=[SM] + [VM] * 8,
        out_specs=HB,
        scratch_shapes=[
            pltpu.VMEM((partners * 3, comps, cap), jnp.float32),
            pltpu.VMEM((comps, cap), jnp.float32),
            pltpu.SemaphoreType.DMA((chunks,)),
        ],
        compiler_params=pltpu.CompilerParams(vmem_limit_bytes=24 * 1024 * 1024),
        cost_estimate=pl.CostEstimate(flops=2 * 10**6, bytes_accessed=2**20, transcendentals=0),
        name="slip",
    )(counts, sampled, state, rate, mass, ports, above, across, below)


def land_kernel(GP, match, second, inlet_now, inlet, arrival, arrived, flow_far, state_far, flow_out, state_out, last_ref, last, packed, sem, out_sems):
    comps, partners, cap = state_out.shape
    total, depth = second.shape
    rows = total // comps
    shift = depth.bit_length() - 1
    cap_shift = cap.bit_length() - 1
    entries = match.shape[0]
    per = entries
    nt = (((1,), (1,)), ((), ()))
    slot = lax.broadcasted_iota(jnp.int32, (1, cap), 1)

    def ends(p, carry):
        moved = arrived[3 * p]
        gift = arrived[3 * p + 1]
        for c in range(comps):
            state_out[c, pl.ds(p, 1), :] = moved[c : c + 1]
        biggest = jnp.max(jnp.abs(gift), axis=0, keepdims=True)
        last_ref[pl.ds(p, 1), :] = jnp.where(biggest > 0.0, slot + 1, 0)
        return carry

    lax.fori_loop(0, partners, ends, 0, unroll=8)
    last_ref[partners:, :] = jnp.zeros_like(last_ref[partners:, :])
    top = jnp.max(last_ref[...].T, axis=0, keepdims=True)
    last_ref[0:1, :] = top
    fetch = pltpu.make_async_copy(last_ref.at[0:1, :], last, sem)
    fetch.start()
    state_copy = pltpu.make_async_copy(state_out, state_far, out_sems.at[2])
    state_copy.start()
    flow_out[...] = second[...]

    def add(cells, values, spot):
        row = lax.broadcasted_iota(jnp.int32, (rows, cells.shape[1]), 0) == (cells >> shift)
        high, low = halves(values)
        parts = []
        for part in (high.astype(jnp.float32), low.astype(jnp.float32)):
            for c in range(values.shape[0]):
                parts.append(jnp.where(row, part[c : c + 1], 0.0).astype(jnp.bfloat16))
        both = lax.dot_general(
            jnp.concatenate(parts, axis=0), column_hot(cells, depth), nt, preferred_element_type=jnp.float32
        )
        half = values.shape[0] * rows
        flow_out[spot : spot + half, :] += both[:half] + both[half:]

    section = lax.axis_index("sec")
    sections = cap // per
    target = jnp.zeros((comps, cap), jnp.float32)
    for k in range(entries):
        port = match[k]
        device = port // entries
        place = (device // partners + sections - section) % sections * per + port % entries
        turned = pltpu.roll(arrived[3 * (device % partners) + 2], (k + cap - place) % cap, 1)
        target = jnp.where(slot == k, turned, target)
    change = jnp.where(slot < entries, 0.5 * (target - inlet_now[...]), 0.0)
    packed[...] = jnp.zeros_like(packed)
    fetch.wait()

    def pack(p, base):
        begin = base & (cap - 1)
        spot = base >> cap_shift
        cells = arrival[pl.ds(p, 1), :].astype(jnp.float32)
        both = jnp.concatenate([arrived[3 * p + 1], jnp.broadcast_to(cells, (8 - comps, cap))], axis=0)
        turned = pltpu.roll(both, begin, 1)
        wide = lax.broadcasted_iota(jnp.int32, (8, cap), 1)
        pltpu.store(packed.at[spot], turned, mask=wide >= begin)
        pltpu.store(packed.at[spot + 1], turned, mask=wide < begin)
        return base + last[0, p]

    used = lax.fori_loop(0, partners, pack, 0, unroll=8)

    spare = (used + cap - 1) >> cap_shift
    cells = jnp.broadcast_to(inlet[0:1, :].astype(jnp.float32), (8 - comps, cap))
    packed[spare] = jnp.concatenate([change, cells], axis=0)

    def load(g):
        both = jnp.concatenate([packed[g * GP + i] for i in range(GP)], axis=1)
        return both[comps : comps + 1].astype(jnp.int32), both[:comps]

    def group(g, carry):
        cells, values = load(g)
        add(cells, values, 0)
        return carry

    final = spare // GP
    lax.fori_loop(0, final, group, 0)
    cells, values = load(final)
    half = comps // 2
    copies = []
    for i in range(2):
        part = pl.ds(i * half * rows, half * rows)
        add(cells, values[i * half : (i + 1) * half], i * half * rows)
        copies.append(pltpu.make_async_copy(flow_out.at[part, :], flow_far.at[part, :], out_sems.at[i]))
        copies[i].start()
    for copy in copies:
        copy.wait()
    state_copy.wait()


def land(match, second, inlet_now, inlet, arrival, arrived, GP=4):
    partners, cap = arrival.shape
    comps = arrived.shape[1]
    return pl.pallas_call(
        functools.partial(land_kernel, GP),
        out_shape=(
            jax.ShapeDtypeStruct(second.shape, jnp.float32),
            jax.ShapeDtypeStruct((comps, partners, cap), jnp.float32),
        ),
        in_specs=[SM] + [VM] * 5,
        out_specs=(HB, HB),
        scratch_shapes=[
            pltpu.VMEM(second.shape, jnp.float32),
            pltpu.VMEM((comps, partners, cap), jnp.float32),
            pltpu.VMEM((cap, cap), jnp.int32),
            pltpu.SMEM((1, cap), jnp.int32),
            pltpu.VMEM((partners + 8, 8, cap), jnp.float32),
            pltpu.SemaphoreType.DMA,
            pltpu.SemaphoreType.DMA((3,)),
        ],
        compiler_params=pltpu.CompilerParams(vmem_limit_bytes=24 * 1024 * 1024),
        cost_estimate=pl.CostEstimate(flops=2 * 8192 * 512 * 1024, bytes_accessed=2**21, transcendentals=0),
        name="land",
    )(match, second, inlet_now, inlet, arrival, arrived)


def tendency(plane, upper, lower, viscosity, keep):
    place = lax.broadcasted_iota(jnp.int32, (1, viscosity.shape[1]), 1)
    depth = viscosity.shape[1]
    centers, laps, dz, dx, dy = [], [], [], [], []
    for c in range(len(plane)):
        whole = plane[c]
        center = whole[:keep]
        up_x = pltpu.roll(whole, whole.shape[0] - 1, 0)[:keep]
        low_x = pltpu.roll(whole, 1, 0)[:keep]
        up_y = jnp.where(place == depth - 1, 0.0, pltpu.roll(center, depth - 1, 1))
        low_y = jnp.where(place == 0, 0.0, pltpu.roll(center, 1, 1))
        centers.append(center)
        laps.append((upper[c] + lower[c]) + (up_x + low_x) + (up_y + low_y) - 6.0 * center)
        dz.append(upper[c] - lower[c])
        dx.append(up_x - low_x)
        dy.append(up_y - low_y)
    strain = sum(d[c] * d[c] for c in range(3) for d in (dz, dx, dy)) * 0.25
    eddy = viscosity * (1.0 + strain / (1.0 + strain))
    out = []
    for c in range(len(plane)):
        carried = centers[0] * dz[c] + centers[1] * dx[c] + centers[2] * dy[c]
        out.append(0.5 * (eddy * laps[c]) - 0.25 * carried)
    return centers, out


def cap_kernel(comps, depth_z, width, flow, viscosity, ports, low_cap, high_cap):
    two = 2 * width
    last = depth_z * width
    for c in range(comps):
        low_cap[c * two : (c + 1) * two, :] = flow[c * last : c * last + two, :]
        high_cap[c * two : (c + 1) * two, :] = flow[(c + 1) * last - two : (c + 1) * last, :]
    base = comps * two
    low_cap[base : base + width, :] = viscosity[0:width, :]
    high_cap[base : base + width, :] = viscosity[last - width : last, :]
    for out in (low_cap, high_cap):
        out[base + width :, :] = jnp.zeros((8, out.shape[1]), jnp.float32)
        out[base + width : base + width + comps, 0 : ports.shape[1]] = ports[...]


def caps(comps, depth_z, width, flow, viscosity, ports):
    depth = flow.shape[1]
    cap = jax.ShapeDtypeStruct((2 * comps * width + width + 8, depth), jnp.float32)
    return pl.pallas_call(
        functools.partial(cap_kernel, comps, depth_z, width),
        out_shape=(cap, cap),
        in_specs=[VM] * 3,
        out_specs=(VM, VM),
        compiler_params=pltpu.CompilerParams(vmem_limit_bytes=60 * 1024 * 1024),
        name="caps",
    )(flow, viscosity, ports)


def edge_kernel(comps, depth_z, width, flow, viscosity, below, above, even_out, odd_out, bottom, top, low_out, high_out):
    section = lax.axis_index("sec")
    bottom[...] = jnp.where(section > 0, below[0 : bottom.shape[0], :], 0.0)
    top[...] = jnp.where(section < lax.axis_size("sec") - 1, above[0 : top.shape[0], :], 0.0)
    two = 2 * width
    for k in range(comps * depth_z):
        low_out[2 * k : 2 * k + 2, :] = flow[k * width : k * width + 2, :]
        high_out[2 * k : 2 * k + 2, :] = flow[(k + 1) * width - 2 : (k + 1) * width, :]
    base = 2 * comps * depth_z
    for c in range(comps):
        low_out[base + 2 * c : base + 2 * c + 1, :] = bottom[c * two + width : c * two + width + 1, :]
        low_out[base + 2 * c + 1 : base + 2 * c + 2, :] = top[c * two : c * two + 1, :]
        high_out[base + 2 * c : base + 2 * c + 1, :] = bottom[(c + 1) * two - 1 : (c + 1) * two, :]
        high_out[base + 2 * c + 1 : base + 2 * c + 2, :] = top[c * two + width - 1 : c * two + width, :]
    base += 2 * comps
    for z in range(depth_z):
        low_out[base + z : base + z + 1, :] = viscosity[z * width : z * width + 1, :]
        high_out[base + z : base + z + 1, :] = viscosity[(z + 1) * width - 1 : (z + 1) * width, :]
    even = lax.axis_index("tile") % 2 == 0
    even_out[...] = jnp.where(even, high_out[...], low_out[...])
    odd_out[...] = jnp.where(even, low_out[...], high_out[...])


def edges(comps, depth_z, width, flow, viscosity, below, above):
    depth = flow.shape[1]
    shape = jax.ShapeDtypeStruct((2 * comps * (depth_z + 1) + depth_z, depth), jnp.float32)
    halo = jax.ShapeDtypeStruct(((2 * comps + 1) * width, depth), jnp.float32)
    return pl.pallas_call(
        functools.partial(edge_kernel, comps, depth_z, width),
        out_shape=(shape, shape, halo, halo),
        in_specs=[VM] * 4,
        out_specs=(VM,) * 4,
        scratch_shapes=[pltpu.VMEM(shape.shape, jnp.float32)] * 2,
        compiler_params=pltpu.CompilerParams(vmem_limit_bytes=24 * 1024 * 1024),
        name="edges",
    )(flow, viscosity, below, above)


def inner_kernel(comps, depth_z, width, flow, viscosity, below, above, first, middle):
    two = 2 * width

    def own(z):
        if z < 0:
            return [below[c * two + (2 + z) * width : c * two + (3 + z) * width, :] for c in range(comps)]
        if z >= depth_z:
            return [above[c * two + (z - depth_z) * width : c * two + (z - depth_z + 1) * width, :] for c in range(comps)]
        return [flow[(c * depth_z + z) * width : (c * depth_z + z + 1) * width, :] for c in range(comps)]

    for z in range(-1, depth_z + 1):
        if z < 0:
            visc = below[comps * two :, :]
        elif z == depth_z:
            visc = above[comps * two :, :]
        else:
            visc = viscosity[z * width : (z + 1) * width, :]
        centers, change = tendency(own(z), own(z + 1), own(z - 1), visc, width)
        for c in range(comps):
            first[c, z + 1, 0:width, :] = centers[c] + change[c]

    def second(z, carry):
        plane, upper, lower = ([first[c, z + 1 + d] for c in range(comps)] for d in (0, 1, -1))
        at = pl.multiple_of(z * width, width)
        centers, change = tendency(plane, upper, lower, viscosity[pl.ds(at, width), :], width)
        for c in range(comps):
            spot = pl.multiple_of((c * depth_z + z) * width, width)
            middle[pl.ds(spot, width), :] = 0.5 * flow[pl.ds(spot, width), :] + 0.5 * (centers[c] + change[c])
        return carry

    lax.fori_loop(0, depth_z, second, 0)


def inner(comps, depth_z, width, flow, viscosity, below, above):
    depth = flow.shape[1]
    return pl.pallas_call(
        functools.partial(inner_kernel, comps, depth_z, width),
        out_shape=(
            jax.ShapeDtypeStruct((comps, depth_z + 2, width, depth), jnp.float32),
            jax.ShapeDtypeStruct(flow.shape, jnp.float32),
        ),
        in_specs=[VM] * 4,
        out_specs=(VM, VM),
        compiler_params=pltpu.CompilerParams(vmem_limit_bytes=24 * 1024 * 1024),
        cost_estimate=pl.CostEstimate(flops=10**7, bytes_accessed=2**22, transcendentals=0),
        name="inner",
    )(flow, viscosity, below, above)


def outer_kernel(comps, depth_z, width, flow, viscosity, below, above, first, middle, by_even, by_odd, inlet, second_out, inlet_now, strip, visc, started, table):
    depth = flow.shape[1]
    two = 2 * width
    rows = depth_z * width
    total = comps * rows
    base = 2 * comps * depth_z
    tile = lax.axis_index("tile")

    even = tile % 2 == 0

    def from_left(spot, count):
        side = pl.ds(spot, count)
        return jnp.where(tile > 0, jnp.where(even, by_odd[side, :], by_even[side, :]), 0.0)

    def from_right(spot, count):
        side = pl.ds(spot, count)
        return jnp.where(tile < lax.axis_size("tile") - 1, jnp.where(even, by_even[side, :], by_odd[side, :]), 0.0)

    strip[...] = jnp.zeros_like(strip)
    visc[...] = jnp.zeros_like(visc)
    for c in range(comps):
        for z in range(-2, depth_z + 2):
            if z < 0:
                ref, spot = below, c * two + (2 + z) * width
            elif z >= depth_z:
                ref, spot = above, c * two + (z - depth_z) * width
            else:
                ref, spot = flow, (c * depth_z + z) * width
            strip[c, z + 2, 2:4, :] = ref[spot : spot + 2, :]
            strip[c, z + 2, 4:6, :] = ref[spot + width - 2 : spot + width, :]
            if 0 <= z < depth_z:
                k = 2 * (c * depth_z + z)
                strip[c, z + 2, 0:2, :] = from_left(k, 2)
                strip[c, z + 2, 6:8, :] = from_right(k, 2)
            elif z in (-1, depth_z):
                k = base + 2 * c + (z == depth_z)
                strip[c, z + 2, 1:2, :] = from_left(k, 1)
                strip[c, z + 2, 6:7, :] = from_right(k, 1)
    side = base + 2 * comps
    for z in range(-1, depth_z + 1):
        if z < 0:
            ref, spot = below, comps * two
        elif z == depth_z:
            ref, spot = above, comps * two
        else:
            ref, spot = viscosity, z * width
            visc[z + 1, 1:2, :] = from_left(side + z, 1)
            visc[z + 1, 6:7, :] = from_right(side + z, 1)
        visc[z + 1, 2:4, :] = ref[spot : spot + 2, :]
        visc[z + 1, 4:6, :] = ref[spot + width - 2 : spot + width, :]

    place = lax.broadcasted_iota(jnp.int32, (8, 1), 0)

    def apart(value):
        return jnp.where(place < 4, pltpu.roll(value, 7, 0), pltpu.roll(value, 1, 0))

    def one(z, carry):
        plane, upper, lower = ([strip[c, z + 1 + d] for c in range(comps)] for d in (0, 1, -1))
        centers, change = tendency(plane, upper, lower, visc[z], 8)
        for c in range(comps):
            ends = apart(centers[c] + change[c])
            near = jnp.where(place < 4, pltpu.roll(first[c, z, 0:8, :], 1, 0), pltpu.roll(first[c, z, width - 8 : width, :], 7, 0))
            started[c, z] = jnp.where((place < 2) | (place > 5), ends, near)
        return carry

    lax.fori_loop(0, depth_z + 2, one, 0, unroll=2)

    def second(z, carry):
        plane, upper, lower = ([started[c, z + 1 + d] for c in range(comps)] for d in (0, 1, -1))
        centers, change = tendency(plane, upper, lower, apart(visc[z + 1]), 8)
        for c in range(comps):
            spot = pl.multiple_of((c * depth_z + z) * width, width)
            edge = 0.5 * apart(strip[c, z + 2]) + 0.5 * (centers[c] + change[c])
            mine = middle[pl.ds(spot, width), :]
            top = jnp.where(place < 2, pltpu.roll(edge, 7, 0), mine[0:8])
            end = jnp.where(place > 5, pltpu.roll(edge, 1, 0), mine[width - 8 :])
            value = jnp.concatenate([top, mine[8 : width - 8], end] if width > 16 else [top, end], axis=0)
            second_out[pl.ds(spot, width), :] = value
            high, low = halves(value)
            table[pl.ds(spot, width), :] = high
            table[pl.ds(total + spot, width), :] = low
        return carry

    lax.fori_loop(0, depth_z, second, 0, unroll=2)

    cells = inlet[0:1, :]
    picked = jnp.dot(table[...], column_hot(cells, depth), preferred_element_type=jnp.float32)
    row = lax.broadcasted_iota(jnp.int32, (rows, cells.shape[1]), 0) == (cells >> (depth.bit_length() - 1))
    for c in range(comps):
        both = picked[c * rows : (c + 1) * rows] + picked[total + c * rows : total + (c + 1) * rows]
        inlet_now[c : c + 1, :] = jnp.sum(jnp.where(row, both, 0.0), axis=0, keepdims=True)


def outer(comps, depth_z, width, flow, viscosity, below, above, first, middle, left, right, inlet):
    depth = flow.shape[1]
    return pl.pallas_call(
        functools.partial(outer_kernel, comps, depth_z, width),
        out_shape=(
            jax.ShapeDtypeStruct(flow.shape, jnp.float32),
            jax.ShapeDtypeStruct((comps, inlet.shape[1]), jnp.float32),
        ),
        in_specs=[VM] * 9,
        out_specs=(VM, VM),
        scratch_shapes=[
            pltpu.VMEM((comps, depth_z + 4, 8, depth), jnp.float32),
            pltpu.VMEM((depth_z + 2, 8, depth), jnp.float32),
            pltpu.VMEM((comps, depth_z + 2, 8, depth), jnp.float32),
            pltpu.VMEM((2 * flow.shape[0], depth), jnp.bfloat16),
        ],
        compiler_params=pltpu.CompilerParams(vmem_limit_bytes=24 * 1024 * 1024),
        cost_estimate=pl.CostEstimate(flops=10**7, bytes_accessed=2**22, transcendentals=0),
        name="outer",
    )(flow, viscosity, below, above, first, middle, left, right, inlet)


def on_device(
    flow_field,
    viscosity,
    port_plane,
    port_match,
    inlet_cell,
    inclusion_state,
    response_rate,
    inclusion_mass,
    anchor_cell,
    live_counts,
    arrival_cell,
):
    comps, depth_z, width, depth = flow_field.shape
    partners, cap = anchor_cell.shape[2:]
    sizes = (comps, depth_z, width)
    flow = flow_field.reshape(-1, depth)
    visc = viscosity.reshape(-1, depth)
    count = lax.axis_size("tile")
    even_pairs = [(i, i ^ 1) for i in range(count)]
    odd_pairs = [(0, 0), (count - 1, count - 1)] + [(i, ((i + 1) ^ 1) - 1) for i in range(1, count - 1)]
    levels = lax.axis_size("sec")
    up = [(i, (i + 1) % levels) for i in range(levels)]
    down = [((i + 1) % levels, i) for i in range(levels)]
    over = [(i, (i + levels // 2) % levels) for i in range(levels)]

    low_cap, high_cap = caps(*sizes, flow, visc, port_plane)
    below = lax.ppermute(high_cap, "sec", up)
    above = lax.ppermute(low_cap, "sec", down)
    across = lax.ppermute(port_plane, "sec", over)
    counts = live_counts.reshape(-1)
    counts, low_cap, high_cap = lax.optimization_barrier((counts, low_cap, high_cap))
    sampled = sample(comps, counts, flow, anchor_cell.reshape(partners, cap))
    outgoing = slip(
        counts,
        sampled,
        inclusion_state.reshape(comps, partners, cap),
        response_rate.reshape(partners, cap),
        inclusion_mass.reshape(partners, cap),
        port_plane,
        above,
        across,
        below,
    )
    below, above, outgoing = lax.optimization_barrier((below, above, outgoing))
    arrived = lax.all_to_all(outgoing, "tile", split_axis=0, concat_axis=0, tiled=True)
    even_edge, odd_edge, bottom, top = edges(*sizes, flow, visc, below, above)
    by_even = lax.ppermute(even_edge, "tile", even_pairs)
    by_odd = lax.ppermute(odd_edge, "tile", odd_pairs)
    inlet = jnp.pad(inlet_cell.reshape(1, -1), ((0, 0), (0, cap - inlet_cell.shape[0])))
    first, middle = inner(*sizes, flow, visc, bottom, top)
    second, inlet_now = outer(*sizes, flow, visc, bottom, top, first, middle, by_even, by_odd, inlet)
    flow_next, arrived_state = land(
        port_match, second, inlet_now, inlet, arrival_cell.reshape(partners, cap), arrived
    )
    return flow_next.reshape(flow_field.shape), arrived_state.reshape(inclusion_state.shape)


def solution(mesh):
    return jax.shard_map(
        on_device,
        mesh=mesh,
        in_specs=(
            P(None, "sec", "tile", None),
            P("sec", "tile", None),
            P(None, ("sec", "tile")),
            P(("sec", "tile")),
            P(("sec", "tile")),
            P(None, "sec", "tile", None, None),
            P("sec", "tile", None, None),
            P("sec", "tile", None, None),
            P("sec", "tile", None, None),
            P("sec", "tile", None),
            P("sec", "tile", None, None),
        ),
        out_specs=(P(None, "sec", "tile", None), P(None, "sec", "tile", None, None)),
        check_vma=False,
    )
```

```python
import functools

import jax
import jax.numpy as jnp
from jax import lax
from jax.experimental import pallas as pl
from jax.experimental.pallas import tpu as pltpu
from jax.sharding import PartitionSpec as P

VM = pl.BlockSpec(memory_space=pltpu.VMEM)
SM = pl.BlockSpec(memory_space=pltpu.SMEM)
HB = pl.BlockSpec(memory_space=pltpu.HBM)


def halves(value):
    high = value.astype(jnp.bfloat16)
    low = (value - high.astype(jnp.float32)).astype(jnp.bfloat16)
    return high, low


def column_hot(cells, depth):
    at = lax.broadcasted_iota(jnp.int32, (depth, cells.shape[1]), 0)
    return jnp.where(at == (cells & (depth - 1)), 1.0, 0.0).astype(jnp.bfloat16)


def sample_kernel(GP, counts, flow, anchor, sampled, table, packed):
    partners, cap = anchor.shape
    total, depth = flow.shape
    comps = sampled.shape[1]
    rows = total // comps
    shift = depth.bit_length() - 1
    cap_shift = cap.bit_length() - 1
    lane = lax.broadcasted_iota(jnp.int32, (1, cap), 1)
    packed[...] = jnp.zeros_like(packed)

    def pack(p, base):
        begin = base & (cap - 1)
        spot = base >> cap_shift
        turned = pltpu.roll(anchor[pl.ds(p, 1), :], begin, 1)
        pltpu.store(packed.at[pl.ds(spot, 1), :], turned, mask=lane >= begin)
        pltpu.store(packed.at[pl.ds(spot + 1, 1), :], turned, mask=lane < begin)
        return base + counts[p]

    used = lax.fori_loop(0, partners, pack, 0, unroll=8)
    high, low = halves(flow[...])
    table[0:total] = high
    table[total:] = low

    def group(g, carry):
        first = g * GP
        cells = jnp.concatenate([packed[pl.ds(first + i, 1), :] for i in range(GP)], axis=1)
        hot = column_hot(cells, depth)
        picked = jnp.dot(table[...], hot, preferred_element_type=jnp.float32)
        row = lax.broadcasted_iota(jnp.int32, (rows, cells.shape[1]), 0) == (cells >> shift)
        parts = []
        for c in range(comps):
            both = picked[c * rows : (c + 1) * rows] + picked[total + c * rows : total + (c + 1) * rows]
            parts.append(jnp.sum(jnp.where(row, both, 0.0), axis=0, keepdims=True))
        found = jnp.concatenate(parts, axis=0)
        for i in range(GP):
            sampled[first + i] = found[:, i * cap : (i + 1) * cap]
        return carry

    lax.fori_loop(0, (used + GP * cap - 1) // (GP * cap), group, 0)


def sample(comps, counts, flow, anchor, GP=4):
    partners, cap = anchor.shape
    return pl.pallas_call(
        functools.partial(sample_kernel, GP),
        out_shape=jax.ShapeDtypeStruct((partners + 8, comps, cap), jnp.float32),
        in_specs=[SM, VM, VM],
        out_specs=VM,
        scratch_shapes=[
            pltpu.VMEM((2 * flow.shape[0], flow.shape[1]), jnp.bfloat16),
            pltpu.VMEM((partners + 8, cap), jnp.int32),
        ],
        compiler_params=pltpu.CompilerParams(vmem_limit_bytes=24 * 1024 * 1024),
        cost_estimate=pl.CostEstimate(flops=2 * 8192 * 512 * 1024, bytes_accessed=2**21, transcendentals=0),
        name="sample",
    )(counts, flow, anchor)


chunks = 4


def slip_kernel(counts, sampled, state, rate, mass, ports, near, across, opposite, far, out, whole, out_sems):
    comps, partners, cap = state.shape
    per = ports.shape[1]
    cap_shift = cap.bit_length() - 1
    last = near.shape[0] - 8
    lane = lax.broadcasted_iota(jnp.int32, (1, cap), 1)
    whole[:, 0:per] = ports[...]
    even = lax.axis_index("sec") % 2 == 0
    close = near[last : last + comps, 0:per]
    whole[:, per : 2 * per] = jnp.where(even, close, opposite[...])
    whole[:, 2 * per : 3 * per] = across[...]
    whole[:, 3 * per :] = jnp.where(even, opposite[...], close)

    def finish(p, base):
        n = counts[p]
        begin = base & (cap - 1)
        spot = base >> cap_shift
        both = jnp.where(lane >= begin, sampled[spot], sampled[spot + 1])
        value = pltpu.roll(both, (cap - begin) & (cap - 1), 1)
        own = jnp.concatenate([state[c, pl.ds(p, 1), :] for c in range(comps)], axis=0)
        r = rate[pl.ds(p, 1), :]
        drop = r * (own - value)
        live = lane < n
        out[3 * p] = jnp.where(live, own - drop, 0.0)
        out[3 * p + 1] = jnp.where(live, mass[pl.ds(p, 1), :] * drop, 0.0)
        out[3 * p + 2] = whole[...]
        return base + n

    block = partners // chunks
    base = 0
    copies = []
    for i in range(chunks):
        base = lax.fori_loop(i * block, (i + 1) * block, finish, base, unroll=8)
        part = pl.ds(3 * i * block, 3 * block)
        copies.append(pltpu.make_async_copy(out.at[part], far.at[part], out_sems.at[i]))
        copies[i].start()
    for copy in copies:
        copy.wait()


def slip(counts, sampled, state, rate, mass, ports, near, across, opposite):
    comps, partners, cap = state.shape
    return pl.pallas_call(
        slip_kernel,
        out_shape=jax.ShapeDtypeStruct((partners * 3, comps, cap), jnp.float32),
        in_specs=[SM] + [VM] * 8,
        out_specs=HB,
        scratch_shapes=[
            pltpu.VMEM((partners * 3, comps, cap), jnp.float32),
            pltpu.VMEM((comps, cap), jnp.float32),
            pltpu.SemaphoreType.DMA((chunks,)),
        ],
        compiler_params=pltpu.CompilerParams(vmem_limit_bytes=24 * 1024 * 1024),
        cost_estimate=pl.CostEstimate(flops=2 * 10**6, bytes_accessed=2**20, transcendentals=0),
        name="slip",
    )(counts, sampled, state, rate, mass, ports, near, across, opposite)


def land_kernel(GP, match, second, inlet_now, inlet, arrival, arrived, flow_far, state_far, flow_out, state_out, last_ref, last, packed, sem, out_sems):
    comps, partners, cap = state_out.shape
    total, depth = second.shape
    rows = total // comps
    shift = depth.bit_length() - 1
    cap_shift = cap.bit_length() - 1
    entries = match.shape[0]
    per = entries
    nt = (((1,), (1,)), ((), ()))
    slot = lax.broadcasted_iota(jnp.int32, (1, cap), 1)

    def ends(p, carry):
        moved = arrived[3 * p]
        gift = arrived[3 * p + 1]
        for c in range(comps):
            state_out[c, pl.ds(p, 1), :] = moved[c : c + 1]
        biggest = jnp.max(jnp.abs(gift), axis=0, keepdims=True)
        last_ref[pl.ds(p, 1), :] = jnp.where(biggest > 0.0, slot + 1, 0)
        return carry

    lax.fori_loop(0, partners, ends, 0, unroll=8)
    last_ref[partners:, :] = jnp.zeros_like(last_ref[partners:, :])
    top = jnp.max(last_ref[...].T, axis=0, keepdims=True)
    last_ref[0:1, :] = top
    fetch = pltpu.make_async_copy(last_ref.at[0:1, :], last, sem)
    fetch.start()
    state_copy = pltpu.make_async_copy(state_out, state_far, out_sems.at[2])
    state_copy.start()
    flow_out[...] = second[...]

    def add(cells, values, spot):
        row = lax.broadcasted_iota(jnp.int32, (rows, cells.shape[1]), 0) == (cells >> shift)
        high, low = halves(values)
        parts = []
        for part in (high.astype(jnp.float32), low.astype(jnp.float32)):
            for c in range(values.shape[0]):
                parts.append(jnp.where(row, part[c : c + 1], 0.0).astype(jnp.bfloat16))
        both = lax.dot_general(
            jnp.concatenate(parts, axis=0), column_hot(cells, depth), nt, preferred_element_type=jnp.float32
        )
        half = values.shape[0] * rows
        flow_out[spot : spot + half, :] += both[:half] + both[half:]

    section = lax.axis_index("sec")
    sections = cap // per
    target = jnp.zeros((comps, cap), jnp.float32)
    for k in range(entries):
        port = match[k]
        device = port // entries
        place = (device // partners + sections - section) % sections * per + port % entries
        turned = pltpu.roll(arrived[3 * (device % partners) + 2], (k + cap - place) % cap, 1)
        target = jnp.where(slot == k, turned, target)
    change = jnp.where(slot < entries, 0.5 * (target - inlet_now[...]), 0.0)
    packed[...] = jnp.zeros_like(packed)
    fetch.wait()

    def pack(p, base):
        begin = base & (cap - 1)
        spot = base >> cap_shift
        cells = arrival[pl.ds(p, 1), :].astype(jnp.float32)
        both = jnp.concatenate([arrived[3 * p + 1], jnp.broadcast_to(cells, (8 - comps, cap))], axis=0)
        turned = pltpu.roll(both, begin, 1)
        wide = lax.broadcasted_iota(jnp.int32, (8, cap), 1)
        pltpu.store(packed.at[spot], turned, mask=wide >= begin)
        pltpu.store(packed.at[spot + 1], turned, mask=wide < begin)
        return base + last[0, p]

    used = lax.fori_loop(0, partners, pack, 0, unroll=8)

    spare = (used + cap - 1) >> cap_shift
    cells = jnp.broadcast_to(inlet[0:1, :].astype(jnp.float32), (8 - comps, cap))
    packed[spare] = jnp.concatenate([change, cells], axis=0)

    def load(g):
        both = jnp.concatenate([packed[g * GP + i] for i in range(GP)], axis=1)
        return both[comps : comps + 1].astype(jnp.int32), both[:comps]

    def group(g, carry):
        cells, values = load(g)
        add(cells, values, 0)
        return carry

    final = spare // GP
    lax.fori_loop(0, final, group, 0)
    cells, values = load(final)
    half = comps // 2
    copies = []
    for i in range(2):
        part = pl.ds(i * half * rows, half * rows)
        add(cells, values[i * half : (i + 1) * half], i * half * rows)
        copies.append(pltpu.make_async_copy(flow_out.at[part, :], flow_far.at[part, :], out_sems.at[i]))
        copies[i].start()
    for copy in copies:
        copy.wait()
    state_copy.wait()


def land(match, second, inlet_now, inlet, arrival, arrived, GP=4):
    partners, cap = arrival.shape
    comps = arrived.shape[1]
    return pl.pallas_call(
        functools.partial(land_kernel, GP),
        out_shape=(
            jax.ShapeDtypeStruct(second.shape, jnp.float32),
            jax.ShapeDtypeStruct((comps, partners, cap), jnp.float32),
        ),
        in_specs=[SM] + [VM] * 5,
        out_specs=(HB, HB),
        scratch_shapes=[
            pltpu.VMEM(second.shape, jnp.float32),
            pltpu.VMEM((comps, partners, cap), jnp.float32),
            pltpu.VMEM((cap, cap), jnp.int32),
            pltpu.SMEM((1, cap), jnp.int32),
            pltpu.VMEM((partners + 8, 8, cap), jnp.float32),
            pltpu.SemaphoreType.DMA,
            pltpu.SemaphoreType.DMA((3,)),
        ],
        compiler_params=pltpu.CompilerParams(vmem_limit_bytes=24 * 1024 * 1024),
        cost_estimate=pl.CostEstimate(flops=2 * 8192 * 512 * 1024, bytes_accessed=2**21, transcendentals=0),
        name="land",
    )(match, second, inlet_now, inlet, arrival, arrived)


def tendency(plane, upper, lower, viscosity, keep):
    place = lax.broadcasted_iota(jnp.int32, (1, viscosity.shape[1]), 1)
    depth = viscosity.shape[1]
    centers, laps, dz, dx, dy = [], [], [], [], []
    for c in range(len(plane)):
        whole = plane[c]
        center = whole[:keep]
        up_x = pltpu.roll(whole, whole.shape[0] - 1, 0)[:keep]
        low_x = pltpu.roll(whole, 1, 0)[:keep]
        up_y = jnp.where(place == depth - 1, 0.0, pltpu.roll(center, depth - 1, 1))
        low_y = jnp.where(place == 0, 0.0, pltpu.roll(center, 1, 1))
        centers.append(center)
        laps.append((upper[c] + lower[c]) + (up_x + low_x) + (up_y + low_y) - 6.0 * center)
        dz.append(upper[c] - lower[c])
        dx.append(up_x - low_x)
        dy.append(up_y - low_y)
    strain = sum(d[c] * d[c] for c in range(3) for d in (dz, dx, dy)) * 0.25
    eddy = viscosity * (1.0 + strain / (1.0 + strain))
    out = []
    for c in range(len(plane)):
        carried = centers[0] * dz[c] + centers[1] * dx[c] + centers[2] * dy[c]
        out.append(0.5 * (eddy * laps[c]) - 0.25 * carried)
    return centers, out


def cap_kernel(comps, depth_z, width, flow, viscosity, ports, near_out, next_out):
    even = lax.axis_index("sec") % 2 == 0
    two = 2 * width
    last = depth_z * width

    def put(spot, count, low, high):
        near_out[spot : spot + count, :] = jnp.where(even, high, low)
        next_out[spot : spot + count, :] = jnp.where(even, low, high)

    for c in range(comps):
        put(c * two, two, flow[c * last : c * last + two, :], flow[(c + 1) * last - two : (c + 1) * last, :])
    base = comps * two
    put(base, width, viscosity[0:width, :], viscosity[last - width : last, :])
    for out in (near_out, next_out):
        out[base + width :, :] = jnp.zeros((8, out.shape[1]), jnp.float32)
        out[base + width : base + width + comps, 0 : ports.shape[1]] = ports[...]


def caps(comps, depth_z, width, flow, viscosity, ports):
    depth = flow.shape[1]
    cap = jax.ShapeDtypeStruct((2 * comps * width + width + 8, depth), jnp.float32)
    return pl.pallas_call(
        functools.partial(cap_kernel, comps, depth_z, width),
        out_shape=(cap, cap),
        in_specs=[VM] * 3,
        out_specs=(VM, VM),
        compiler_params=pltpu.CompilerParams(vmem_limit_bytes=60 * 1024 * 1024),
        name="caps",
    )(flow, viscosity, ports)


def edge_kernel(comps, depth_z, width, flow, viscosity, by_near, by_next, even_out, odd_out, bottom, top, low_out, high_out):
    section = lax.axis_index("sec")
    upper = section % 2 == 0
    near = by_near[0 : bottom.shape[0], :]
    beyond = by_next[0 : bottom.shape[0], :]
    bottom[...] = jnp.where(section > 0, jnp.where(upper, beyond, near), 0.0)
    top[...] = jnp.where(section < lax.axis_size("sec") - 1, jnp.where(upper, near, beyond), 0.0)
    two = 2 * width
    for k in range(comps * depth_z):
        low_out[2 * k : 2 * k + 2, :] = flow[k * width : k * width + 2, :]
        high_out[2 * k : 2 * k + 2, :] = flow[(k + 1) * width - 2 : (k + 1) * width, :]
    base = 2 * comps * depth_z
    for c in range(comps):
        low_out[base + 2 * c : base + 2 * c + 1, :] = bottom[c * two + width : c * two + width + 1, :]
        low_out[base + 2 * c + 1 : base + 2 * c + 2, :] = top[c * two : c * two + 1, :]
        high_out[base + 2 * c : base + 2 * c + 1, :] = bottom[(c + 1) * two - 1 : (c + 1) * two, :]
        high_out[base + 2 * c + 1 : base + 2 * c + 2, :] = top[c * two + width - 1 : c * two + width, :]
    base += 2 * comps
    for z in range(depth_z):
        low_out[base + z : base + z + 1, :] = viscosity[z * width : z * width + 1, :]
        high_out[base + z : base + z + 1, :] = viscosity[(z + 1) * width - 1 : (z + 1) * width, :]
    even = lax.axis_index("tile") % 2 == 0
    even_out[...] = jnp.where(even, high_out[...], low_out[...])
    odd_out[...] = jnp.where(even, low_out[...], high_out[...])


def edges(comps, depth_z, width, flow, viscosity, below, above):
    depth = flow.shape[1]
    shape = jax.ShapeDtypeStruct((2 * comps * (depth_z + 1) + depth_z, depth), jnp.float32)
    halo = jax.ShapeDtypeStruct(((2 * comps + 1) * width, depth), jnp.float32)
    return pl.pallas_call(
        functools.partial(edge_kernel, comps, depth_z, width),
        out_shape=(shape, shape, halo, halo),
        in_specs=[VM] * 4,
        out_specs=(VM,) * 4,
        scratch_shapes=[pltpu.VMEM(shape.shape, jnp.float32)] * 2,
        compiler_params=pltpu.CompilerParams(vmem_limit_bytes=24 * 1024 * 1024),
        name="edges",
    )(flow, viscosity, below, above)


def inner_kernel(comps, depth_z, width, flow, viscosity, below, above, first, middle):
    two = 2 * width

    def own(z):
        if z < 0:
            return [below[c * two + (2 + z) * width : c * two + (3 + z) * width, :] for c in range(comps)]
        if z >= depth_z:
            return [above[c * two + (z - depth_z) * width : c * two + (z - depth_z + 1) * width, :] for c in range(comps)]
        return [flow[(c * depth_z + z) * width : (c * depth_z + z + 1) * width, :] for c in range(comps)]

    for z in range(-1, depth_z + 1):
        if z < 0:
            visc = below[comps * two :, :]
        elif z == depth_z:
            visc = above[comps * two :, :]
        else:
            visc = viscosity[z * width : (z + 1) * width, :]
        centers, change = tendency(own(z), own(z + 1), own(z - 1), visc, width)
        for c in range(comps):
            first[c, z + 1, 0:width, :] = centers[c] + change[c]

    def second(z, carry):
        plane, upper, lower = ([first[c, z + 1 + d] for c in range(comps)] for d in (0, 1, -1))
        at = pl.multiple_of(z * width, width)
        centers, change = tendency(plane, upper, lower, viscosity[pl.ds(at, width), :], width)
        for c in range(comps):
            spot = pl.multiple_of((c * depth_z + z) * width, width)
            middle[pl.ds(spot, width), :] = 0.5 * flow[pl.ds(spot, width), :] + 0.5 * (centers[c] + change[c])
        return carry

    lax.fori_loop(0, depth_z, second, 0)


def inner(comps, depth_z, width, flow, viscosity, below, above):
    depth = flow.shape[1]
    return pl.pallas_call(
        functools.partial(inner_kernel, comps, depth_z, width),
        out_shape=(
            jax.ShapeDtypeStruct((comps, depth_z + 2, width, depth), jnp.float32),
            jax.ShapeDtypeStruct(flow.shape, jnp.float32),
        ),
        in_specs=[VM] * 4,
        out_specs=(VM, VM),
        compiler_params=pltpu.CompilerParams(vmem_limit_bytes=24 * 1024 * 1024),
        cost_estimate=pl.CostEstimate(flops=10**7, bytes_accessed=2**22, transcendentals=0),
        name="inner",
    )(flow, viscosity, below, above)


def outer_kernel(comps, depth_z, width, flow, viscosity, below, above, first, middle, by_even, by_odd, inlet, second_out, inlet_now, strip, visc, started, table):
    depth = flow.shape[1]
    two = 2 * width
    rows = depth_z * width
    total = comps * rows
    base = 2 * comps * depth_z
    tile = lax.axis_index("tile")

    even = tile % 2 == 0

    def from_left(spot, count):
        side = pl.ds(spot, count)
        return jnp.where(tile > 0, jnp.where(even, by_odd[side, :], by_even[side, :]), 0.0)

    def from_right(spot, count):
        side = pl.ds(spot, count)
        return jnp.where(tile < lax.axis_size("tile") - 1, jnp.where(even, by_even[side, :], by_odd[side, :]), 0.0)

    strip[...] = jnp.zeros_like(strip)
    visc[...] = jnp.zeros_like(visc)
    for c in range(comps):
        for z in range(-2, depth_z + 2):
            if z < 0:
                ref, spot = below, c * two + (2 + z) * width
            elif z >= depth_z:
                ref, spot = above, c * two + (z - depth_z) * width
            else:
                ref, spot = flow, (c * depth_z + z) * width
            strip[c, z + 2, 2:4, :] = ref[spot : spot + 2, :]
            strip[c, z + 2, 4:6, :] = ref[spot + width - 2 : spot + width, :]
            if 0 <= z < depth_z:
                k = 2 * (c * depth_z + z)
                strip[c, z + 2, 0:2, :] = from_left(k, 2)
                strip[c, z + 2, 6:8, :] = from_right(k, 2)
            elif z in (-1, depth_z):
                k = base + 2 * c + (z == depth_z)
                strip[c, z + 2, 1:2, :] = from_left(k, 1)
                strip[c, z + 2, 6:7, :] = from_right(k, 1)
    side = base + 2 * comps
    for z in range(-1, depth_z + 1):
        if z < 0:
            ref, spot = below, comps * two
        elif z == depth_z:
            ref, spot = above, comps * two
        else:
            ref, spot = viscosity, z * width
            visc[z + 1, 1:2, :] = from_left(side + z, 1)
            visc[z + 1, 6:7, :] = from_right(side + z, 1)
        visc[z + 1, 2:4, :] = ref[spot : spot + 2, :]
        visc[z + 1, 4:6, :] = ref[spot + width - 2 : spot + width, :]

    place = lax.broadcasted_iota(jnp.int32, (8, 1), 0)

    def apart(value):
        return jnp.where(place < 4, pltpu.roll(value, 7, 0), pltpu.roll(value, 1, 0))

    def one(z, carry):
        plane, upper, lower = ([strip[c, z + 1 + d] for c in range(comps)] for d in (0, 1, -1))
        centers, change = tendency(plane, upper, lower, visc[z], 8)
        for c in range(comps):
            ends = apart(centers[c] + change[c])
            near = jnp.where(place < 4, pltpu.roll(first[c, z, 0:8, :], 1, 0), pltpu.roll(first[c, z, width - 8 : width, :], 7, 0))
            started[c, z] = jnp.where((place < 2) | (place > 5), ends, near)
        return carry

    lax.fori_loop(0, depth_z + 2, one, 0, unroll=2)

    def second(z, carry):
        plane, upper, lower = ([started[c, z + 1 + d] for c in range(comps)] for d in (0, 1, -1))
        centers, change = tendency(plane, upper, lower, apart(visc[z + 1]), 8)
        for c in range(comps):
            spot = pl.multiple_of((c * depth_z + z) * width, width)
            edge = 0.5 * apart(strip[c, z + 2]) + 0.5 * (centers[c] + change[c])
            mine = middle[pl.ds(spot, width), :]
            top = jnp.where(place < 2, pltpu.roll(edge, 7, 0), mine[0:8])
            end = jnp.where(place > 5, pltpu.roll(edge, 1, 0), mine[width - 8 :])
            value = jnp.concatenate([top, mine[8 : width - 8], end] if width > 16 else [top, end], axis=0)
            second_out[pl.ds(spot, width), :] = value
            high, low = halves(value)
            table[pl.ds(spot, width), :] = high
            table[pl.ds(total + spot, width), :] = low
        return carry

    lax.fori_loop(0, depth_z, second, 0, unroll=2)

    cells = inlet[0:1, :]
    picked = jnp.dot(table[...], column_hot(cells, depth), preferred_element_type=jnp.float32)
    row = lax.broadcasted_iota(jnp.int32, (rows, cells.shape[1]), 0) == (cells >> (depth.bit_length() - 1))
    for c in range(comps):
        both = picked[c * rows : (c + 1) * rows] + picked[total + c * rows : total + (c + 1) * rows]
        inlet_now[c : c + 1, :] = jnp.sum(jnp.where(row, both, 0.0), axis=0, keepdims=True)


def outer(comps, depth_z, width, flow, viscosity, below, above, first, middle, left, right, inlet):
    depth = flow.shape[1]
    return pl.pallas_call(
        functools.partial(outer_kernel, comps, depth_z, width),
        out_shape=(
            jax.ShapeDtypeStruct(flow.shape, jnp.float32),
            jax.ShapeDtypeStruct((comps, inlet.shape[1]), jnp.float32),
        ),
        in_specs=[VM] * 9,
        out_specs=(VM, VM),
        scratch_shapes=[
            pltpu.VMEM((comps, depth_z + 4, 8, depth), jnp.float32),
            pltpu.VMEM((depth_z + 2, 8, depth), jnp.float32),
            pltpu.VMEM((comps, depth_z + 2, 8, depth), jnp.float32),
            pltpu.VMEM((2 * flow.shape[0], depth), jnp.bfloat16),
        ],
        compiler_params=pltpu.CompilerParams(vmem_limit_bytes=24 * 1024 * 1024),
        cost_estimate=pl.CostEstimate(flops=10**7, bytes_accessed=2**22, transcendentals=0),
        name="outer",
    )(flow, viscosity, below, above, first, middle, left, right, inlet)


def on_device(
    flow_field,
    viscosity,
    port_plane,
    port_match,
    inlet_cell,
    inclusion_state,
    response_rate,
    inclusion_mass,
    anchor_cell,
    live_counts,
    arrival_cell,
):
    comps, depth_z, width, depth = flow_field.shape
    partners, cap = anchor_cell.shape[2:]
    sizes = (comps, depth_z, width)
    flow = flow_field.reshape(-1, depth)
    visc = viscosity.reshape(-1, depth)
    count = lax.axis_size("tile")
    even_pairs = [(i, i ^ 1) for i in range(count)]
    odd_pairs = [(0, 0), (count - 1, count - 1)] + [(i, ((i + 1) ^ 1) - 1) for i in range(1, count - 1)]
    levels = lax.axis_size("sec")
    near_pairs = [(i, i ^ 1) for i in range(levels)]
    next_pairs = [(0, 0), (levels - 1, levels - 1)] + [(i, ((i + 1) ^ 1) - 1) for i in range(1, levels - 1)]

    near_cap, next_cap = caps(*sizes, flow, visc, port_plane)
    by_near = lax.ppermute(near_cap, "sec", near_pairs)
    by_next = lax.ppermute(next_cap, "sec", next_pairs)
    across = lax.ppermute(port_plane, "sec", [(i, (i + levels // 2) % levels) for i in range(levels)])
    opposite = lax.ppermute(port_plane, "sec", [(i, levels - 1 - i) for i in range(levels)])
    counts = live_counts.reshape(-1)
    counts, near_cap, next_cap = lax.optimization_barrier((counts, near_cap, next_cap))
    sampled = sample(comps, counts, flow, anchor_cell.reshape(partners, cap))
    outgoing = slip(
        counts,
        sampled,
        inclusion_state.reshape(comps, partners, cap),
        response_rate.reshape(partners, cap),
        inclusion_mass.reshape(partners, cap),
        port_plane,
        by_near,
        across,
        opposite,
    )
    by_near, by_next, outgoing = lax.optimization_barrier((by_near, by_next, outgoing))
    arrived = lax.all_to_all(outgoing, "tile", split_axis=0, concat_axis=0, tiled=True)
    even_edge, odd_edge, bottom, top = edges(*sizes, flow, visc, by_near, by_next)
    by_even = lax.ppermute(even_edge, "tile", even_pairs)
    by_odd = lax.ppermute(odd_edge, "tile", odd_pairs)
    inlet = jnp.pad(inlet_cell.reshape(1, -1), ((0, 0), (0, cap - inlet_cell.shape[0])))
    first, middle = inner(*sizes, flow, visc, bottom, top)
    second, inlet_now = outer(*sizes, flow, visc, bottom, top, first, middle, by_even, by_odd, inlet)
    flow_next, arrived_state = land(
        port_match, second, inlet_now, inlet, arrival_cell.reshape(partners, cap), arrived
    )
    return flow_next.reshape(flow_field.shape), arrived_state.reshape(inclusion_state.shape)


def solution(mesh):
    return jax.shard_map(
        on_device,
        mesh=mesh,
        in_specs=(
            P(None, "sec", "tile", None),
            P("sec", "tile", None),
            P(None, ("sec", "tile")),
            P(("sec", "tile")),
            P(("sec", "tile")),
            P(None, "sec", "tile", None, None),
            P("sec", "tile", None, None),
            P("sec", "tile", None, None),
            P("sec", "tile", None, None),
            P("sec", "tile", None),
            P("sec", "tile", None, None),
        ),
        out_specs=(P(None, "sec", "tile", None), P(None, "sec", "tile", None, None)),
        check_vma=False,
    )
```

```python
import functools

import jax
import jax.numpy as jnp
from jax import lax
from jax.experimental import pallas as pl
from jax.experimental.pallas import tpu as pltpu
from jax.sharding import PartitionSpec as P

VM = pl.BlockSpec(memory_space=pltpu.VMEM)
SM = pl.BlockSpec(memory_space=pltpu.SMEM)
HB = pl.BlockSpec(memory_space=pltpu.HBM)


def halves(value):
    high = value.astype(jnp.bfloat16)
    low = (value - high.astype(jnp.float32)).astype(jnp.bfloat16)
    return high, low


def column_hot(cells, depth):
    at = lax.broadcasted_iota(jnp.int32, (depth, cells.shape[1]), 0)
    return jnp.where(at == (cells & (depth - 1)), 1.0, 0.0).astype(jnp.bfloat16)


def sample_kernel(GP, counts, flow, anchor, sampled, table, packed):
    partners, cap = anchor.shape
    total, depth = flow.shape
    comps = sampled.shape[1]
    rows = total // comps
    shift = depth.bit_length() - 1
    cap_shift = cap.bit_length() - 1
    lane = lax.broadcasted_iota(jnp.int32, (1, cap), 1)
    packed[...] = jnp.zeros_like(packed)

    def pack(p, base):
        begin = base & (cap - 1)
        spot = base >> cap_shift
        turned = pltpu.roll(anchor[pl.ds(p, 1), :], begin, 1)
        pltpu.store(packed.at[pl.ds(spot, 1), :], turned, mask=lane >= begin)
        pltpu.store(packed.at[pl.ds(spot + 1, 1), :], turned, mask=lane < begin)
        return base + counts[p]

    used = lax.fori_loop(0, partners, pack, 0, unroll=8)
    high, low = halves(flow[...])
    table[0:total] = high
    table[total:] = low

    def group(g, carry):
        first = g * GP
        cells = jnp.concatenate([packed[pl.ds(first + i, 1), :] for i in range(GP)], axis=1)
        hot = column_hot(cells, depth)
        picked = jnp.dot(table[...], hot, preferred_element_type=jnp.float32)
        row = lax.broadcasted_iota(jnp.int32, (rows, cells.shape[1]), 0) == (cells >> shift)
        parts = []
        for c in range(comps):
            both = picked[c * rows : (c + 1) * rows] + picked[total + c * rows : total + (c + 1) * rows]
            parts.append(jnp.sum(jnp.where(row, both, 0.0), axis=0, keepdims=True))
        found = jnp.concatenate(parts, axis=0)
        for i in range(GP):
            sampled[first + i] = found[:, i * cap : (i + 1) * cap]
        return carry

    lax.fori_loop(0, (used + GP * cap - 1) // (GP * cap), group, 0)


def sample(comps, counts, flow, anchor, GP=4):
    partners, cap = anchor.shape
    return pl.pallas_call(
        functools.partial(sample_kernel, GP),
        out_shape=jax.ShapeDtypeStruct((partners + 8, comps, cap), jnp.float32),
        in_specs=[SM, VM, VM],
        out_specs=VM,
        scratch_shapes=[
            pltpu.VMEM((2 * flow.shape[0], flow.shape[1]), jnp.bfloat16),
            pltpu.VMEM((partners + 8, cap), jnp.int32),
        ],
        compiler_params=pltpu.CompilerParams(vmem_limit_bytes=24 * 1024 * 1024),
        cost_estimate=pl.CostEstimate(flops=2 * 8192 * 512 * 1024, bytes_accessed=2**21, transcendentals=0),
        name="sample",
    )(counts, flow, anchor)


chunks = 4


def slip_kernel(counts, sampled, state, rate, mass, ports, near, across, opposite, far, out, whole, out_sems):
    comps, partners, cap = state.shape
    per = ports.shape[1]
    cap_shift = cap.bit_length() - 1
    last = near.shape[0] - 8
    lane = lax.broadcasted_iota(jnp.int32, (1, cap), 1)
    whole[:, 0:per] = ports[...]
    even = lax.axis_index("sec") % 2 == 0
    close = near[last : last + comps, 0:per]
    whole[:, per : 2 * per] = jnp.where(even, close, opposite[...])
    whole[:, 2 * per : 3 * per] = across[...]
    whole[:, 3 * per :] = jnp.where(even, opposite[...], close)

    def finish(p, base):
        n = counts[p]
        begin = base & (cap - 1)
        spot = base >> cap_shift
        both = jnp.where(lane >= begin, sampled[spot], sampled[spot + 1])
        value = pltpu.roll(both, (cap - begin) & (cap - 1), 1)
        own = jnp.concatenate([state[c, pl.ds(p, 1), :] for c in range(comps)], axis=0)
        r = rate[pl.ds(p, 1), :]
        drop = r * (own - value)
        live = lane < n
        out[3 * p] = jnp.where(live, own - drop, 0.0)
        out[3 * p + 1] = jnp.where(live, mass[pl.ds(p, 1), :] * drop, 0.0)
        out[3 * p + 2] = whole[...]
        return base + n

    block = partners // chunks
    base = 0
    copies = []
    for i in range(chunks):
        base = lax.fori_loop(i * block, (i + 1) * block, finish, base, unroll=8)
        part = pl.ds(3 * i * block, 3 * block)
        copies.append(pltpu.make_async_copy(out.at[part], far.at[part], out_sems.at[i]))
        copies[i].start()
    for copy in copies:
        copy.wait()


def slip(counts, sampled, state, rate, mass, ports, near, across, opposite):
    comps, partners, cap = state.shape
    return pl.pallas_call(
        slip_kernel,
        out_shape=jax.ShapeDtypeStruct((partners * 3, comps, cap), jnp.float32),
        in_specs=[SM] + [VM] * 8,
        out_specs=HB,
        scratch_shapes=[
            pltpu.VMEM((partners * 3, comps, cap), jnp.float32),
            pltpu.VMEM((comps, cap), jnp.float32),
            pltpu.SemaphoreType.DMA((chunks,)),
        ],
        compiler_params=pltpu.CompilerParams(vmem_limit_bytes=24 * 1024 * 1024),
        cost_estimate=pl.CostEstimate(flops=2 * 10**6, bytes_accessed=2**20, transcendentals=0),
        name="slip",
    )(counts, sampled, state, rate, mass, ports, near, across, opposite)


def land_kernel(GP, match, second, inlet_now, inlet, arrival, arrived, flow_far, state_far, flow_out, state_out, last_ref, last, packed, sem, out_sems):
    comps, partners, cap = state_out.shape
    total, depth = second.shape
    rows = total // comps
    shift = depth.bit_length() - 1
    cap_shift = cap.bit_length() - 1
    entries = match.shape[0]
    per = entries
    nt = (((1,), (1,)), ((), ()))
    slot = lax.broadcasted_iota(jnp.int32, (1, cap), 1)

    def ends(p, carry):
        moved = arrived[3 * p]
        gift = arrived[3 * p + 1]
        for c in range(comps):
            state_out[c, pl.ds(p, 1), :] = moved[c : c + 1]
        biggest = jnp.max(jnp.abs(gift), axis=0, keepdims=True)
        last_ref[pl.ds(p, 1), :] = jnp.where(biggest > 0.0, slot + 1, 0)
        return carry

    lax.fori_loop(0, partners, ends, 0, unroll=8)
    last_ref[partners:, :] = jnp.zeros_like(last_ref[partners:, :])
    top = jnp.max(last_ref[...].T, axis=0, keepdims=True)
    last_ref[0:1, :] = top
    fetch = pltpu.make_async_copy(last_ref.at[0:1, :], last, sem)
    fetch.start()
    state_copy = pltpu.make_async_copy(state_out, state_far, out_sems.at[2])
    state_copy.start()
    flow_out[...] = second[...]

    def add(cells, values, spot):
        row = lax.broadcasted_iota(jnp.int32, (rows, cells.shape[1]), 0) == (cells >> shift)
        high, low = halves(values)
        parts = []
        for part in (high.astype(jnp.float32), low.astype(jnp.float32)):
            for c in range(values.shape[0]):
                parts.append(jnp.where(row, part[c : c + 1], 0.0).astype(jnp.bfloat16))
        both = lax.dot_general(
            jnp.concatenate(parts, axis=0), column_hot(cells, depth), nt, preferred_element_type=jnp.float32
        )
        half = values.shape[0] * rows
        flow_out[spot : spot + half, :] += both[:half] + both[half:]

    section = lax.axis_index("sec")
    sections = cap // per
    target = jnp.zeros((comps, cap), jnp.float32)
    for k in range(entries):
        port = match[k]
        device = port // entries
        place = (device // partners + sections - section) % sections * per + port % entries
        turned = pltpu.roll(arrived[3 * (device % partners) + 2], (k + cap - place) % cap, 1)
        target = jnp.where(slot == k, turned, target)
    change = jnp.where(slot < entries, 0.5 * (target - inlet_now[...]), 0.0)
    packed[...] = jnp.zeros_like(packed)
    fetch.wait()

    def pack(p, base):
        begin = base & (cap - 1)
        spot = base >> cap_shift
        cells = arrival[pl.ds(p, 1), :].astype(jnp.float32)
        both = jnp.concatenate([arrived[3 * p + 1], jnp.broadcast_to(cells, (8 - comps, cap))], axis=0)
        turned = pltpu.roll(both, begin, 1)
        wide = lax.broadcasted_iota(jnp.int32, (8, cap), 1)
        pltpu.store(packed.at[spot], turned, mask=wide >= begin)
        pltpu.store(packed.at[spot + 1], turned, mask=wide < begin)
        return base + last[0, p]

    used = lax.fori_loop(0, partners, pack, 0, unroll=8)

    spare = (used + cap - 1) >> cap_shift
    cells = jnp.broadcast_to(inlet[0:1, :].astype(jnp.float32), (8 - comps, cap))
    packed[spare] = jnp.concatenate([change, cells], axis=0)

    def load(g):
        both = jnp.concatenate([packed[g * GP + i] for i in range(GP)], axis=1)
        return both[comps : comps + 1].astype(jnp.int32), both[:comps]

    def group(g, carry):
        cells, values = load(g)
        add(cells, values, 0)
        return carry

    final = spare // GP
    lax.fori_loop(0, final, group, 0)
    cells, values = load(final)
    half = comps // 2
    copies = []
    for i in range(2):
        part = pl.ds(i * half * rows, half * rows)
        add(cells, values[i * half : (i + 1) * half], i * half * rows)
        copies.append(pltpu.make_async_copy(flow_out.at[part, :], flow_far.at[part, :], out_sems.at[i]))
        copies[i].start()
    for copy in copies:
        copy.wait()
    state_copy.wait()


def land(match, second, inlet_now, inlet, arrival, arrived, GP=4):
    partners, cap = arrival.shape
    comps = arrived.shape[1]
    return pl.pallas_call(
        functools.partial(land_kernel, GP),
        out_shape=(
            jax.ShapeDtypeStruct(second.shape, jnp.float32),
            jax.ShapeDtypeStruct((comps, partners, cap), jnp.float32),
        ),
        in_specs=[SM] + [VM] * 5,
        out_specs=(HB, HB),
        scratch_shapes=[
            pltpu.VMEM(second.shape, jnp.float32),
            pltpu.VMEM((comps, partners, cap), jnp.float32),
            pltpu.VMEM((cap, cap), jnp.int32),
            pltpu.SMEM((1, cap), jnp.int32),
            pltpu.VMEM((partners + 8, 8, cap), jnp.float32),
            pltpu.SemaphoreType.DMA,
            pltpu.SemaphoreType.DMA((3,)),
        ],
        compiler_params=pltpu.CompilerParams(vmem_limit_bytes=24 * 1024 * 1024),
        cost_estimate=pl.CostEstimate(flops=2 * 8192 * 512 * 1024, bytes_accessed=2**21, transcendentals=0),
        name="land",
    )(match, second, inlet_now, inlet, arrival, arrived)


def tendency(plane, upper, lower, viscosity, keep):
    place = lax.broadcasted_iota(jnp.int32, (1, viscosity.shape[1]), 1)
    depth = viscosity.shape[1]
    centers, laps, dz, dx, dy = [], [], [], [], []
    for c in range(len(plane)):
        whole = plane[c]
        center = whole[:keep]
        up_x = pltpu.roll(whole, whole.shape[0] - 1, 0)[:keep]
        low_x = pltpu.roll(whole, 1, 0)[:keep]
        up_y = jnp.where(place == depth - 1, 0.0, pltpu.roll(center, depth - 1, 1))
        low_y = jnp.where(place == 0, 0.0, pltpu.roll(center, 1, 1))
        centers.append(center)
        laps.append((upper[c] + lower[c]) + (up_x + low_x) + (up_y + low_y) - 6.0 * center)
        dz.append(upper[c] - lower[c])
        dx.append(up_x - low_x)
        dy.append(up_y - low_y)
    strain = sum(d[c] * d[c] for c in range(3) for d in (dz, dx, dy)) * 0.25
    eddy = viscosity * (1.0 + strain / (1.0 + strain))
    out = []
    for c in range(len(plane)):
        carried = centers[0] * dz[c] + centers[1] * dx[c] + centers[2] * dy[c]
        out.append(0.5 * (eddy * laps[c]) - 0.25 * carried)
    return centers, out


def cap_kernel(comps, depth_z, width, flow, viscosity, ports, near_out, next_out):
    even = lax.axis_index("sec") % 2 == 0
    two = 2 * width
    last = depth_z * width

    def put(spot, count, low, high):
        near_out[spot : spot + count, :] = jnp.where(even, high, low)
        next_out[spot : spot + count, :] = jnp.where(even, low, high)

    for c in range(comps):
        put(c * two, two, flow[c * last : c * last + two, :], flow[(c + 1) * last - two : (c + 1) * last, :])
    base = comps * two
    put(base, width, viscosity[0:width, :], viscosity[last - width : last, :])
    for out in (near_out, next_out):
        out[base + width :, :] = jnp.zeros((8, out.shape[1]), jnp.float32)
        out[base + width : base + width + comps, 0 : ports.shape[1]] = ports[...]


def caps(comps, depth_z, width, flow, viscosity, ports):
    depth = flow.shape[1]
    cap = jax.ShapeDtypeStruct((2 * comps * width + width + 8, depth), jnp.float32)
    return pl.pallas_call(
        functools.partial(cap_kernel, comps, depth_z, width),
        out_shape=(cap, cap),
        in_specs=[VM] * 3,
        out_specs=(VM, VM),
        compiler_params=pltpu.CompilerParams(vmem_limit_bytes=60 * 1024 * 1024),
        name="caps",
    )(flow, viscosity, ports)


def edge_kernel(comps, depth_z, width, flow, viscosity, by_near, by_next, even_out, odd_out, bottom, top, low_out, high_out):
    section = lax.axis_index("sec")
    upper = section % 2 == 0
    near = by_near[0 : bottom.shape[0], :]
    beyond = by_next[0 : bottom.shape[0], :]
    bottom[...] = jnp.where(section > 0, jnp.where(upper, beyond, near), 0.0)
    top[...] = jnp.where(section < lax.axis_size("sec") - 1, jnp.where(upper, near, beyond), 0.0)
    two = 2 * width
    for k in range(comps * depth_z):
        low_out[2 * k : 2 * k + 2, :] = flow[k * width : k * width + 2, :]
        high_out[2 * k : 2 * k + 2, :] = flow[(k + 1) * width - 2 : (k + 1) * width, :]
    base = 2 * comps * depth_z
    for c in range(comps):
        low_out[base + 2 * c : base + 2 * c + 1, :] = bottom[c * two + width : c * two + width + 1, :]
        low_out[base + 2 * c + 1 : base + 2 * c + 2, :] = top[c * two : c * two + 1, :]
        high_out[base + 2 * c : base + 2 * c + 1, :] = bottom[(c + 1) * two - 1 : (c + 1) * two, :]
        high_out[base + 2 * c + 1 : base + 2 * c + 2, :] = top[c * two + width - 1 : c * two + width, :]
    base += 2 * comps
    for z in range(depth_z):
        low_out[base + z : base + z + 1, :] = viscosity[z * width : z * width + 1, :]
        high_out[base + z : base + z + 1, :] = viscosity[(z + 1) * width - 1 : (z + 1) * width, :]
    even = lax.axis_index("tile") % 2 == 0
    even_out[...] = jnp.where(even, high_out[...], low_out[...])
    odd_out[...] = jnp.where(even, low_out[...], high_out[...])


def edges(comps, depth_z, width, flow, viscosity, below, above):
    depth = flow.shape[1]
    shape = jax.ShapeDtypeStruct((2 * comps * (depth_z + 1) + depth_z, depth), jnp.float32)
    halo = jax.ShapeDtypeStruct(((2 * comps + 1) * width, depth), jnp.float32)
    return pl.pallas_call(
        functools.partial(edge_kernel, comps, depth_z, width),
        out_shape=(shape, shape, halo, halo),
        in_specs=[VM] * 4,
        out_specs=(VM,) * 4,
        scratch_shapes=[pltpu.VMEM(shape.shape, jnp.float32)] * 2,
        compiler_params=pltpu.CompilerParams(vmem_limit_bytes=24 * 1024 * 1024),
        name="edges",
    )(flow, viscosity, below, above)


def inner_kernel(comps, depth_z, width, flow, viscosity, below, above, first, middle):
    two = 2 * width

    def own(z):
        if z < 0:
            return [below[c * two + (2 + z) * width : c * two + (3 + z) * width, :] for c in range(comps)]
        if z >= depth_z:
            return [above[c * two + (z - depth_z) * width : c * two + (z - depth_z + 1) * width, :] for c in range(comps)]
        return [flow[(c * depth_z + z) * width : (c * depth_z + z + 1) * width, :] for c in range(comps)]

    for z in range(-1, depth_z + 1):
        if z < 0:
            visc = below[comps * two :, :]
        elif z == depth_z:
            visc = above[comps * two :, :]
        else:
            visc = viscosity[z * width : (z + 1) * width, :]
        centers, change = tendency(own(z), own(z + 1), own(z - 1), visc, width)
        for c in range(comps):
            first[c, z + 1, 0:width, :] = centers[c] + change[c]

    def second(z, carry):
        plane, upper, lower = ([first[c, z + 1 + d] for c in range(comps)] for d in (0, 1, -1))
        at = pl.multiple_of(z * width, width)
        centers, change = tendency(plane, upper, lower, viscosity[pl.ds(at, width), :], width)
        for c in range(comps):
            spot = pl.multiple_of((c * depth_z + z) * width, width)
            middle[pl.ds(spot, width), :] = 0.5 * flow[pl.ds(spot, width), :] + 0.5 * (centers[c] + change[c])
        return carry

    lax.fori_loop(0, depth_z, second, 0)


def inner(comps, depth_z, width, flow, viscosity, below, above):
    depth = flow.shape[1]
    return pl.pallas_call(
        functools.partial(inner_kernel, comps, depth_z, width),
        out_shape=(
            jax.ShapeDtypeStruct((comps, depth_z + 2, width, depth), jnp.float32),
            jax.ShapeDtypeStruct(flow.shape, jnp.float32),
        ),
        in_specs=[VM] * 4,
        out_specs=(VM, VM),
        compiler_params=pltpu.CompilerParams(vmem_limit_bytes=24 * 1024 * 1024),
        cost_estimate=pl.CostEstimate(flops=10**7, bytes_accessed=2**22, transcendentals=0),
        name="inner",
    )(flow, viscosity, below, above)


def outer_kernel(comps, depth_z, width, flow, viscosity, below, above, first, middle, by_odd, by_even, inlet, second_out, inlet_now, strip, visc, started, table):
    depth = flow.shape[1]
    two = 2 * width
    rows = depth_z * width
    total = comps * rows
    base = 2 * comps * depth_z
    tile = lax.axis_index("tile")

    even = tile % 2 == 0

    def from_left(spot, count):
        side = pl.ds(spot, count)
        return jnp.where(tile > 0, jnp.where(even, by_odd[side, :], by_even[side, :]), 0.0)

    def from_right(spot, count):
        side = pl.ds(spot, count)
        return jnp.where(tile < lax.axis_size("tile") - 1, jnp.where(even, by_even[side, :], by_odd[side, :]), 0.0)

    strip[...] = jnp.zeros_like(strip)
    visc[...] = jnp.zeros_like(visc)
    for c in range(comps):
        for z in range(-2, depth_z + 2):
            if z < 0:
                ref, spot = below, c * two + (2 + z) * width
            elif z >= depth_z:
                ref, spot = above, c * two + (z - depth_z) * width
            else:
                ref, spot = flow, (c * depth_z + z) * width
            strip[c, z + 2, 2:4, :] = ref[spot : spot + 2, :]
            strip[c, z + 2, 4:6, :] = ref[spot + width - 2 : spot + width, :]
            if 0 <= z < depth_z:
                k = 2 * (c * depth_z + z)
                strip[c, z + 2, 0:2, :] = from_left(k, 2)
                strip[c, z + 2, 6:8, :] = from_right(k, 2)
            elif z in (-1, depth_z):
                k = base + 2 * c + (z == depth_z)
                strip[c, z + 2, 1:2, :] = from_left(k, 1)
                strip[c, z + 2, 6:7, :] = from_right(k, 1)
    side = base + 2 * comps
    for z in range(-1, depth_z + 1):
        if z < 0:
            ref, spot = below, comps * two
        elif z == depth_z:
            ref, spot = above, comps * two
        else:
            ref, spot = viscosity, z * width
            visc[z + 1, 1:2, :] = from_left(side + z, 1)
            visc[z + 1, 6:7, :] = from_right(side + z, 1)
        visc[z + 1, 2:4, :] = ref[spot : spot + 2, :]
        visc[z + 1, 4:6, :] = ref[spot + width - 2 : spot + width, :]

    place = lax.broadcasted_iota(jnp.int32, (8, 1), 0)

    def apart(value):
        return jnp.where(place < 4, pltpu.roll(value, 7, 0), pltpu.roll(value, 1, 0))

    def one(z, carry):
        plane, upper, lower = ([strip[c, z + 1 + d] for c in range(comps)] for d in (0, 1, -1))
        centers, change = tendency(plane, upper, lower, visc[z], 8)
        for c in range(comps):
            ends = apart(centers[c] + change[c])
            near = jnp.where(place < 4, pltpu.roll(first[c, z, 0:8, :], 1, 0), pltpu.roll(first[c, z, width - 8 : width, :], 7, 0))
            started[c, z] = jnp.where((place < 2) | (place > 5), ends, near)
        return carry

    lax.fori_loop(0, depth_z + 2, one, 0, unroll=2)

    def second(z, carry):
        plane, upper, lower = ([started[c, z + 1 + d] for c in range(comps)] for d in (0, 1, -1))
        centers, change = tendency(plane, upper, lower, apart(visc[z + 1]), 8)
        for c in range(comps):
            spot = pl.multiple_of((c * depth_z + z) * width, width)
            edge = 0.5 * apart(strip[c, z + 2]) + 0.5 * (centers[c] + change[c])
            mine = middle[pl.ds(spot, width), :]
            top = jnp.where(place < 2, pltpu.roll(edge, 7, 0), mine[0:8])
            end = jnp.where(place > 5, pltpu.roll(edge, 1, 0), mine[width - 8 :])
            value = jnp.concatenate([top, mine[8 : width - 8], end] if width > 16 else [top, end], axis=0)
            second_out[pl.ds(spot, width), :] = value
            high, low = halves(value)
            table[pl.ds(spot, width), :] = high
            table[pl.ds(total + spot, width), :] = low
        return carry

    lax.fori_loop(0, depth_z, second, 0, unroll=2)

    cells = inlet[0:1, :]
    picked = jnp.dot(table[...], column_hot(cells, depth), preferred_element_type=jnp.float32)
    row = lax.broadcasted_iota(jnp.int32, (rows, cells.shape[1]), 0) == (cells >> (depth.bit_length() - 1))
    for c in range(comps):
        both = picked[c * rows : (c + 1) * rows] + picked[total + c * rows : total + (c + 1) * rows]
        inlet_now[c : c + 1, :] = jnp.sum(jnp.where(row, both, 0.0), axis=0, keepdims=True)


def outer(comps, depth_z, width, flow, viscosity, below, above, first, middle, left, right, inlet):
    depth = flow.shape[1]
    return pl.pallas_call(
        functools.partial(outer_kernel, comps, depth_z, width),
        out_shape=(
            jax.ShapeDtypeStruct(flow.shape, jnp.float32),
            jax.ShapeDtypeStruct((comps, inlet.shape[1]), jnp.float32),
        ),
        in_specs=[VM] * 9,
        out_specs=(VM, VM),
        scratch_shapes=[
            pltpu.VMEM((comps, depth_z + 4, 8, depth), jnp.float32),
            pltpu.VMEM((depth_z + 2, 8, depth), jnp.float32),
            pltpu.VMEM((comps, depth_z + 2, 8, depth), jnp.float32),
            pltpu.VMEM((2 * flow.shape[0], depth), jnp.bfloat16),
        ],
        compiler_params=pltpu.CompilerParams(vmem_limit_bytes=24 * 1024 * 1024),
        cost_estimate=pl.CostEstimate(flops=10**7, bytes_accessed=2**22, transcendentals=0),
        name="outer",
    )(flow, viscosity, below, above, first, middle, left, right, inlet)


def on_device(
    flow_field,
    viscosity,
    port_plane,
    port_match,
    inlet_cell,
    inclusion_state,
    response_rate,
    inclusion_mass,
    anchor_cell,
    live_counts,
    arrival_cell,
):
    comps, depth_z, width, depth = flow_field.shape
    partners, cap = anchor_cell.shape[2:]
    sizes = (comps, depth_z, width)
    flow = flow_field.reshape(-1, depth)
    visc = viscosity.reshape(-1, depth)
    count = lax.axis_size("tile")
    even_pairs = [(i, i ^ 1) for i in range(count)]
    odd_pairs = [(0, 0), (count - 1, count - 1)] + [(i, ((i + 1) ^ 1) - 1) for i in range(1, count - 1)]
    levels = lax.axis_size("sec")
    near_pairs = [(i, i ^ 1) for i in range(levels)]
    next_pairs = [(0, 0), (levels - 1, levels - 1)] + [(i, ((i + 1) ^ 1) - 1) for i in range(1, levels - 1)]

    near_cap, next_cap = caps(*sizes, flow, visc, port_plane)
    by_near = lax.ppermute(near_cap, "sec", near_pairs)
    by_next = lax.ppermute(next_cap, "sec", next_pairs)
    across = lax.ppermute(port_plane, "sec", [(i, (i + levels // 2) % levels) for i in range(levels)])
    opposite = lax.ppermute(port_plane, "sec", [(i, levels - 1 - i) for i in range(levels)])
    counts = live_counts.reshape(-1)
    counts, near_cap, next_cap = lax.optimization_barrier((counts, near_cap, next_cap))
    sampled = sample(comps, counts, flow, anchor_cell.reshape(partners, cap))
    outgoing = slip(
        counts,
        sampled,
        inclusion_state.reshape(comps, partners, cap),
        response_rate.reshape(partners, cap),
        inclusion_mass.reshape(partners, cap),
        port_plane,
        by_near,
        across,
        opposite,
    )
    by_near, by_next, outgoing = lax.optimization_barrier((by_near, by_next, outgoing))
    arrived = lax.all_to_all(outgoing, "tile", split_axis=0, concat_axis=0, tiled=True)
    even_edge, odd_edge, bottom, top = edges(*sizes, flow, visc, by_near, by_next)
    by_odd = lax.ppermute(odd_edge, "tile", odd_pairs)
    by_even = lax.ppermute(even_edge, "tile", even_pairs)
    inlet = jnp.pad(inlet_cell.reshape(1, -1), ((0, 0), (0, cap - inlet_cell.shape[0])))
    first, middle = inner(*sizes, flow, visc, bottom, top)
    second, inlet_now = outer(*sizes, flow, visc, bottom, top, first, middle, by_odd, by_even, inlet)
    flow_next, arrived_state = land(
        port_match, second, inlet_now, inlet, arrival_cell.reshape(partners, cap), arrived
    )
    return flow_next.reshape(flow_field.shape), arrived_state.reshape(inclusion_state.shape)


def solution(mesh):
    return jax.shard_map(
        on_device,
        mesh=mesh,
        in_specs=(
            P(None, "sec", "tile", None),
            P("sec", "tile", None),
            P(None, ("sec", "tile")),
            P(("sec", "tile")),
            P(("sec", "tile")),
            P(None, "sec", "tile", None, None),
            P("sec", "tile", None, None),
            P("sec", "tile", None, None),
            P("sec", "tile", None, None),
            P("sec", "tile", None),
            P("sec", "tile", None, None),
        ),
        out_specs=(P(None, "sec", "tile", None), P(None, "sec", "tile", None, None)),
        check_vma=False,
    )
```

```python
import functools

import jax
import jax.numpy as jnp
from jax import lax
from jax.experimental import pallas as pl
from jax.experimental.pallas import tpu as pltpu
from jax.sharding import PartitionSpec as P

VM = pl.BlockSpec(memory_space=pltpu.VMEM)
SM = pl.BlockSpec(memory_space=pltpu.SMEM)
HB = pl.BlockSpec(memory_space=pltpu.HBM)


def halves(value):
    high = value.astype(jnp.bfloat16)
    low = (value - high.astype(jnp.float32)).astype(jnp.bfloat16)
    return high, low


def column_hot(cells, depth):
    at = lax.broadcasted_iota(jnp.int32, (depth, cells.shape[1]), 0)
    return jnp.where(at == (cells & (depth - 1)), 1.0, 0.0).astype(jnp.bfloat16)


def sample_kernel(GP, counts, flow, anchor, sampled, table, packed):
    partners, cap = anchor.shape
    total, depth = flow.shape
    comps = sampled.shape[1]
    rows = total // comps
    shift = depth.bit_length() - 1
    cap_shift = cap.bit_length() - 1
    lane = lax.broadcasted_iota(jnp.int32, (1, cap), 1)
    packed[...] = jnp.zeros_like(packed)

    def pack(p, base):
        begin = base & (cap - 1)
        spot = base >> cap_shift
        turned = pltpu.roll(anchor[pl.ds(p, 1), :], begin, 1)
        pltpu.store(packed.at[pl.ds(spot, 1), :], turned, mask=lane >= begin)
        pltpu.store(packed.at[pl.ds(spot + 1, 1), :], turned, mask=lane < begin)
        return base + counts[p]

    used = lax.fori_loop(0, partners, pack, 0, unroll=16)
    high, low = halves(flow[...])
    table[0:total] = high
    table[total:] = low

    def group(g, carry):
        first = g * GP
        cells = jnp.concatenate([packed[pl.ds(first + i, 1), :] for i in range(GP)], axis=1)
        hot = column_hot(cells, depth)
        picked = jnp.dot(table[...], hot, preferred_element_type=jnp.float32)
        row = lax.broadcasted_iota(jnp.int32, (rows, cells.shape[1]), 0) == (cells >> shift)
        parts = []
        for c in range(comps):
            both = picked[c * rows : (c + 1) * rows] + picked[total + c * rows : total + (c + 1) * rows]
            parts.append(jnp.sum(jnp.where(row, both, 0.0), axis=0, keepdims=True))
        found = jnp.concatenate(parts, axis=0)
        for i in range(GP):
            sampled[first + i] = found[:, i * cap : (i + 1) * cap]
        return carry

    lax.fori_loop(0, (used + GP * cap - 1) // (GP * cap), group, 0)


def sample(comps, counts, flow, anchor, GP=4):
    partners, cap = anchor.shape
    return pl.pallas_call(
        functools.partial(sample_kernel, GP),
        out_shape=jax.ShapeDtypeStruct((partners + 8, comps, cap), jnp.float32),
        in_specs=[SM, VM, VM],
        out_specs=VM,
        scratch_shapes=[
            pltpu.VMEM((2 * flow.shape[0], flow.shape[1]), jnp.bfloat16),
            pltpu.VMEM((partners + 8, cap), jnp.int32),
        ],
        compiler_params=pltpu.CompilerParams(vmem_limit_bytes=24 * 1024 * 1024),
        cost_estimate=pl.CostEstimate(flops=2 * 8192 * 512 * 1024, bytes_accessed=2**21, transcendentals=0),
        name="sample",
    )(counts, flow, anchor)


chunks = 4


def slip_kernel(counts, sampled, state, rate, mass, ports, near, across, opposite, far, out, whole, out_sems):
    comps, partners, cap = state.shape
    per = ports.shape[1]
    cap_shift = cap.bit_length() - 1
    last = near.shape[0] - 8
    lane = lax.broadcasted_iota(jnp.int32, (1, cap), 1)
    whole[:, 0:per] = ports[...]
    even = lax.axis_index("sec") % 2 == 0
    close = near[last : last + comps, 0:per]
    whole[:, per : 2 * per] = jnp.where(even, close, opposite[...])
    whole[:, 2 * per : 3 * per] = across[...]
    whole[:, 3 * per :] = jnp.where(even, opposite[...], close)

    def finish(p, base):
        n = counts[p]
        begin = base & (cap - 1)
        spot = base >> cap_shift
        both = jnp.where(lane >= begin, sampled[spot], sampled[spot + 1])
        value = pltpu.roll(both, (cap - begin) & (cap - 1), 1)
        own = jnp.concatenate([state[c, pl.ds(p, 1), :] for c in range(comps)], axis=0)
        r = rate[pl.ds(p, 1), :]
        drop = r * (own - value)
        live = lane < n
        out[3 * p] = jnp.where(live, own - drop, 0.0)
        out[3 * p + 1] = jnp.where(live, mass[pl.ds(p, 1), :] * drop, 0.0)
        out[3 * p + 2] = whole[...]
        return base + n

    block = partners // chunks
    base = 0
    copies = []
    for i in range(chunks):
        base = lax.fori_loop(i * block, (i + 1) * block, finish, base, unroll=16)
        part = pl.ds(3 * i * block, 3 * block)
        copies.append(pltpu.make_async_copy(out.at[part], far.at[part], out_sems.at[i]))
        copies[i].start()
    for copy in copies:
        copy.wait()


def slip(counts, sampled, state, rate, mass, ports, near, across, opposite):
    comps, partners, cap = state.shape
    return pl.pallas_call(
        slip_kernel,
        out_shape=jax.ShapeDtypeStruct((partners * 3, comps, cap), jnp.float32),
        in_specs=[SM] + [VM] * 8,
        out_specs=HB,
        scratch_shapes=[
            pltpu.VMEM((partners * 3, comps, cap), jnp.float32),
            pltpu.VMEM((comps, cap), jnp.float32),
            pltpu.SemaphoreType.DMA((chunks,)),
        ],
        compiler_params=pltpu.CompilerParams(vmem_limit_bytes=24 * 1024 * 1024),
        cost_estimate=pl.CostEstimate(flops=2 * 10**6, bytes_accessed=2**20, transcendentals=0),
        name="slip",
    )(counts, sampled, state, rate, mass, ports, near, across, opposite)


def land_kernel(GP, match, second, inlet_now, inlet, arrival, arrived, flow_far, state_far, flow_out, state_out, last_ref, last, packed, sem, out_sems):
    comps, partners, cap = state_out.shape
    total, depth = second.shape
    rows = total // comps
    shift = depth.bit_length() - 1
    cap_shift = cap.bit_length() - 1
    entries = match.shape[0]
    per = entries
    nt = (((1,), (1,)), ((), ()))
    slot = lax.broadcasted_iota(jnp.int32, (1, cap), 1)

    def ends(p, carry):
        moved = arrived[3 * p]
        gift = arrived[3 * p + 1]
        for c in range(comps):
            state_out[c, pl.ds(p, 1), :] = moved[c : c + 1]
        biggest = jnp.max(jnp.abs(gift), axis=0, keepdims=True)
        last_ref[pl.ds(p, 1), :] = jnp.where(biggest > 0.0, slot + 1, 0)
        return carry

    lax.fori_loop(0, partners, ends, 0, unroll=16)
    last_ref[partners:, :] = jnp.zeros_like(last_ref[partners:, :])
    top = jnp.max(last_ref[...].T, axis=0, keepdims=True)
    last_ref[0:1, :] = top
    fetch = pltpu.make_async_copy(last_ref.at[0:1, :], last, sem)
    fetch.start()
    state_copy = pltpu.make_async_copy(state_out, state_far, out_sems.at[2])
    state_copy.start()
    flow_out[...] = second[...]

    def add(cells, values, spot):
        row = lax.broadcasted_iota(jnp.int32, (rows, cells.shape[1]), 0) == (cells >> shift)
        high, low = halves(values)
        parts = []
        for part in (high.astype(jnp.float32), low.astype(jnp.float32)):
            for c in range(values.shape[0]):
                parts.append(jnp.where(row, part[c : c + 1], 0.0).astype(jnp.bfloat16))
        both = lax.dot_general(
            jnp.concatenate(parts, axis=0), column_hot(cells, depth), nt, preferred_element_type=jnp.float32
        )
        half = values.shape[0] * rows
        flow_out[spot : spot + half, :] += both[:half] + both[half:]

    section = lax.axis_index("sec")
    sections = cap // per
    target = jnp.zeros((comps, cap), jnp.float32)
    for k in range(entries):
        port = match[k]
        device = port // entries
        place = (device // partners + sections - section) % sections * per + port % entries
        turned = pltpu.roll(arrived[3 * (device % partners) + 2], (k + cap - place) % cap, 1)
        target = jnp.where(slot == k, turned, target)
    change = jnp.where(slot < entries, 0.5 * (target - inlet_now[...]), 0.0)
    packed[...] = jnp.zeros_like(packed)
    fetch.wait()

    def pack(p, base):
        begin = base & (cap - 1)
        spot = base >> cap_shift
        cells = arrival[pl.ds(p, 1), :].astype(jnp.float32)
        both = jnp.concatenate([arrived[3 * p + 1], jnp.broadcast_to(cells, (8 - comps, cap))], axis=0)
        turned = pltpu.roll(both, begin, 1)
        wide = lax.broadcasted_iota(jnp.int32, (8, cap), 1)
        pltpu.store(packed.at[spot], turned, mask=wide >= begin)
        pltpu.store(packed.at[spot + 1], turned, mask=wide < begin)
        return base + last[0, p]

    used = lax.fori_loop(0, partners, pack, 0, unroll=16)

    spare = (used + cap - 1) >> cap_shift
    cells = jnp.broadcast_to(inlet[0:1, :].astype(jnp.float32), (8 - comps, cap))
    packed[spare] = jnp.concatenate([change, cells], axis=0)

    def load(g):
        both = jnp.concatenate([packed[g * GP + i] for i in range(GP)], axis=1)
        return both[comps : comps + 1].astype(jnp.int32), both[:comps]

    def group(g, carry):
        cells, values = load(g)
        add(cells, values, 0)
        return carry

    final = spare // GP
    lax.fori_loop(0, final, group, 0)
    cells, values = load(final)
    half = comps // 2
    copies = []
    for i in range(2):
        part = pl.ds(i * half * rows, half * rows)
        add(cells, values[i * half : (i + 1) * half], i * half * rows)
        copies.append(pltpu.make_async_copy(flow_out.at[part, :], flow_far.at[part, :], out_sems.at[i]))
        copies[i].start()
    for copy in copies:
        copy.wait()
    state_copy.wait()


def land(match, second, inlet_now, inlet, arrival, arrived, GP=4):
    partners, cap = arrival.shape
    comps = arrived.shape[1]
    return pl.pallas_call(
        functools.partial(land_kernel, GP),
        out_shape=(
            jax.ShapeDtypeStruct(second.shape, jnp.float32),
            jax.ShapeDtypeStruct((comps, partners, cap), jnp.float32),
        ),
        in_specs=[SM] + [VM] * 5,
        out_specs=(HB, HB),
        scratch_shapes=[
            pltpu.VMEM(second.shape, jnp.float32),
            pltpu.VMEM((comps, partners, cap), jnp.float32),
            pltpu.VMEM((cap, cap), jnp.int32),
            pltpu.SMEM((1, cap), jnp.int32),
            pltpu.VMEM((partners + 8, 8, cap), jnp.float32),
            pltpu.SemaphoreType.DMA,
            pltpu.SemaphoreType.DMA((3,)),
        ],
        compiler_params=pltpu.CompilerParams(vmem_limit_bytes=24 * 1024 * 1024),
        cost_estimate=pl.CostEstimate(flops=2 * 8192 * 512 * 1024, bytes_accessed=2**21, transcendentals=0),
        name="land",
    )(match, second, inlet_now, inlet, arrival, arrived)


def tendency(plane, upper, lower, viscosity, keep):
    place = lax.broadcasted_iota(jnp.int32, (1, viscosity.shape[1]), 1)
    depth = viscosity.shape[1]
    centers, laps, dz, dx, dy = [], [], [], [], []
    for c in range(len(plane)):
        whole = plane[c]
        center = whole[:keep]
        up_x = pltpu.roll(whole, whole.shape[0] - 1, 0)[:keep]
        low_x = pltpu.roll(whole, 1, 0)[:keep]
        up_y = jnp.where(place == depth - 1, 0.0, pltpu.roll(center, depth - 1, 1))
        low_y = jnp.where(place == 0, 0.0, pltpu.roll(center, 1, 1))
        centers.append(center)
        laps.append((upper[c] + lower[c]) + (up_x + low_x) + (up_y + low_y) - 6.0 * center)
        dz.append(upper[c] - lower[c])
        dx.append(up_x - low_x)
        dy.append(up_y - low_y)
    strain = sum(d[c] * d[c] for c in range(3) for d in (dz, dx, dy)) * 0.25
    eddy = viscosity * (1.0 + strain / (1.0 + strain))
    out = []
    for c in range(len(plane)):
        carried = centers[0] * dz[c] + centers[1] * dx[c] + centers[2] * dy[c]
        out.append(0.5 * (eddy * laps[c]) - 0.25 * carried)
    return centers, out


def cap_kernel(comps, depth_z, width, flow, viscosity, ports, near_out, next_out):
    even = lax.axis_index("sec") % 2 == 0
    two = 2 * width
    last = depth_z * width

    def put(spot, count, low, high):
        near_out[spot : spot + count, :] = jnp.where(even, high, low)
        next_out[spot : spot + count, :] = jnp.where(even, low, high)

    for c in range(comps):
        put(c * two, two, flow[c * last : c * last + two, :], flow[(c + 1) * last - two : (c + 1) * last, :])
    base = comps * two
    put(base, width, viscosity[0:width, :], viscosity[last - width : last, :])
    for out in (near_out, next_out):
        out[base + width :, :] = jnp.zeros((8, out.shape[1]), jnp.float32)
        out[base + width : base + width + comps, 0 : ports.shape[1]] = ports[...]


def caps(comps, depth_z, width, flow, viscosity, ports):
    depth = flow.shape[1]
    cap = jax.ShapeDtypeStruct((2 * comps * width + width + 8, depth), jnp.float32)
    return pl.pallas_call(
        functools.partial(cap_kernel, comps, depth_z, width),
        out_shape=(cap, cap),
        in_specs=[VM] * 3,
        out_specs=(VM, VM),
        compiler_params=pltpu.CompilerParams(vmem_limit_bytes=60 * 1024 * 1024),
        name="caps",
    )(flow, viscosity, ports)


def edge_kernel(comps, depth_z, width, flow, viscosity, by_near, by_next, even_out, odd_out, bottom, top, low_out, high_out):
    section = lax.axis_index("sec")
    upper = section % 2 == 0
    near = by_near[0 : bottom.shape[0], :]
    beyond = by_next[0 : bottom.shape[0], :]
    bottom[...] = jnp.where(section > 0, jnp.where(upper, beyond, near), 0.0)
    top[...] = jnp.where(section < lax.axis_size("sec") - 1, jnp.where(upper, near, beyond), 0.0)
    two = 2 * width
    for k in range(comps * depth_z):
        low_out[2 * k : 2 * k + 2, :] = flow[k * width : k * width + 2, :]
        high_out[2 * k : 2 * k + 2, :] = flow[(k + 1) * width - 2 : (k + 1) * width, :]
    base = 2 * comps * depth_z
    for c in range(comps):
        low_out[base + 2 * c : base + 2 * c + 1, :] = bottom[c * two + width : c * two + width + 1, :]
        low_out[base + 2 * c + 1 : base + 2 * c + 2, :] = top[c * two : c * two + 1, :]
        high_out[base + 2 * c : base + 2 * c + 1, :] = bottom[(c + 1) * two - 1 : (c + 1) * two, :]
        high_out[base + 2 * c + 1 : base + 2 * c + 2, :] = top[c * two + width - 1 : c * two + width, :]
    base += 2 * comps
    for z in range(depth_z):
        low_out[base + z : base + z + 1, :] = viscosity[z * width : z * width + 1, :]
        high_out[base + z : base + z + 1, :] = viscosity[(z + 1) * width - 1 : (z + 1) * width, :]
    even = lax.axis_index("tile") % 2 == 0
    even_out[...] = jnp.where(even, high_out[...], low_out[...])
    odd_out[...] = jnp.where(even, low_out[...], high_out[...])


def edges(comps, depth_z, width, flow, viscosity, below, above):
    depth = flow.shape[1]
    shape = jax.ShapeDtypeStruct((2 * comps * (depth_z + 1) + depth_z, depth), jnp.float32)
    halo = jax.ShapeDtypeStruct(((2 * comps + 1) * width, depth), jnp.float32)
    return pl.pallas_call(
        functools.partial(edge_kernel, comps, depth_z, width),
        out_shape=(shape, shape, halo, halo),
        in_specs=[VM] * 4,
        out_specs=(VM,) * 4,
        scratch_shapes=[pltpu.VMEM(shape.shape, jnp.float32)] * 2,
        compiler_params=pltpu.CompilerParams(vmem_limit_bytes=24 * 1024 * 1024),
        name="edges",
    )(flow, viscosity, below, above)


def inner_kernel(comps, depth_z, width, flow, viscosity, below, above, first, middle):
    two = 2 * width

    def own(z):
        if z < 0:
            return [below[c * two + (2 + z) * width : c * two + (3 + z) * width, :] for c in range(comps)]
        if z >= depth_z:
            return [above[c * two + (z - depth_z) * width : c * two + (z - depth_z + 1) * width, :] for c in range(comps)]
        return [flow[(c * depth_z + z) * width : (c * depth_z + z + 1) * width, :] for c in range(comps)]

    for z in range(-1, depth_z + 1):
        if z < 0:
            visc = below[comps * two :, :]
        elif z == depth_z:
            visc = above[comps * two :, :]
        else:
            visc = viscosity[z * width : (z + 1) * width, :]
        centers, change = tendency(own(z), own(z + 1), own(z - 1), visc, width)
        for c in range(comps):
            first[c, z + 1, 0:width, :] = centers[c] + change[c]

    def second(z, carry):
        plane, upper, lower = ([first[c, z + 1 + d] for c in range(comps)] for d in (0, 1, -1))
        at = pl.multiple_of(z * width, width)
        centers, change = tendency(plane, upper, lower, viscosity[pl.ds(at, width), :], width)
        for c in range(comps):
            spot = pl.multiple_of((c * depth_z + z) * width, width)
            middle[pl.ds(spot, width), :] = 0.5 * flow[pl.ds(spot, width), :] + 0.5 * (centers[c] + change[c])
        return carry

    lax.fori_loop(0, depth_z, second, 0)


def inner(comps, depth_z, width, flow, viscosity, below, above):
    depth = flow.shape[1]
    return pl.pallas_call(
        functools.partial(inner_kernel, comps, depth_z, width),
        out_shape=(
            jax.ShapeDtypeStruct((comps, depth_z + 2, width, depth), jnp.float32),
            jax.ShapeDtypeStruct(flow.shape, jnp.float32),
        ),
        in_specs=[VM] * 4,
        out_specs=(VM, VM),
        compiler_params=pltpu.CompilerParams(vmem_limit_bytes=24 * 1024 * 1024),
        cost_estimate=pl.CostEstimate(flops=10**7, bytes_accessed=2**22, transcendentals=0),
        name="inner",
    )(flow, viscosity, below, above)


def outer_kernel(comps, depth_z, width, flow, viscosity, below, above, first, middle, by_even, by_odd, inlet, second_out, inlet_now, strip, visc, started, table):
    depth = flow.shape[1]
    two = 2 * width
    rows = depth_z * width
    total = comps * rows
    base = 2 * comps * depth_z
    tile = lax.axis_index("tile")

    even = tile % 2 == 0

    def from_left(spot, count):
        side = pl.ds(spot, count)
        return jnp.where(tile > 0, jnp.where(even, by_odd[side, :], by_even[side, :]), 0.0)

    def from_right(spot, count):
        side = pl.ds(spot, count)
        return jnp.where(tile < lax.axis_size("tile") - 1, jnp.where(even, by_even[side, :], by_odd[side, :]), 0.0)

    strip[...] = jnp.zeros_like(strip)
    visc[...] = jnp.zeros_like(visc)
    for c in range(comps):
        for z in range(-2, depth_z + 2):
            if z < 0:
                ref, spot = below, c * two + (2 + z) * width
            elif z >= depth_z:
                ref, spot = above, c * two + (z - depth_z) * width
            else:
                ref, spot = flow, (c * depth_z + z) * width
            strip[c, z + 2, 2:4, :] = ref[spot : spot + 2, :]
            strip[c, z + 2, 4:6, :] = ref[spot + width - 2 : spot + width, :]
            if 0 <= z < depth_z:
                k = 2 * (c * depth_z + z)
                strip[c, z + 2, 0:2, :] = from_left(k, 2)
                strip[c, z + 2, 6:8, :] = from_right(k, 2)
            elif z in (-1, depth_z):
                k = base + 2 * c + (z == depth_z)
                strip[c, z + 2, 1:2, :] = from_left(k, 1)
                strip[c, z + 2, 6:7, :] = from_right(k, 1)
    side = base + 2 * comps
    for z in range(-1, depth_z + 1):
        if z < 0:
            ref, spot = below, comps * two
        elif z == depth_z:
            ref, spot = above, comps * two
        else:
            ref, spot = viscosity, z * width
            visc[z + 1, 1:2, :] = from_left(side + z, 1)
            visc[z + 1, 6:7, :] = from_right(side + z, 1)
        visc[z + 1, 2:4, :] = ref[spot : spot + 2, :]
        visc[z + 1, 4:6, :] = ref[spot + width - 2 : spot + width, :]

    place = lax.broadcasted_iota(jnp.int32, (8, 1), 0)

    def apart(value):
        return jnp.where(place < 4, pltpu.roll(value, 7, 0), pltpu.roll(value, 1, 0))

    def one(z, carry):
        plane, upper, lower = ([strip[c, z + 1 + d] for c in range(comps)] for d in (0, 1, -1))
        centers, change = tendency(plane, upper, lower, visc[z], 8)
        for c in range(comps):
            ends = apart(centers[c] + change[c])
            near = jnp.where(place < 4, pltpu.roll(first[c, z, 0:8, :], 1, 0), pltpu.roll(first[c, z, width - 8 : width, :], 7, 0))
            started[c, z] = jnp.where((place < 2) | (place > 5), ends, near)
        return carry

    lax.fori_loop(0, depth_z + 2, one, 0, unroll=2)

    def second(z, carry):
        plane, upper, lower = ([started[c, z + 1 + d] for c in range(comps)] for d in (0, 1, -1))
        centers, change = tendency(plane, upper, lower, apart(visc[z + 1]), 8)
        for c in range(comps):
            spot = pl.multiple_of((c * depth_z + z) * width, width)
            edge = 0.5 * apart(strip[c, z + 2]) + 0.5 * (centers[c] + change[c])
            mine = middle[pl.ds(spot, width), :]
            top = jnp.where(place < 2, pltpu.roll(edge, 7, 0), mine[0:8])
            end = jnp.where(place > 5, pltpu.roll(edge, 1, 0), mine[width - 8 :])
            value = jnp.concatenate([top, mine[8 : width - 8], end] if width > 16 else [top, end], axis=0)
            second_out[pl.ds(spot, width), :] = value
            high, low = halves(value)
            table[pl.ds(spot, width), :] = high
            table[pl.ds(total + spot, width), :] = low
        return carry

    lax.fori_loop(0, depth_z, second, 0, unroll=2)

    cells = inlet[0:1, :]
    picked = jnp.dot(table[...], column_hot(cells, depth), preferred_element_type=jnp.float32)
    row = lax.broadcasted_iota(jnp.int32, (rows, cells.shape[1]), 0) == (cells >> (depth.bit_length() - 1))
    for c in range(comps):
        both = picked[c * rows : (c + 1) * rows] + picked[total + c * rows : total + (c + 1) * rows]
        inlet_now[c : c + 1, :] = jnp.sum(jnp.where(row, both, 0.0), axis=0, keepdims=True)


def outer(comps, depth_z, width, flow, viscosity, below, above, first, middle, left, right, inlet):
    depth = flow.shape[1]
    return pl.pallas_call(
        functools.partial(outer_kernel, comps, depth_z, width),
        out_shape=(
            jax.ShapeDtypeStruct(flow.shape, jnp.float32),
            jax.ShapeDtypeStruct((comps, inlet.shape[1]), jnp.float32),
        ),
        in_specs=[VM] * 9,
        out_specs=(VM, VM),
        scratch_shapes=[
            pltpu.VMEM((comps, depth_z + 4, 8, depth), jnp.float32),
            pltpu.VMEM((depth_z + 2, 8, depth), jnp.float32),
            pltpu.VMEM((comps, depth_z + 2, 8, depth), jnp.float32),
            pltpu.VMEM((2 * flow.shape[0], depth), jnp.bfloat16),
        ],
        compiler_params=pltpu.CompilerParams(vmem_limit_bytes=24 * 1024 * 1024),
        cost_estimate=pl.CostEstimate(flops=10**7, bytes_accessed=2**22, transcendentals=0),
        name="outer",
    )(flow, viscosity, below, above, first, middle, left, right, inlet)


def on_device(
    flow_field,
    viscosity,
    port_plane,
    port_match,
    inlet_cell,
    inclusion_state,
    response_rate,
    inclusion_mass,
    anchor_cell,
    live_counts,
    arrival_cell,
):
    comps, depth_z, width, depth = flow_field.shape
    partners, cap = anchor_cell.shape[2:]
    sizes = (comps, depth_z, width)
    flow = flow_field.reshape(-1, depth)
    visc = viscosity.reshape(-1, depth)
    count = lax.axis_size("tile")
    even_pairs = [(i, i ^ 1) for i in range(count)]
    odd_pairs = [(0, 0), (count - 1, count - 1)] + [(i, ((i + 1) ^ 1) - 1) for i in range(1, count - 1)]
    levels = lax.axis_size("sec")
    near_pairs = [(i, i ^ 1) for i in range(levels)]
    next_pairs = [(0, 0), (levels - 1, levels - 1)] + [(i, ((i + 1) ^ 1) - 1) for i in range(1, levels - 1)]

    near_cap, next_cap = caps(*sizes, flow, visc, port_plane)
    by_near = lax.ppermute(near_cap, "sec", near_pairs)
    by_next = lax.ppermute(next_cap, "sec", next_pairs)
    across = lax.ppermute(port_plane, "sec", [(i, (i + levels // 2) % levels) for i in range(levels)])
    opposite = lax.ppermute(port_plane, "sec", [(i, levels - 1 - i) for i in range(levels)])
    counts = live_counts.reshape(-1)
    counts, near_cap, next_cap = lax.optimization_barrier((counts, near_cap, next_cap))
    sampled = sample(comps, counts, flow, anchor_cell.reshape(partners, cap))
    outgoing = slip(
        counts,
        sampled,
        inclusion_state.reshape(comps, partners, cap),
        response_rate.reshape(partners, cap),
        inclusion_mass.reshape(partners, cap),
        port_plane,
        by_near,
        across,
        opposite,
    )
    by_near, by_next, outgoing = lax.optimization_barrier((by_near, by_next, outgoing))
    arrived = lax.all_to_all(outgoing, "tile", split_axis=0, concat_axis=0, tiled=True)
    even_edge, odd_edge, bottom, top = edges(*sizes, flow, visc, by_near, by_next)
    by_even = lax.ppermute(even_edge, "tile", even_pairs)
    by_odd = lax.ppermute(odd_edge, "tile", odd_pairs)
    inlet = jnp.pad(inlet_cell.reshape(1, -1), ((0, 0), (0, cap - inlet_cell.shape[0])))
    first, middle = inner(*sizes, flow, visc, bottom, top)
    second, inlet_now = outer(*sizes, flow, visc, bottom, top, first, middle, by_even, by_odd, inlet)
    flow_next, arrived_state = land(
        port_match, second, inlet_now, inlet, arrival_cell.reshape(partners, cap), arrived
    )
    return flow_next.reshape(flow_field.shape), arrived_state.reshape(inclusion_state.shape)


def solution(mesh):
    return jax.shard_map(
        on_device,
        mesh=mesh,
        in_specs=(
            P(None, "sec", "tile", None),
            P("sec", "tile", None),
            P(None, ("sec", "tile")),
            P(("sec", "tile")),
            P(("sec", "tile")),
            P(None, "sec", "tile", None, None),
            P("sec", "tile", None, None),
            P("sec", "tile", None, None),
            P("sec", "tile", None, None),
            P("sec", "tile", None),
            P("sec", "tile", None, None),
        ),
        out_specs=(P(None, "sec", "tile", None), P(None, "sec", "tile", None, None)),
        check_vma=False,
    )
```
